128 devices in a mesh: gx: 8 (over z, core), gy: 16 (over y, x).
Axes of the slice: x: 4, y: 4, z: 4, core: 2. Of those that a mesh axis runs over, the one named last changes fastest.
Arguments:
- displacement: float32 [3, 24, 384, 384], P(None, 'gx', 'gy'), may hold values from -1.6015 to 1.6015, as said below
- velocity: float32 [3, 24, 384, 384], P(None, 'gx', 'gy'), may hold values from -6 to 6
- energy: float32 [27, 8, 128, 128], P(None, 'gx', 'gy'), may hold values from 0.5 to 18
- mass_weight: float32 [216, 8, 128, 128], P(None, 'gx', 'gy'), may hold values from 0.002 to 0.02
- pinned_flags: int32 [3, 24, 384, 384], P(None, 'gx', 'gy'), may hold values 0 or 1
Outputs:
- acceleration: float32 [3, 24, 384, 384], P(None, 'gx', 'gy')
- velocity_new: float32 [3, 24, 384, 384], P(None, 'gx', 'gy')
- displacement_new: float32 [3, 24, 384, 384], P(None, 'gx', 'gy')
- energy_new: float32 [27, 8, 128, 128], P(None, 'gx', 'gy')
The draws below stay inside these ranges and needn't reach their ends.
Inputs may be any that keep to these rules, and one draw needn't show every extreme that they name: Every entry of the displacement's derivative along local element coordinates stays below 0.11 in magnitude.
All inputs are finite; a program needn't handle non-finite values. No bound on the sum of `pinned_flags` on one device may be relied on, other than what follows from the above.
Results may differ from the reference program's by a relative error of at most 0.00018.
Values sent between devices are 32-bit elements; how exact they have to be, the bound alone decides.
No kernel may reach another device: no remote copies, remote signals or barrier semaphores. Data moves between devices by JAX's collectives and lax.ppermute only.
A program may use at most 128 MiB of HBM per device.

```python
import math
from functools import partial
import jax
import jax.numpy as jnp
import numpy as np
from jax import lax

EZ = 128
Q = 6
ITERS = 3
NX = 24
NY = 384
NZ = 384
NEX = 8
NEY = 128
QP = 216


def lattice_coord(num_nodes):
    inner_point = 0.5 / math.sqrt(5.0)
    positions = jnp.arange(num_nodes, dtype=jnp.int32)
    within = positions % 3
    offset = jnp.where(within == 0, 0.0, jnp.where(within == 1, 0.5 - inner_point, 0.5 + inner_point))
    return (positions // 3).astype(jnp.float32) + offset.astype(jnp.float32)


def draw_displacement(key, part):
    key_list = jax.random.split(key, 2)
    coord_list = [lattice_coord(NX), lattice_coord(NY), lattice_coord(NZ)]
    length_list = [NX / 3.0, NY / 3.0, NZ / 3.0]
    phase_draw = jax.random.uniform(key_list[0], (3,), jnp.float32, -math.pi, math.pi)
    rough_part = jax.random.uniform(key_list[1], (3, NX, NY, NZ), jnp.float32, -0.0015, 0.0015)
    components = []
    for c in range(3):
        d = (c + 1) % 3
        wave_part = 0.0125 * length_list[d] * jnp.sin(2.0 * math.pi * coord_list[d] / length_list[d] + phase_draw[c])
        view_shape = [1, 1, 1]
        view_shape[d] = -1
        components.append(jnp.broadcast_to(wave_part.reshape(view_shape), (NX, NY, NZ)))
    return jnp.stack(components) + rough_part


def draw_energy(key, part):
    base_draw = jnp.exp(jax.random.uniform(key, (27, NEX, NEY, EZ), jnp.float32, math.log(0.5), math.log(2.0)))
    ramp_x = 1.0 + 2.0 * jnp.arange(NEX, dtype=jnp.float32) / NEX
    ramp_y = 1.0 + 2.0 * jnp.arange(NEY, dtype=jnp.float32) / NEY
    return base_draw * ramp_x[None, :, None, None] * ramp_y[None, None, :, None]


def with_ends(values, key, smallest, high):
    place = [jax.random.randint(jax.random.fold_in(key, axis), (), 0, length) for axis, length in enumerate(values.shape)]
    widest = values.shape.index(max(values.shape))
    neighbour = place[:widest] + [(place[widest] + 1) % values.shape[widest]] + place[widest + 1:]
    return values.at[tuple(place)].set(smallest).at[tuple(neighbour)].set(high)


def block_levels(stream_key, dims, cuts, low, largest):
    gain, own = 1.0, jax.random.fold_in(stream_key, 6)
    for position, blocks in cuts:
        heights = jnp.exp(jax.random.uniform(jax.random.fold_in(own, position), (blocks,), jnp.float32, low / len(cuts), largest / len(cuts)))
        gain = gain * jnp.repeat(heights, dims[position] // blocks).reshape([-1 if axis == position else 1 for axis in range(len(dims))])
    return gain


def normal_values(own_key, extent, scale, reach, cuts=(), kind=jnp.bfloat16):
    factor_of = block_levels(own_key, extent, cuts, -0.22, 0.18) if cuts else 1.0
    drawn = jax.random.normal(own_key, extent, jnp.float32) * scale * factor_of
    return jnp.minimum(jnp.maximum(drawn, -reach), reach).astype(kind)


def setup_inputs(seed: int = 0) -> dict:
    streams_of = jax.random.split(jax.random.key(seed), 6)
    return {
        "displacement": draw_displacement(jax.random.fold_in(streams_of[5], 71), 0),
        "velocity": normal_values(streams_of[1], (3, NX, NY, NZ), 1.0, 6.0, ((1, 8), (2, 16)), jnp.float32),
        "energy": draw_energy(jax.random.fold_in(streams_of[5], 71), 0),
        "mass_weight": jnp.clip(jnp.exp(math.log(0.02) - 2.30258502 * jax.random.uniform(streams_of[3], (QP, NEX, NEY, EZ), jnp.float32) ** block_levels(streams_of[3], (QP, NEX, NEY, EZ), ((1, 8), (2, 16)), -0.2, 0.2)), 0.002, 0.02),
        "pinned_flags": with_ends((jax.random.randint(streams_of[4], (3, NX, NY, NZ), 0, 8) < 1).astype(jnp.int32), jax.random.fold_in(streams_of[4], 1), 0, 1),
    }


HIGHEST = lax.Precision.HIGHEST
step_size = 0.05
viscosity = 0.3
gamma_less = 0.4

def basis_tables():
    root_five = 1.0 / math.sqrt(5.0)
    lobatto = np.array([0.0, 0.5 - 0.5 * root_five, 0.5 + 0.5 * root_five, 1.0])
    legendre = np.array([-0.932469514203152, -0.6612093864662645, -0.2386191860831909, 0.2386191860831909, 0.6612093864662645, 0.932469514203152])
    abscissa = 0.5 + 0.5 * legendre
    shape_values = np.ones((6, 4))
    shape_slopes = np.zeros((6, 4))
    for a in range(4):
        for b in range(4):
            if b != a:
                shape_values[:, a] = shape_values[:, a] * (abscissa - lobatto[b]) / (lobatto[a] - lobatto[b])
        for c in range(4):
            if c != a:
                factor_term = np.ones(6) / (lobatto[a] - lobatto[c])
                for b in range(4):
                    if b != a and b != c:
                        factor_term = factor_term * (abscissa - lobatto[b]) / (lobatto[a] - lobatto[b])
                shape_slopes[:, a] = shape_slopes[:, a] + factor_term
    thermo_values = np.stack([(1.0 - abscissa) * (1.0 - abscissa), 2.0 * abscissa * (1.0 - abscissa), abscissa * abscissa], axis=1)
    return (jnp.asarray(shape_values, jnp.float32), jnp.asarray(shape_slopes, jnp.float32), jnp.asarray(thermo_values, jnp.float32))

def along_x(matrix, operand):
    return jnp.einsum('qa,cabgjk->cqbgjk', matrix, operand, precision=HIGHEST)

def along_y(matrix, operand):
    return jnp.einsum('qb,cabgjk->caqgjk', matrix, operand, precision=HIGHEST)

def along_z(matrix, operand):
    return jnp.einsum('qg,cabgjk->cabqjk', matrix, operand, precision=HIGHEST)

def split_nodes(operand, which_axis):
    num_cells = (operand.shape[which_axis] - 1) // 3
    outer_dims = operand.shape[:which_axis]
    inner_dims = operand.shape[which_axis + 1:]
    head_part = lax.slice_in_dim(operand, 0, 3 * num_cells, axis=which_axis).reshape(outer_dims + (num_cells, 3) + inner_dims)
    head_part = jnp.moveaxis(head_part, which_axis + 1, which_axis)
    tail_part = lax.slice_in_dim(operand, 3, 3 * num_cells + 1, stride=3, axis=which_axis)
    return jnp.concatenate([head_part, jnp.expand_dims(tail_part, which_axis)], axis=which_axis)

def merge_nodes(operand, which_axis):
    num_cells = operand.shape[which_axis + 1]
    outer_dims = operand.shape[:which_axis]
    inner_dims = operand.shape[which_axis + 2:]
    head_part = jnp.moveaxis(lax.slice_in_dim(operand, 0, 3, axis=which_axis), which_axis, which_axis + 1)
    head_part = head_part.reshape(outer_dims + (3 * num_cells,) + inner_dims)
    tail_part = jnp.moveaxis(lax.slice_in_dim(operand, 3, 4, axis=which_axis), which_axis, which_axis + 1)
    pad_tail = [(0, 0)] * tail_part.ndim
    pad_tail[which_axis + 1] = (0, 2)
    tail_part = jnp.pad(tail_part, pad_tail).reshape(outer_dims + (3 * num_cells,) + inner_dims)
    pad_head = [(0, 0)] * head_part.ndim
    pad_head[which_axis] = (0, 1)
    pad_shift = [(0, 0)] * head_part.ndim
    pad_shift[which_axis] = (3, 0)
    shifted = lax.slice_in_dim(jnp.pad(tail_part, pad_shift), 0, 3 * num_cells + 1, axis=which_axis)
    return jnp.pad(head_part, pad_head) + shifted

def slab_elements(slab_field):
    closed = jnp.concatenate([slab_field, slab_field[..., :1]], axis=-1)
    parts_y = split_nodes(closed, 2)
    parts_z = split_nodes(parts_y, 4)
    return jnp.moveaxis(parts_z, 4, 3)

def slab_assemble(element_field):
    parts_z = merge_nodes(jnp.moveaxis(element_field, 3, 4), 4)
    parts_y = merge_nodes(parts_z, 2)
    return jnp.concatenate([parts_y[..., :1] + parts_y[..., -1:], parts_y[..., 1:-1]], axis=-1)

def over_blocks(node_fields, cell_data, element_fn):
    num_cells = cell_data[0].shape[1]

    def one_block(block_index):
        node_start = 3 * block_index
        element_sets = tuple((slab_elements(lax.dynamic_slice_in_dim(field_in, node_start, 4, axis=1)) for field_in in node_fields))
        cell_block = tuple((lax.dynamic_index_in_dim(member, block_index, axis=1, keepdims=False) for member in cell_data))
        contribution, outputs_extra = element_fn(element_sets, cell_block)
        return (slab_assemble(contribution), outputs_extra)
    node_pieces, extra_parts = lax.map(one_block, jnp.arange(num_cells, dtype=jnp.int32))
    assembled = merge_nodes(jnp.moveaxis(node_pieces, 0, 2), 1)
    return (assembled, tuple((jnp.moveaxis(member, 0, 1) for member in extra_parts)))

def thermo_interp(thermo_values, dofs):
    return along_x(thermo_values, along_y(thermo_values, along_z(thermo_values, dofs[None])))[0]

def thermo_project(thermo_values, at_quad):
    moved = thermo_values.T
    return along_x(moved, along_y(moved, along_z(moved, at_quad[None])))[0]

def force_block(element_sets, cell_block, basis_set):
    shape_values, shape_slopes, thermo_values = basis_set
    kinematic = element_sets[0]
    energy_block, weight_block = cell_block
    trailing_shape = energy_block.shape[1:]
    z_values = along_z(shape_values, kinematic)
    z_slopes = along_z(shape_slopes, kinematic)
    yz_values = along_y(shape_values, z_values)
    gradients = [along_x(shape_slopes, yz_values), along_x(shape_values, along_y(shape_slopes, z_values)), along_x(shape_values, along_y(shape_values, z_slopes))]
    jacobian = [[gradients[d][c] + (1.0 if c == d else 0.0) for d in range(3)] for c in range(3)]
    grad_vel = [[gradients[d][3 + c] for d in range(3)] for c in range(3)]
    cofactor = [[jacobian[(c + 1) % 3][(d + 1) % 3] * jacobian[(c + 2) % 3][(d + 2) % 3] - jacobian[(c + 1) % 3][(d + 2) % 3] * jacobian[(c + 2) % 3][(d + 1) % 3] for d in range(3)] for c in range(3)]
    determinant = jacobian[0][0] * cofactor[0][0] + jacobian[0][1] * cofactor[0][1] + jacobian[0][2] * cofactor[0][2]
    inverse_det = 1.0 / determinant
    spatial_grad = [[(grad_vel[c][0] * cofactor[e][0] + grad_vel[c][1] * cofactor[e][1] + grad_vel[c][2] * cofactor[e][2]) * inverse_det for e in range(3)] for c in range(3)]
    energy_quad = thermo_interp(thermo_values, energy_block.reshape((3, 3, 3) + trailing_shape))
    mass_quad = weight_block.reshape((Q, Q, Q) + trailing_shape)
    scale_quad = mass_quad * inverse_det
    stress_shape = [[viscosity * (spatial_grad[c][d] + spatial_grad[d][c]) - (gamma_less * energy_quad if c == d else 0.0) for d in range(3)] for c in range(3)]
    flux = [[scale_quad * (stress_shape[c][0] * cofactor[0][f] + stress_shape[c][1] * cofactor[1][f] + stress_shape[c][2] * cofactor[2][f]) for f in range(3)] for c in range(3)]
    power_quad = jnp.zeros_like(mass_quad)
    for c in range(3):
        for f in range(3):
            power_quad = power_quad + flux[c][f] * grad_vel[c][f]
    flux_cols = [jnp.stack([flux[c][f] for c in range(3)]) for f in range(3)]
    moved = along_x(shape_slopes.T, along_y(shape_values.T, along_z(shape_values.T, flux_cols[0])))
    moved = moved + along_x(shape_values.T, along_y(shape_slopes.T, along_z(shape_values.T, flux_cols[1])) + along_y(shape_values.T, along_z(shape_slopes.T, flux_cols[2])))
    energy_rhs = thermo_project(thermo_values, power_quad)
    lumped_mass = thermo_project(thermo_values, mass_quad)
    energy_next = energy_block + step_size * (energy_rhs / lumped_mass).reshape(energy_block.shape)
    return (-moved, (energy_next,))

def mass_block(element_sets, cell_block, basis_set):
    shape_values = basis_set[0]
    mass_quad = cell_block[0].reshape((Q, Q, Q) + cell_block[0].shape[1:])
    at_quad = along_x(shape_values, along_y(shape_values, along_z(shape_values, element_sets[0]))) * mass_quad
    return (along_x(shape_values.T, along_y(shape_values.T, along_z(shape_values.T, at_quad))), ())

def wrap_periodic(field_in):
    field_in = jnp.concatenate([field_in, field_in[:, :1]], axis=1)
    return jnp.concatenate([field_in, field_in[:, :, :1]], axis=2)

def fold_periodic(field_in):
    field_in = jnp.concatenate([field_in[:, :1] + field_in[:, -1:], field_in[:, 1:-1]], axis=1)
    return jnp.concatenate([field_in[:, :, :1] + field_in[:, :, -1:], field_in[:, :, 1:-1]], axis=2)

def reference(displacement, velocity, energy, mass_weight, pinned_flags):
    basis_set = basis_tables()
    free_mask = (1 - pinned_flags).astype(jnp.float32)
    kinematic = jnp.concatenate([displacement, velocity], axis=0)
    assembled, extra_parts = over_blocks((wrap_periodic(kinematic),), (energy, mass_weight), partial(force_block, basis_set=basis_set))
    nodal_force = fold_periodic(assembled)
    energy_new = extra_parts[0]
    mass_apply = partial(mass_block, basis_set=basis_set)

    def apply_mass(vector):
        contribution = over_blocks((wrap_periodic(vector),), (mass_weight,), mass_apply)[0]
        return free_mask * fold_periodic(contribution)
    residual = free_mask * nodal_force
    acceleration = jnp.zeros_like(residual)
    direction = residual
    norm_now = jnp.sum(residual * residual)
    for iteration in range(ITERS):
        mass_image = apply_mass(direction)
        step_length = norm_now / jnp.sum(direction * mass_image)
        acceleration = acceleration + step_length * direction
        residual = residual - step_length * mass_image
        norm_next = jnp.sum(residual * residual)
        direction = residual + norm_next / norm_now * direction
        norm_now = norm_next
    velocity_new = velocity + step_size * acceleration
    displacement_new = displacement + step_size * velocity_new
    return (acceleration, velocity_new, displacement_new, energy_new)
```

```python
import math

import jax
import jax.numpy as jnp
import numpy as np
from jax import lax
from jax.experimental import pallas as pl
from jax.experimental.pallas import tpu as pltpu
from jax.sharding import PartitionSpec as P

step_size = 0.05
viscosity = 0.3
gamma_less = 0.4
F32 = jnp.float32
VMEM_LIMIT = 48 * 1024 * 1024


def tables():
    root_five = 1.0 / math.sqrt(5.0)
    lobatto = np.array([0.0, 0.5 - 0.5 * root_five, 0.5 + 0.5 * root_five, 1.0])
    legendre = np.array(
        [
            -0.932469514203152,
            -0.6612093864662645,
            -0.2386191860831909,
            0.2386191860831909,
            0.6612093864662645,
            0.932469514203152,
        ]
    )
    t = 0.5 + 0.5 * legendre
    values = np.ones((6, 4))
    slopes = np.zeros((6, 4))
    for a in range(4):
        for b in range(4):
            if b != a:
                values[:, a] *= (t - lobatto[b]) / (lobatto[a] - lobatto[b])
        for c in range(4):
            if c != a:
                term = np.ones(6) / (lobatto[a] - lobatto[c])
                for b in range(4):
                    if b != a and b != c:
                        term = term * (t - lobatto[b]) / (lobatto[a] - lobatto[b])
                slopes[:, a] += term
    thermo = np.stack([(1.0 - t) * (1.0 - t), 2.0 * t * (1.0 - t), t * t], axis=1)
    return values, slopes, thermo


def even_odd(matrix):
    even = [[float((matrix[q, a] + matrix[q, 3 - a]) / 2) for a in range(2)] for q in range(3)]
    odd = [[float((matrix[q, a] - matrix[q, 3 - a]) / 2) for a in range(2)] for q in range(3)]
    return even, odd


VALUES, SLOPES, THERMO = tables()
BE, BO = even_odd(VALUES)
DE, DO = even_odd(SLOPES)
TE = [float((THERMO[q, 0] + THERMO[q, 2]) / 2) for q in range(3)]
TO = [float((THERMO[q, 0] - THERMO[q, 2]) / 2) for q in range(3)]
TM = [float(THERMO[q, 1]) for q in range(3)]


def butterfly(u):
    return [u[0] + u[3], u[1] + u[2], u[0] - u[3], u[1] - u[2]]


def unbutterfly(r):
    return [r[0] + r[2], r[1] + r[3], r[1] - r[3], r[0] - r[2]]


def interp_pair(h, q):
    even = BE[q][0] * h[0] + BE[q][1] * h[1]
    odd = BO[q][0] * h[2] + BO[q][1] * h[3]
    return even + odd, even - odd


def slope_pair(h, q):
    even = DE[q][0] * h[0] + DE[q][1] * h[1]
    odd = DO[q][0] * h[2] + DO[q][1] * h[3]
    return odd + even, odd - even


def along(pair_fn, h):
    out = [None] * 6
    for q in range(3):
        out[q], out[5 - q] = pair_fn(h, q)
    return out


def plus(total, term):
    return term if total is None else total + term


def interp_back(f, h=None, sign=1.0):
    h = [None] * 4 if h is None else list(h)
    for q in range(3):
        even, odd = f[q] + f[5 - q], f[q] - f[5 - q]
        for a in range(2):
            h[a] = plus(h[a], (sign * BE[q][a]) * even)
            h[2 + a] = plus(h[2 + a], (sign * BO[q][a]) * odd)
    return h


def slope_back(f, h=None, sign=1.0):
    h = [None] * 4 if h is None else list(h)
    for q in range(3):
        even, odd = f[q] + f[5 - q], f[q] - f[5 - q]
        for a in range(2):
            h[a] = plus(h[a], (sign * DE[q][a]) * odd)
            h[2 + a] = plus(h[2 + a], (sign * DO[q][a]) * even)
    return h


def thermo_along(u):
    even, odd, mid = u[0] + u[2], u[0] - u[2], u[1]
    out = [None] * 6
    for q in range(3):
        both, one = TE[q] * even + TM[q] * mid, TO[q] * odd
        out[q], out[5 - q] = both + one, both - one
    return out


def thermo_back(f):
    even = mid = odd = None
    for q in range(3):
        both, one = f[q] + f[5 - q], f[q] - f[5 - q]
        even = plus(even, TE[q] * both)
        mid = plus(mid, TM[q] * both)
        odd = plus(odd, TO[q] * one)
    return [even + odd, mid, even - odd]


def iotas(rows=8):
    shape = (rows, 128)
    return lax.broadcasted_iota(jnp.int32, shape, 0), lax.broadcasted_iota(jnp.int32, shape, 1)


def gather_lanes(x, index):
    return jnp.take_along_axis(x, index, axis=1, mode="promise_in_bounds")


def split_lanes(parts, rows=8):
    lane = iotas(rows)[1]
    out = []
    for g in range(3):
        place = 3 * lane + g
        index = place & 127
        moved = [gather_lanes(p, index) for p in parts]
        out.append(
            jnp.where(place < 128, moved[0], jnp.where(place < 256, moved[1], moved[2]))
        )
    return out


def join_lanes(parts):
    lane = iotas()[1]
    out = []
    for v in range(3):
        place = lane + 128 * v
        index = place // 3
        g = place - 3 * index
        moved = [gather_lanes(p, index) for p in parts]
        out.append(jnp.where(g == 0, moved[0], jnp.where(g == 1, moved[1], moved[2])))
    return out


def next_lane(x):
    return pltpu.roll(x, 127, 1)


def previous_lane(x):
    return pltpu.roll(x, 1, 1)


def pack_kernel(d_ref, v_ref, f_ref, x_ref, y_ref, c_ref):
    for n, ref in enumerate((d_ref, v_ref, f_ref)):
        for c in range(3):
            k = 3 * n + c
            face = ref[c, 0].astype(F32)
            x_ref[k] = face
            c_ref[k : k + 1, :] = face[0:1]
            for x in range(3):
                r = 9 * x + k
                y_ref[r : r + 1, :] = ref[c, x, 0:1, :].astype(F32)


def element_rows(load, place):
    for t in range(3):
        tiles = split_lanes([load(8 * t, 128 * v) for v in range(3)])
        for g in range(3):
            place[g, 8 * t : 8 * t + 8, :] = tiles[g]
    return [place[g, pl.ds(b, 8, stride=3), :] for b in range(3) for g in range(3)]


def prep_kernel(d_ref, v_ref, f_ref, u_ref, m_ref, place):
    def body(c, _):
        for x in range(3):
            for k, ref in enumerate((d_ref, v_ref, f_ref)):
                tiles = element_rows(
                    lambda s, l: ref[c, x, s : s + 8, l : l + 128].astype(F32), place.at[3 * x + k]
                )
                for n in range(9):
                    if k < 2:
                        u_ref[3 * k + c, x * 9 + n] = tiles[n]
                    else:
                        m_ref[x, c * 9 + n] = 1.0 - tiles[n]
        return 0

    lax.fori_loop(0, 3, body, 0)


def point(jac, vel, energy, mass):
    cof = [
        [
            jac[(c + 1) % 3][(d + 1) % 3] * jac[(c + 2) % 3][(d + 2) % 3]
            - jac[(c + 1) % 3][(d + 2) % 3] * jac[(c + 2) % 3][(d + 1) % 3]
            for d in range(3)
        ]
        for c in range(3)
    ]
    det = jac[0][0] * cof[0][0] + jac[0][1] * cof[0][1] + jac[0][2] * cof[0][2]
    inv = pl.reciprocal(det, approx=True)
    inv = inv * (2.0 - det * inv)
    inv = inv * (2.0 - det * inv)
    scale = mass * inv
    shear = (viscosity * scale) * inv
    press = scale * energy
    rate = [
        [vel[c][0] * cof[e][0] + vel[c][1] * cof[e][1] + vel[c][2] * cof[e][2] for e in range(3)]
        for c in range(3)
    ]
    stress = [[None] * 3 for _ in range(3)]
    power = None
    for c in range(3):
        stress[c][c] = shear * (rate[c][c] + rate[c][c]) - press
        power = plus(power, stress[c][c] * rate[c][c])
        for d in range(c + 1, 3):
            both = rate[c][d] + rate[d][c]
            stress[c][d] = stress[d][c] = shear * both
            power = power + stress[c][d] * both
    flux = [
        [
            stress[c][0] * cof[0][f] + stress[c][1] * cof[1][f] + stress[c][2] * cof[2][f]
            for f in range(3)
        ]
        for c in range(3)
    ]
    return flux, power


def spread_y(first, row):
    sub = iotas()[0]
    return jnp.where(sub == 7, row, pltpu.roll(first, 7, 0))


def store_parts(nodes_of, minus_ref, plus_ref, inner_ref, rim_ref):
    sub = iotas()[0]

    def body(c, _):
        for g in range(3):
            nodes = nodes_of(c, g)
            for x in range(4):
                over = nodes[x][3]
                nodes[x][0] = nodes[x][0] + jnp.where(sub == 0, 0.0, pltpu.roll(over, 1, 0))
                r = c * 3 + g
                if x in (0, 3):
                    ref = minus_ref if x == 0 else plus_ref
                    ref[pl.ds(216 + r, 1), :] = over[7:8]
                    for b in range(3):
                        ref[pl.ds(pl.multiple_of((c * 9 + b * 3 + g) * 8, 8), 8), :] = nodes[x][b]
                else:
                    rim_ref[x - 1, pl.ds(r, 1), :] = over[7:8]
                    for b in range(3):
                        inner_ref[x - 1, c * 9 + b * 3 + g] = nodes[x][b]
        return 0

    lax.fori_loop(0, 3, body, 0)


def force_kernel(
    u_ref, hx_ref, hy_ref, hc_ref, e_ref, w_ref,
    minus_ref, plus_ref, inner_ref, rim_ref, face_mask_ref, rim_mask_ref, energy_ref,
    hx_s, hy_s, q_s, zv_s, zs_s, w_s, ez_s, ey_s, xt_s, ya_s, yb_s, zn_s, px_s, py_s, place,
):
    rows = [
        jnp.concatenate(
            [hy_ref[:, 128 * v : 128 * v + 128], hc_ref[:, 128 * v : 128 * v + 128]], axis=0
        )
        for v in range(3)
    ]
    rows = [jnp.concatenate([r, jnp.zeros((4, 128), F32)], axis=0) for r in rows]
    for t in range(5):
        for g, tile in enumerate(split_lanes([r[8 * t : 8 * t + 8] for r in rows])):
            hy_s[g, 8 * t : 8 * t + 8, :] = tile
    for x in range(4):
        for c in range(3):
            for g in range(3):
                r = 9 * x + 6 + c
                rim_mask_ref[x, c * 3 + g : c * 3 + g + 1, :] = 1.0 - hy_s[g, r : r + 1, :]

    def face(j, _):
        for i in range(3):
            k = 3 * j + i
            tiles = element_rows(lambda s, l: hx_ref[k, s : s + 8, l : l + 128], place.at[i])
            for n in range(9):
                hx_s[k, n] = tiles[n]
        return 0

    lax.fori_loop(0, 3, face, 0)
    for c in range(3):
        for n in range(9):
            face_mask_ref[c * 9 + n] = 1.0 - hx_s[6 + c, n]

    def gather_nodes(c, _):
        for g in range(3):
            cols = []
            for x in range(4):
                if x < 3:
                    u = [u_ref[c, x * 9 + b * 3 + g] for b in range(3)]
                else:
                    u = [hx_s[c, b * 3 + g] for b in range(3)]
                row = hy_s[g, pl.ds(9 * x + c, 1), :]
                u.append(spread_y(u[0], row))
                cols.append(butterfly(u))
            for y in range(4):
                for x, t in enumerate(butterfly([cols[x][y] for x in range(4)])):
                    q_s[c, (x * 4 + y) * 3 + g] = t
        return 0

    lax.fori_loop(0, 6, gather_nodes, 0)

    def along_z(c, _):
        for n in range(16):
            u = [q_s[c, 3 * n + g] for g in range(3)]
            u.append(next_lane(u[0]))
            h = butterfly(u)
            for q, t in enumerate(along(interp_pair, h)):
                zv_s[q, c, n] = t
            for q, t in enumerate(along(slope_pair, h)):
                zs_s[q, c, n] = t
        return 0

    lax.fori_loop(0, 6, along_z, 0)
    for n in range(9):
        for q, t in enumerate(thermo_along([e_ref[3 * n + g] for g in range(3)])):
            ez_s[q, n] = t

    def plane(z, _):
        def along_y(c, _):
            for x in range(4):
                h = [zv_s[z, c, x * 4 + y] for y in range(4)]
                s = [zs_s[z, c, x * 4 + y] for y in range(4)]
                for q, t in enumerate(along(interp_pair, h)):
                    w_s[q, 0, c * 4 + x] = t
                for q, t in enumerate(along(slope_pair, h)):
                    w_s[q, 1, c * 4 + x] = t
                for q, t in enumerate(along(interp_pair, s)):
                    w_s[q, 2, c * 4 + x] = t
            return 0

        lax.fori_loop(0, 6, along_y, 0)
        for x in range(3):
            for q, t in enumerate(thermo_along([ez_s[z, 3 * x + y] for y in range(3)])):
                ey_s[q, x] = t

        def line(y, _):
            energy = thermo_along([gamma_less * ey_s[y, x] for x in range(3)])
            power = [None] * 6
            mass = [None] * 6
            back = [[[None] * 4 for _ in range(3)] for _ in range(3)]
            for q in range(3):
                grads = [[[None] * 3 for _ in range(6)] for _ in range(2)]
                for c in range(6):
                    for d in range(3):
                        h = [w_s[y, d, c * 4 + x] for x in range(4)]
                        pair = slope_pair(h, q) if d == 0 else interp_pair(h, q)
                        for side in range(2):
                            t = pair[side]
                            grads[side][c][d] = t + 1.0 if c == d else t
                flux = []
                for side in range(2):
                    p = q if side == 0 else 5 - q
                    mass[p] = w_ref[p * 36 + y * 6 + z]
                    f, power[p] = point(grads[side][:3], grads[side][3:], energy[p], mass[p])
                    flux.append(f)
                for c in range(3):
                    for f in range(3):
                        even = flux[0][c][f] + flux[1][c][f]
                        odd = flux[0][c][f] - flux[1][c][f]
                        h = back[c][f]
                        for a in range(2):
                            if f == 0:
                                h[a] = plus(h[a], DE[q][a] * odd)
                                h[2 + a] = plus(h[2 + a], DO[q][a] * even)
                            else:
                                h[a] = plus(h[a], BE[q][a] * even)
                                h[2 + a] = plus(h[2 + a], BO[q][a] * odd)
            for c in range(3):
                for f in range(3):
                    for x in range(4):
                        xt_s[y, f, c * 4 + x] = back[c][f][x]
            for x, t in enumerate(thermo_back(power)):
                px_s[y, x] = t
            for x, t in enumerate(thermo_back(mass)):
                px_s[y, 3 + x] = t
            return 0

        lax.fori_loop(0, 6, line, 0)

        def back_y(c, _):
            for x in range(4):
                f = [[xt_s[q, d, c * 4 + x] for q in range(6)] for d in range(3)]
                h = slope_back(f[1], interp_back(f[0]))
                s = interp_back(f[2])
                for y in range(4):
                    ya_s[z, c, x * 4 + y] = h[y]
                    yb_s[z, c, x * 4 + y] = s[y]
            return 0

        lax.fori_loop(0, 3, back_y, 0)
        for x in range(6):
            for y, t in enumerate(thermo_back([px_s[q, x] for q in range(6)])):
                py_s[z, 3 * x + y] = t
        return 0

    lax.fori_loop(0, 6, plane, 0)

    for n in range(9):
        work = thermo_back([py_s[q, n] for q in range(6)])
        lump = thermo_back([py_s[q, 9 + n] for q in range(6)])
        for g in range(3):
            energy_ref[3 * n + g] = e_ref[3 * n + g] + step_size * (work[g] / lump[g])

    def back_z(c, _):
        for n in range(16):
            h = interp_back([ya_s[q, c, n] for q in range(6)], sign=-1.0)
            h = slope_back([yb_s[q, c, n] for q in range(6)], h, sign=-1.0)
            u = unbutterfly(h)
            zn_s[c, n * 3] = u[0] + previous_lane(u[3])
            zn_s[c, n * 3 + 1] = u[1]
            zn_s[c, n * 3 + 2] = u[2]
        return 0

    lax.fori_loop(0, 3, back_z, 0)
    store_parts(lambda c, g: nodes_from(zn_s, c, g), minus_ref, plus_ref, inner_ref, rim_ref)


def nodes_from(zn_s, c, g):
    cols = [unbutterfly([zn_s[c, (x * 4 + y) * 3 + g] for y in range(4)]) for x in range(4)]
    rows = [unbutterfly([cols[x][b] for x in range(4)]) for b in range(4)]
    return [[rows[b][x] for b in range(4)] for x in range(4)]


def rows_kernel(minus_ref, plus_ref, inner_ref, rim_ref, got_low_ref, got_high_ref, down_ref, up_ref):
    for c in range(3):
        for g in range(3):
            r = c * 3 + g
            n = (c * 9 + g) * 8
            down_ref[r : r + 1, :] = minus_ref[n : n + 1, :] + got_low_ref[n : n + 1, :]
            down_ref[27 + r : 28 + r, :] = plus_ref[n : n + 1, :] + got_high_ref[n : n + 1, :]
            for x in range(2):
                down_ref[9 * (x + 1) + r : 9 * (x + 1) + r + 1, :] = inner_ref[x, c * 9 + g, 0:1, :]
    up_ref[0:9, :] = minus_ref[216:225, :] + got_low_ref[216:225, :]
    up_ref[27:36, :] = plus_ref[216:225, :] + got_high_ref[216:225, :]
    for x in range(2):
        up_ref[9 * (x + 1) : 9 * (x + 1) + 9, :] = rim_ref[x, 0:9, :]


def assemble(c, parts, mask_ref, face_mask_ref, rim_mask_ref, own_ref, q_s):
    minus_ref, plus_ref, inner_ref, rim_ref, low_ref, high_ref, from_down_ref, from_up_ref = parts
    sub = iotas()[0]
    for g in range(3):
        r = c * 3 + g
        cols = []
        for x in range(4):
            u = []
            for b in range(3):
                n = c * 9 + b * 3 + g
                tile = pl.ds(pl.multiple_of(n * 8, 8), 8)
                if x == 0:
                    t = minus_ref[tile, :] + low_ref[tile, :]
                elif x == 3:
                    t = plus_ref[tile, :] + high_ref[tile, :]
                else:
                    t = inner_ref[x - 1, n]
                if b == 0:
                    below = from_down_ref[pl.ds(9 * x + r, 1), :]
                    t = t + jnp.where(sub == 0, below, 0.0)
                t = t * (face_mask_ref[n] if x == 3 else mask_ref[x, n])
                u.append(t)
                if x < 3:
                    own_ref[x, n] = t
            edge = pl.ds(216 + r, 1)
            if x == 0:
                top = minus_ref[edge, :] + low_ref[edge, :]
            elif x == 3:
                top = plus_ref[edge, :] + high_ref[edge, :]
            else:
                top = rim_ref[x - 1, pl.ds(r, 1), :]
            top = (top + from_up_ref[pl.ds(9 * x + r, 1), :]) * rim_mask_ref[x, pl.ds(r, 1), :]
            u.append(spread_y(u[0], top))
            cols.append(butterfly(u))
        for y in range(4):
            for x, t in enumerate(butterfly([cols[x][y] for x in range(4)])):
                q_s[c, (x * 4 + y) * 3 + g] = t


def mass_along_z(c, q_s, zv_s):
    for n in range(16):
        u = [q_s[c, 3 * n + g] for g in range(3)]
        u.append(next_lane(u[0]))
        for q, t in enumerate(along(interp_pair, butterfly(u))):
            zv_s[q, c, n] = t


def apply_kernel(
    minus_ref, plus_ref, inner_ref, rim_ref, low_ref, high_ref, from_down_ref, from_up_ref,
    mask_ref, face_mask_ref, rim_mask_ref, w_ref,
    own_ref, out_minus_ref, out_plus_ref, out_inner_ref, out_rim_ref,
    q_s, zv_s, xt_s, ya_s, zn_s,
):
    parts = (
        minus_ref, plus_ref, inner_ref, rim_ref, low_ref, high_ref, from_down_ref, from_up_ref,
    )

    def first(c, _):
        assemble(c, parts, mask_ref, face_mask_ref, rim_mask_ref, own_ref, q_s)
        mass_along_z(c, q_s, zv_s)
        return 0

    lax.fori_loop(0, 3, first, 0)

    def plane(z, _):
        for c in range(3):
            lines = [along(interp_pair, [zv_s[z, c, x * 4 + y] for y in range(4)]) for x in range(4)]
            for y in range(6):
                h = [lines[x][y] for x in range(4)]
                at = along(interp_pair, h)
                at = [at[p] * w_ref[p * 36 + y * 6 + z] for p in range(6)]
                for x, t in enumerate(interp_back(at)):
                    xt_s[c, x, y] = t
            for x in range(4):
                for y, t in enumerate(interp_back([xt_s[c, x, q] for q in range(6)])):
                    ya_s[z, c, x * 4 + y] = t
        return 0

    lax.fori_loop(0, 6, plane, 0)

    def back_z(c, _):
        for n in range(16):
            u = unbutterfly(interp_back([ya_s[q, c, n] for q in range(6)]))
            zn_s[c, n * 3] = u[0] + previous_lane(u[3])
            zn_s[c, n * 3 + 1] = u[1]
            zn_s[c, n * 3 + 2] = u[2]
        return 0

    lax.fori_loop(0, 3, back_z, 0)
    store_parts(
        lambda c, g: nodes_from(zn_s, c, g), out_minus_ref, out_plus_ref, out_inner_ref, out_rim_ref
    )


def total(t):
    return jnp.sum(jnp.sum(t, axis=0, keepdims=True), axis=1, keepdims=True)


def moments_kernel(
    minus_ref, plus_ref, inner_ref, rim_ref, low_ref, high_ref, from_down_ref, from_up_ref,
    mask_ref, face_mask_ref, rim_mask_ref, w_ref, r_ref, v_ref,
    own_ref, sums_ref, q_s, zv_s,
):
    parts = (
        minus_ref, plus_ref, inner_ref, rim_ref, low_ref, high_ref, from_down_ref, from_up_ref,
    )

    def first(c, _):
        assemble(c, parts, mask_ref, face_mask_ref, rim_mask_ref, own_ref, q_s)
        mass_along_z(c, q_s, zv_s)
        return 0

    lax.fori_loop(0, 3, first, 0)
    zero = jnp.zeros((8, 128), F32)

    def dots(n, s):
        s = list(s)
        for x in range(3):
            r, v, w = r_ref[x, n], v_ref[x, n], own_ref[x, n]
            s = [
                s[0] + r * r, s[1] + r * v, s[2] + v * v, s[3] + v * w, s[4] + w * w,
            ]
        return tuple(s)

    sums = lax.fori_loop(0, 27, dots, (zero,) * 5)

    def plane(z, s):
        s = list(s)
        for c in range(3):
            lines = [along(interp_pair, [zv_s[z, c, x * 4 + y] for y in range(4)]) for x in range(4)]
            for y in range(6):
                at = along(interp_pair, [lines[x][y] for x in range(4)])
                for p in range(6):
                    s[c] = s[c] + (at[p] * at[p]) * w_ref[p * 36 + y * 6 + z]
        return tuple(s)

    last = lax.fori_loop(0, 6, plane, (zero,) * 3)
    sums = list(sums) + [last[0] + last[1] + last[2]]
    lane = iotas(1)[1]
    row = jnp.zeros((1, 128), F32)
    for k in range(6):
        row = row + jnp.where(lane == k, total(sums[k]), 0.0)
    sums_ref[...] = jnp.broadcast_to(row, (128, 128))


def coefficients(mu):
    unit = mu[1] / mu[0]
    m = [None] * 6
    scale = 1.0 / mu[0]
    for k in range(6):
        m[k] = mu[k] * scale
        scale = scale / unit
    a0 = m[0] / m[1]
    rr1 = a0 * a0 * m[2] - 2.0 * a0 * m[1] + m[0]
    b0 = rr1 / m[0]
    d1 = [1.0 + b0, -a0]
    a1 = rr1 / (d1[0] * d1[0] * m[1] + 2.0 * d1[0] * d1[1] * m[2] + d1[1] * d1[1] * m[3])
    p1 = -(a0 + a1 * d1[0])
    p2 = -a1 * d1[1]
    rr2 = (
        m[0] + p1 * p1 * m[2] + p2 * p2 * m[4]
        + 2.0 * (p1 * m[1] + p2 * m[2] + p1 * p2 * m[3])
    )
    b1 = rr2 / rr1
    q = [1.0 + b1 * d1[0], p1 + b1 * d1[1], p2]
    a2 = rr2 / (
        q[0] * q[0] * m[1] + q[1] * q[1] * m[3] + q[2] * q[2] * m[5]
        + 2.0 * (q[0] * q[1] * m[2] + q[0] * q[2] * m[3] + q[1] * q[2] * m[4])
    )
    x = [a0 + a1 * d1[0] + a2 * q[0], a1 * d1[1] + a2 * q[1], a2 * q[2]]
    return [x[0] / unit, x[1] / (unit * unit), x[2] / (unit * unit * unit)]


def final_kernel(sums_ref, r_ref, v_ref, w_ref, d_ref, vel_ref, a_out, v_out, d_out, place):
    lane = iotas(1)[1]
    row = jnp.sum(sums_ref[...], axis=0, keepdims=True)
    mu = [
        jnp.broadcast_to(jnp.sum(jnp.where(lane == k, row, 0.0), axis=1, keepdims=True), (8, 128))
        for k in range(6)
    ]
    k0, k1, k2 = coefficients(mu)

    def body(c, _):
        for x in range(3):
            for b in range(3):
                for g in range(3):
                    n = c * 9 + b * 3 + g
                    place[x, g, pl.ds(b, 8, stride=3), :] = (
                        k0 * r_ref[x, n] + k1 * v_ref[x, n] + k2 * w_ref[x, n]
                    )
            for s in range(3):
                rows = slice(8 * s, 8 * s + 8)
                for v, t in enumerate(join_lanes([place[x, g, rows, :] for g in range(3)])):
                    lanes = slice(128 * v, 128 * v + 128)
                    a_out[c, x, rows, lanes] = t
                    new = vel_ref[c, x, rows, lanes] + step_size * t
                    v_out[c, x, rows, lanes] = new
                    d_out[c, x, rows, lanes] = d_ref[c, x, rows, lanes] + step_size * new
        return 0

    lax.fori_loop(0, 3, body, 0)


def call(kernel, outs, scratch, name, flops=0):
    def run(*args):
        moved = sum(a.size * 4 for a in args) + sum(4 * math.prod(s) for s in outs)
        return pl.pallas_call(
            kernel,
            out_shape=[jax.ShapeDtypeStruct(s, F32) for s in outs],
            scratch_shapes=[pltpu.VMEM(s, F32) for s in scratch],
            compiler_params=pltpu.CompilerParams(vmem_limit_bytes=VMEM_LIMIT),
            cost_estimate=pl.CostEstimate(flops=flops, bytes_accessed=moved, transcendentals=0),
            name=name,
        )(*args)

    return run


T = (8, 128)
FACE = (232, 128)
PARTS = [FACE, FACE, (2, 27) + T, (2, 16, 128)]


def solution(mesh):
    gx, gy = mesh.shape["gx"], mesh.shape["gy"]

    def moved(value, by_x, by_y):
        pairs = [
            (i * gy + j, ((i + by_x) % gx) * gy + (j + by_y) % gy)
            for i in range(gx)
            for j in range(gy)
        ]
        return lax.ppermute(value, ("gx", "gy"), pairs)

    def complete(parts):
        minus, plus_face, inner, rim = parts
        low = moved(plus_face, 1, 0)
        high = moved(minus, -1, 0)
        down, up = call(rows_kernel, [(40, 128), (40, 128)], [], "rows")(
            minus, plus_face, inner, rim, low, high
        )
        from_up = moved(down, 0, -1)
        from_down = moved(up, 0, 1)
        return (minus, plus_face, inner, rim, low, high, from_down, from_up)

    def on_device(displacement, velocity, energy, mass_weight, pinned):
        weight = mass_weight.reshape((216,) + T)
        dofs = energy.reshape((27,) + T)
        face, row, corner = call(pack_kernel, [(9, 24, 384), (27, 384), (9, 384)], [], "pack")(
            displacement, velocity, pinned
        )
        hx = moved(face, -1, 0)
        hy = moved(row, 0, -1)
        hc = moved(corner, -1, -1)
        nodes, mask = call(prep_kernel, [(6, 27) + T, (3, 27) + T], [(9, 3, 24, 128)], "prep", flops=4000000)(
            displacement, velocity, pinned
        )
        out = call(
            force_kernel,
            PARTS + [(27,) + T, (4, 16, 128), (27,) + T],
            [
                (9, 9) + T, (3, 40, 128), (6, 48) + T, (6, 6, 16) + T, (6, 6, 16) + T,
                (6, 3, 24) + T, (6, 9) + T, (6, 3) + T, (6, 3, 12) + T, (6, 3, 16) + T,
                (6, 3, 16) + T, (3, 48) + T, (6, 6) + T, (6, 18) + T,
                (3, 3, 24, 128),
            ],
            "force",
            flops=90000 * 1024,
        )(nodes, hx, hy, hc, dofs, weight)
        parts, (face_mask, rim_mask, energy_new) = out[:4], out[4:]
        masks = (mask, face_mask, rim_mask)
        scratch = [
            (3, 48) + T, (6, 3, 16) + T, (3, 4, 6) + T, (6, 3, 16) + T, (3, 48) + T,
        ]
        apply = call(apply_kernel, [(3, 27) + T] + PARTS, scratch, "apply", flops=13000 * 1024)
        out = apply(*complete(parts), *masks, weight)
        r, parts = out[0], out[1:]
        out = apply(*complete(parts), *masks, weight)
        v, parts = out[0], out[1:]
        w, sums = call(
            moments_kernel, [(3, 27) + T, (128, 128)], scratch[:2], "moments", flops=8000 * 1024
        )(*complete(parts), *masks, weight, r, v)
        sums = sums.reshape(gx * gy, -1, 128)
        sums = lax.all_to_all(sums, ("gx", "gy"), 0, 0).reshape(-1, 128)
        shape = displacement.shape
        acceleration, velocity_new, displacement_new = call(
            final_kernel, [shape] * 3, [(3, 3, 24, 128)], "final", flops=1000 * 1024
        )(sums, r, v, w, displacement, velocity)
        return acceleration, velocity_new, displacement_new, energy_new.reshape(energy.shape)

    spec = P(None, "gx", "gy", None)
    return jax.shard_map(
        on_device, mesh=mesh, in_specs=(spec,) * 5, out_specs=(spec,) * 4, check_vma=False
    )
```

```python
import math

import jax
import jax.numpy as jnp
import numpy as np
from jax import lax
from jax.experimental import pallas as pl
from jax.experimental.pallas import tpu as pltpu
from jax.sharding import PartitionSpec as P

step_size = 0.05
viscosity = 0.3
gamma_less = 0.4
F32 = jnp.float32
VMEM_LIMIT = 32 * 1024 * 1024


def tables():
    root_five = 1.0 / math.sqrt(5.0)
    lobatto = np.array([0.0, 0.5 - 0.5 * root_five, 0.5 + 0.5 * root_five, 1.0])
    legendre = np.array(
        [
            -0.932469514203152,
            -0.6612093864662645,
            -0.2386191860831909,
            0.2386191860831909,
            0.6612093864662645,
            0.932469514203152,
        ]
    )
    t = 0.5 + 0.5 * legendre
    values = np.ones((6, 4))
    slopes = np.zeros((6, 4))
    for a in range(4):
        for b in range(4):
            if b != a:
                values[:, a] *= (t - lobatto[b]) / (lobatto[a] - lobatto[b])
        for c in range(4):
            if c != a:
                term = np.ones(6) / (lobatto[a] - lobatto[c])
                for b in range(4):
                    if b != a and b != c:
                        term = term * (t - lobatto[b]) / (lobatto[a] - lobatto[b])
                slopes[:, a] += term
    thermo = np.stack([(1.0 - t) * (1.0 - t), 2.0 * t * (1.0 - t), t * t], axis=1)
    return values, slopes, thermo


def even_odd(matrix):
    even = [[float((matrix[q, a] + matrix[q, 3 - a]) / 2) for a in range(2)] for q in range(3)]
    odd = [[float((matrix[q, a] - matrix[q, 3 - a]) / 2) for a in range(2)] for q in range(3)]
    return even, odd


VALUES, SLOPES, THERMO = tables()
BE, BO = even_odd(VALUES)
DE, DO = even_odd(SLOPES)
TE = [float((THERMO[q, 0] + THERMO[q, 2]) / 2) for q in range(3)]
TO = [float((THERMO[q, 0] - THERMO[q, 2]) / 2) for q in range(3)]
TM = [float(THERMO[q, 1]) for q in range(3)]


def butterfly(u):
    return [u[0] + u[3], u[1] + u[2], u[0] - u[3], u[1] - u[2]]


def unbutterfly(r):
    return [r[0] + r[2], r[1] + r[3], r[1] - r[3], r[0] - r[2]]


def interp_pair(h, q):
    even = BE[q][0] * h[0] + BE[q][1] * h[1]
    odd = BO[q][0] * h[2] + BO[q][1] * h[3]
    return even + odd, even - odd


def slope_pair(h, q):
    even = DE[q][0] * h[0] + DE[q][1] * h[1]
    odd = DO[q][0] * h[2] + DO[q][1] * h[3]
    return odd + even, odd - even


def along(pair_fn, h):
    out = [None] * 6
    for q in range(3):
        out[q], out[5 - q] = pair_fn(h, q)
    return out


def plus(total, term):
    return term if total is None else total + term


def interp_back(f, h=None, sign=1.0):
    h = [None] * 4 if h is None else list(h)
    for q in range(3):
        even, odd = f[q] + f[5 - q], f[q] - f[5 - q]
        for a in range(2):
            h[a] = plus(h[a], (sign * BE[q][a]) * even)
            h[2 + a] = plus(h[2 + a], (sign * BO[q][a]) * odd)
    return h


def slope_back(f, h=None, sign=1.0):
    h = [None] * 4 if h is None else list(h)
    for q in range(3):
        even, odd = f[q] + f[5 - q], f[q] - f[5 - q]
        for a in range(2):
            h[a] = plus(h[a], (sign * DE[q][a]) * odd)
            h[2 + a] = plus(h[2 + a], (sign * DO[q][a]) * even)
    return h


def thermo_along(u):
    even, odd, mid = u[0] + u[2], u[0] - u[2], u[1]
    out = [None] * 6
    for q in range(3):
        both, one = TE[q] * even + TM[q] * mid, TO[q] * odd
        out[q], out[5 - q] = both + one, both - one
    return out


def thermo_back(f):
    even = mid = odd = None
    for q in range(3):
        both, one = f[q] + f[5 - q], f[q] - f[5 - q]
        even = plus(even, TE[q] * both)
        mid = plus(mid, TM[q] * both)
        odd = plus(odd, TO[q] * one)
    return [even + odd, mid, even - odd]


def iotas(rows=8):
    shape = (rows, 128)
    return lax.broadcasted_iota(jnp.int32, shape, 0), lax.broadcasted_iota(jnp.int32, shape, 1)


def gather_lanes(x, index):
    return jnp.take_along_axis(x, index, axis=1, mode="promise_in_bounds")


def split_lanes(parts, rows=8):
    lane = iotas(rows)[1]
    out = []
    for g in range(3):
        place = 3 * lane + g
        index = place & 127
        moved = [gather_lanes(p, index) for p in parts]
        out.append(
            jnp.where(place < 128, moved[0], jnp.where(place < 256, moved[1], moved[2]))
        )
    return out


def join_lanes(parts):
    lane = iotas()[1]
    out = []
    for v in range(3):
        place = lane + 128 * v
        index = place // 3
        g = place - 3 * index
        moved = [gather_lanes(p, index) for p in parts]
        out.append(jnp.where(g == 0, moved[0], jnp.where(g == 1, moved[1], moved[2])))
    return out


def next_lane(x):
    return pltpu.roll(x, 127, 1)


def previous_lane(x):
    return pltpu.roll(x, 1, 1)


def pack_kernel(d_ref, v_ref, f_ref, x_ref, y_ref, c_ref, face, face_f, low, low_f, sems):
    copies = []
    for n, ref in enumerate((d_ref, v_ref, f_ref)):
        to_face, to_low = (face.at[n], low.at[n]) if n < 2 else (face_f, low_f)
        copies.append(pltpu.make_async_copy(ref.at[:, 0], to_face, sems.at[2 * n]))
        copies.append(pltpu.make_async_copy(ref.at[:, :, 0:8], to_low, sems.at[2 * n + 1]))
    for copy in copies:
        copy.start()
    for copy in copies:
        copy.wait()
    for n in range(3):
        for c in range(3):
            k = 3 * n + c
            layer = (face[n, c] if n < 2 else face_f[c]).astype(F32)
            x_ref[k] = layer
            c_ref[k : k + 1, :] = layer[0:1]
            for x in range(3):
                r = 9 * x + k
                row = low[n, c, x, 0:1, :] if n < 2 else low_f[c, x, 0:1, :]
                y_ref[r : r + 1, :] = row.astype(F32)


def element_rows(load, place):
    for t in range(3):
        tiles = split_lanes([load(8 * t, 128 * v) for v in range(3)])
        for g in range(3):
            place[g, 8 * t : 8 * t + 8, :] = tiles[g]
    return [place[g, pl.ds(b, 8, stride=3), :] for b in range(3) for g in range(3)]


def prep_kernel(d_ref, v_ref, f_ref, e_ref, w_ref, u_ref, m_ref, eq_ref, lump_ref, place, ez_s, ey_s):
    def body(c, _):
        for x in range(3):
            for k, ref in enumerate((d_ref, v_ref, f_ref)):
                tiles = element_rows(
                    lambda s, l: ref[c, x, s : s + 8, l : l + 128].astype(F32), place.at[3 * x + k]
                )
                for n in range(9):
                    if k < 2:
                        u_ref[3 * k + c, x * 9 + n] = tiles[n]
                    else:
                        m_ref[x, c * 9 + n] = 1.0 - tiles[n]
        return 0

    lax.fori_loop(0, 3, body, 0)
    for n in range(9):
        for q, t in enumerate(thermo_along([gamma_less * e_ref[3 * n + g] for g in range(3)])):
            ez_s[q, n] = t

    def plane(z, _):
        for x in range(3):
            for q, t in enumerate(thermo_along([ez_s[z, 3 * x + y] for y in range(3)])):
                ey_s[q, x] = t
        for y in range(6):
            for q, t in enumerate(thermo_along([ey_s[y, x] for x in range(3)])):
                eq_ref[q * 36 + y * 6 + z] = t
        return 0

    lax.fori_loop(0, 6, plane, 0)
    project(w_ref, ez_s, ey_s, lump_ref)


def project(at_ref, z_s, x_s, out_ref):
    def plane(z, _):
        for y in range(6):
            for x, t in enumerate(thermo_back([at_ref[p * 36 + y * 6 + z] for p in range(6)])):
                x_s[y, x] = t
        for x in range(3):
            for y, t in enumerate(thermo_back([x_s[q, x] for q in range(6)])):
                z_s[z, 3 * x + y] = t
        return 0

    lax.fori_loop(0, 6, plane, 0)
    for n in range(9):
        for g, t in enumerate(thermo_back([z_s[q, n] for q in range(6)])):
            out_ref[3 * n + g] = t


def energy_kernel(power_ref, lump_ref, e_ref, out_ref, sum_s, z_s, x_s):
    project(power_ref, z_s, x_s, sum_s)

    def body(n, _):
        out_ref[n] = e_ref[n] + step_size * (sum_s[n] / lump_ref[n])
        return 0

    lax.fori_loop(0, 27, body, 0)


def point(jac, vel, energy, mass):
    cof = [
        [
            jac[(c + 1) % 3][(d + 1) % 3] * jac[(c + 2) % 3][(d + 2) % 3]
            - jac[(c + 1) % 3][(d + 2) % 3] * jac[(c + 2) % 3][(d + 1) % 3]
            for d in range(3)
        ]
        for c in range(3)
    ]
    det = jac[0][0] * cof[0][0] + jac[0][1] * cof[0][1] + jac[0][2] * cof[0][2]
    inv = pl.reciprocal(det, approx=True)
    inv = inv * (2.0 - det * inv)
    inv = inv * (2.0 - det * inv)
    scale = mass * inv
    shear = (viscosity * scale) * inv
    press = scale * energy
    rate = [
        [vel[c][0] * cof[e][0] + vel[c][1] * cof[e][1] + vel[c][2] * cof[e][2] for e in range(3)]
        for c in range(3)
    ]
    stress = [[None] * 3 for _ in range(3)]
    power = None
    for c in range(3):
        stress[c][c] = shear * (rate[c][c] + rate[c][c]) - press
        power = plus(power, stress[c][c] * rate[c][c])
        for d in range(c + 1, 3):
            both = rate[c][d] + rate[d][c]
            stress[c][d] = stress[d][c] = shear * both
            power = power + stress[c][d] * both
    flux = [
        [
            stress[c][0] * cof[0][f] + stress[c][1] * cof[1][f] + stress[c][2] * cof[2][f]
            for f in range(3)
        ]
        for c in range(3)
    ]
    return flux, power


def spread_y(first, row):
    sub = iotas()[0]
    return jnp.where(sub == 7, row, pltpu.roll(first, 7, 0))


def store_parts(nodes_of, minus_ref, plus_ref, inner_ref, rim_ref):
    sub = iotas()[0]

    def body(c, _):
        for g in range(3):
            nodes = nodes_of(c, g)
            for x in range(4):
                over = nodes[x][3]
                nodes[x][0] = nodes[x][0] + jnp.where(sub == 0, 0.0, pltpu.roll(over, 1, 0))
                r = c * 3 + g
                if x in (0, 3):
                    ref = minus_ref if x == 0 else plus_ref
                    ref[pl.ds(216 + r, 1), :] = over[7:8]
                    for b in range(3):
                        ref[pl.ds(pl.multiple_of((c * 9 + b * 3 + g) * 8, 8), 8), :] = nodes[x][b]
                else:
                    rim_ref[x - 1, pl.ds(r, 1), :] = over[7:8]
                    for b in range(3):
                        inner_ref[x - 1, c * 9 + b * 3 + g] = nodes[x][b]
        return 0

    lax.fori_loop(0, 3, body, 0)


def force_kernel(
    u_ref, hx_ref, hy_ref, hc_ref, eq_ref, w_ref,
    minus_ref, plus_ref, inner_ref, rim_ref, face_mask_ref, rim_mask_ref, power_ref,
    hx_s, hy_s, q_s, zv_s, zs_s, w_s, xt_s, ya_s, yb_s, zn_s, place,
):
    rows = [
        jnp.concatenate(
            [hy_ref[:, 128 * v : 128 * v + 128], hc_ref[:, 128 * v : 128 * v + 128]], axis=0
        )
        for v in range(3)
    ]
    rows = [jnp.concatenate([r, jnp.zeros((4, 128), F32)], axis=0) for r in rows]
    for t in range(5):
        for g, tile in enumerate(split_lanes([r[8 * t : 8 * t + 8] for r in rows])):
            hy_s[g, 8 * t : 8 * t + 8, :] = tile
    for x in range(4):
        for c in range(3):
            for g in range(3):
                r = 9 * x + 6 + c
                rim_mask_ref[x, c * 3 + g : c * 3 + g + 1, :] = 1.0 - hy_s[g, r : r + 1, :]

    def face(j, _):
        for i in range(3):
            k = 3 * j + i
            tiles = element_rows(lambda s, l: hx_ref[k, s : s + 8, l : l + 128], place.at[i])
            for n in range(9):
                hx_s[k, n] = tiles[n]
        return 0

    lax.fori_loop(0, 3, face, 0)
    for c in range(3):
        for n in range(9):
            face_mask_ref[c * 9 + n] = 1.0 - hx_s[6 + c, n]

    def gather_nodes(c, _):
        for g in range(3):
            cols = []
            for x in range(4):
                if x < 3:
                    u = [u_ref[c, x * 9 + b * 3 + g] for b in range(3)]
                else:
                    u = [hx_s[c, b * 3 + g] for b in range(3)]
                row = hy_s[g, pl.ds(9 * x + c, 1), :]
                u.append(spread_y(u[0], row))
                cols.append(butterfly(u))
            for y in range(4):
                for x, t in enumerate(butterfly([cols[x][y] for x in range(4)])):
                    q_s[c, (x * 4 + y) * 3 + g] = t
        return 0

    lax.fori_loop(0, 6, gather_nodes, 0)

    def along_z(c, _):
        for n in range(16):
            u = [q_s[c, 3 * n + g] for g in range(3)]
            u.append(next_lane(u[0]))
            h = butterfly(u)
            for q, t in enumerate(along(interp_pair, h)):
                zv_s[q, c, n] = t
            for q, t in enumerate(along(slope_pair, h)):
                zs_s[q, c, n] = t
        return 0

    lax.fori_loop(0, 6, along_z, 0)

    def plane(z, _):
        def along_y(c, _):
            for x in range(4):
                h = [zv_s[z, c, x * 4 + y] for y in range(4)]
                s = [zs_s[z, c, x * 4 + y] for y in range(4)]
                for q, t in enumerate(along(interp_pair, h)):
                    w_s[q, 0, c * 4 + x] = t
                for q, t in enumerate(along(slope_pair, h)):
                    w_s[q, 1, c * 4 + x] = t
                for q, t in enumerate(along(interp_pair, s)):
                    w_s[q, 2, c * 4 + x] = t
            return 0

        lax.fori_loop(0, 6, along_y, 0)

        def line(y, _):
            back = [[[None] * 4 for _ in range(3)] for _ in range(3)]
            for q in range(3):
                grads = [[[None] * 3 for _ in range(6)] for _ in range(2)]
                for c in range(6):
                    for d in range(3):
                        h = [w_s[y, d, c * 4 + x] for x in range(4)]
                        pair = slope_pair(h, q) if d == 0 else interp_pair(h, q)
                        for side in range(2):
                            t = pair[side]
                            grads[side][c][d] = t + 1.0 if c == d else t
                flux = []
                for side in range(2):
                    p = q if side == 0 else 5 - q
                    n = p * 36 + y * 6 + z
                    f, power_ref[n] = point(grads[side][:3], grads[side][3:], eq_ref[n], w_ref[n])
                    flux.append(f)
                for c in range(3):
                    for f in range(3):
                        even = flux[0][c][f] + flux[1][c][f]
                        odd = flux[0][c][f] - flux[1][c][f]
                        h = back[c][f]
                        for a in range(2):
                            if f == 0:
                                h[a] = plus(h[a], DE[q][a] * odd)
                                h[2 + a] = plus(h[2 + a], DO[q][a] * even)
                            else:
                                h[a] = plus(h[a], BE[q][a] * even)
                                h[2 + a] = plus(h[2 + a], BO[q][a] * odd)
            for c in range(3):
                for f in range(3):
                    for x in range(4):
                        xt_s[y, f, c * 4 + x] = back[c][f][x]
            return 0

        lax.fori_loop(0, 6, line, 0)

        def back_y(c, _):
            for x in range(4):
                f = [[xt_s[q, d, c * 4 + x] for q in range(6)] for d in range(3)]
                h = slope_back(f[1], interp_back(f[0]))
                s = interp_back(f[2])
                for y in range(4):
                    ya_s[z, c, x * 4 + y] = h[y]
                    yb_s[z, c, x * 4 + y] = s[y]
            return 0

        lax.fori_loop(0, 3, back_y, 0)
        return 0

    lax.fori_loop(0, 6, plane, 0)

    def back_z(c, _):
        for n in range(16):
            h = interp_back([ya_s[q, c, n] for q in range(6)], sign=-1.0)
            h = slope_back([yb_s[q, c, n] for q in range(6)], h, sign=-1.0)
            u = unbutterfly(h)
            zn_s[c, n * 3] = u[0] + previous_lane(u[3])
            zn_s[c, n * 3 + 1] = u[1]
            zn_s[c, n * 3 + 2] = u[2]
        return 0

    lax.fori_loop(0, 3, back_z, 0)
    store_parts(lambda c, g: nodes_from(zn_s, c, g), minus_ref, plus_ref, inner_ref, rim_ref)


def nodes_from(zn_s, c, g):
    cols = [unbutterfly([zn_s[c, (x * 4 + y) * 3 + g] for y in range(4)]) for x in range(4)]
    rows = [unbutterfly([cols[x][b] for x in range(4)]) for b in range(4)]
    return [[rows[b][x] for b in range(4)] for x in range(4)]


def rows_kernel(minus_ref, plus_ref, inner_ref, rim_ref, got_low_ref, got_high_ref, down_ref, up_ref):
    for c in range(3):
        for g in range(3):
            r = c * 3 + g
            n = (c * 9 + g) * 8
            down_ref[r : r + 1, :] = minus_ref[n : n + 1, :] + got_low_ref[n : n + 1, :]
            down_ref[27 + r : 28 + r, :] = plus_ref[n : n + 1, :] + got_high_ref[n : n + 1, :]
            for x in range(2):
                down_ref[9 * (x + 1) + r : 9 * (x + 1) + r + 1, :] = inner_ref[x, c * 9 + g, 0:1, :]
    up_ref[0:9, :] = minus_ref[216:225, :] + got_low_ref[216:225, :]
    up_ref[27:36, :] = plus_ref[216:225, :] + got_high_ref[216:225, :]
    for x in range(2):
        up_ref[9 * (x + 1) : 9 * (x + 1) + 9, :] = rim_ref[x, 0:9, :]


def assemble(c, parts, mask_ref, face_mask_ref, rim_mask_ref, own_ref, q_s):
    minus_ref, plus_ref, inner_ref, rim_ref, low_ref, high_ref, from_down_ref, from_up_ref = parts
    sub = iotas()[0]
    for g in range(3):
        r = c * 3 + g
        cols = []
        for x in range(4):
            u = []
            for b in range(3):
                n = c * 9 + b * 3 + g
                tile = pl.ds(pl.multiple_of(n * 8, 8), 8)
                if x == 0:
                    t = minus_ref[tile, :] + low_ref[tile, :]
                elif x == 3:
                    t = plus_ref[tile, :] + high_ref[tile, :]
                else:
                    t = inner_ref[x - 1, n]
                if b == 0:
                    below = from_down_ref[pl.ds(9 * x + r, 1), :]
                    t = t + jnp.where(sub == 0, below, 0.0)
                t = t * (face_mask_ref[n] if x == 3 else mask_ref[x, n])
                u.append(t)
                if x < 3:
                    own_ref[x, n] = t
            edge = pl.ds(216 + r, 1)
            if x == 0:
                top = minus_ref[edge, :] + low_ref[edge, :]
            elif x == 3:
                top = plus_ref[edge, :] + high_ref[edge, :]
            else:
                top = rim_ref[x - 1, pl.ds(r, 1), :]
            top = (top + from_up_ref[pl.ds(9 * x + r, 1), :]) * rim_mask_ref[x, pl.ds(r, 1), :]
            u.append(spread_y(u[0], top))
            cols.append(butterfly(u))
        for y in range(4):
            for x, t in enumerate(butterfly([cols[x][y] for x in range(4)])):
                q_s[c, (x * 4 + y) * 3 + g] = t


def mass_along_z(c, q_s, zv_s):
    for n in range(16):
        u = [q_s[c, 3 * n + g] for g in range(3)]
        u.append(next_lane(u[0]))
        for q, t in enumerate(along(interp_pair, butterfly(u))):
            zv_s[q, c, n] = t


def apply_kernel(
    minus_ref, plus_ref, inner_ref, rim_ref, low_ref, high_ref, from_down_ref, from_up_ref,
    mask_ref, face_mask_ref, rim_mask_ref, w_ref,
    own_ref, out_minus_ref, out_plus_ref, out_inner_ref, out_rim_ref,
    q_s, zv_s, xt_s, ya_s, zn_s,
):
    parts = (
        minus_ref, plus_ref, inner_ref, rim_ref, low_ref, high_ref, from_down_ref, from_up_ref,
    )

    def first(c, _):
        assemble(c, parts, mask_ref, face_mask_ref, rim_mask_ref, own_ref, q_s)
        mass_along_z(c, q_s, zv_s)
        return 0

    lax.fori_loop(0, 3, first, 0)

    def plane(z, _):
        for c in range(3):
            lines = [along(interp_pair, [zv_s[z, c, x * 4 + y] for y in range(4)]) for x in range(4)]
            for y in range(6):
                h = [lines[x][y] for x in range(4)]
                at = along(interp_pair, h)
                at = [at[p] * w_ref[p * 36 + y * 6 + z] for p in range(6)]
                for x, t in enumerate(interp_back(at)):
                    xt_s[c, x, y] = t
            for x in range(4):
                for y, t in enumerate(interp_back([xt_s[c, x, q] for q in range(6)])):
                    ya_s[z, c, x * 4 + y] = t
        return 0

    lax.fori_loop(0, 6, plane, 0)

    def back_z(c, _):
        for n in range(16):
            u = unbutterfly(interp_back([ya_s[q, c, n] for q in range(6)]))
            zn_s[c, n * 3] = u[0] + previous_lane(u[3])
            zn_s[c, n * 3 + 1] = u[1]
            zn_s[c, n * 3 + 2] = u[2]
        return 0

    lax.fori_loop(0, 3, back_z, 0)
    store_parts(
        lambda c, g: nodes_from(zn_s, c, g), out_minus_ref, out_plus_ref, out_inner_ref, out_rim_ref
    )


def total(t):
    return jnp.sum(jnp.sum(t, axis=0, keepdims=True), axis=1, keepdims=True)


def moments_kernel(
    minus_ref, plus_ref, inner_ref, rim_ref, low_ref, high_ref, from_down_ref, from_up_ref,
    mask_ref, face_mask_ref, rim_mask_ref, w_ref, r_ref, v_ref,
    own_ref, sums_ref, q_s, zv_s,
):
    parts = (
        minus_ref, plus_ref, inner_ref, rim_ref, low_ref, high_ref, from_down_ref, from_up_ref,
    )

    def first(c, _):
        assemble(c, parts, mask_ref, face_mask_ref, rim_mask_ref, own_ref, q_s)
        mass_along_z(c, q_s, zv_s)
        return 0

    lax.fori_loop(0, 3, first, 0)
    zero = jnp.zeros((8, 128), F32)

    def dots(n, s):
        s = list(s)
        for x in range(3):
            r, v, w = r_ref[x, n], v_ref[x, n], own_ref[x, n]
            s = [
                s[0] + r * r, s[1] + r * v, s[2] + v * v, s[3] + v * w, s[4] + w * w,
            ]
        return tuple(s)

    sums = lax.fori_loop(0, 27, dots, (zero,) * 5)

    def plane(z, s):
        s = list(s)
        for c in range(3):
            lines = [along(interp_pair, [zv_s[z, c, x * 4 + y] for y in range(4)]) for x in range(4)]
            for y in range(6):
                at = along(interp_pair, [lines[x][y] for x in range(4)])
                for p in range(6):
                    s[c] = s[c] + (at[p] * at[p]) * w_ref[p * 36 + y * 6 + z]
        return tuple(s)

    last = lax.fori_loop(0, 6, plane, (zero,) * 3)
    sums = list(sums) + [last[0] + last[1] + last[2]]
    lane = iotas(1)[1]
    row = jnp.zeros((1, 128), F32)
    for k in range(6):
        row = row + jnp.where(lane == k, total(sums[k]), 0.0)
    sums_ref[...] = jnp.broadcast_to(row, sums_ref.shape)


def coefficients(mu):
    unit = mu[1] / mu[0]
    m = [None] * 6
    scale = 1.0 / mu[0]
    for k in range(6):
        m[k] = mu[k] * scale
        scale = scale / unit
    a0 = m[0] / m[1]
    rr1 = a0 * a0 * m[2] - 2.0 * a0 * m[1] + m[0]
    b0 = rr1 / m[0]
    d1 = [1.0 + b0, -a0]
    a1 = rr1 / (d1[0] * d1[0] * m[1] + 2.0 * d1[0] * d1[1] * m[2] + d1[1] * d1[1] * m[3])
    p1 = -(a0 + a1 * d1[0])
    p2 = -a1 * d1[1]
    rr2 = (
        m[0] + p1 * p1 * m[2] + p2 * p2 * m[4]
        + 2.0 * (p1 * m[1] + p2 * m[2] + p1 * p2 * m[3])
    )
    b1 = rr2 / rr1
    q = [1.0 + b1 * d1[0], p1 + b1 * d1[1], p2]
    a2 = rr2 / (
        q[0] * q[0] * m[1] + q[1] * q[1] * m[3] + q[2] * q[2] * m[5]
        + 2.0 * (q[0] * q[1] * m[2] + q[0] * q[2] * m[3] + q[1] * q[2] * m[4])
    )
    x = [a0 + a1 * d1[0] + a2 * q[0], a1 * d1[1] + a2 * q[1], a2 * q[2]]
    return [x[0] / unit, x[1] / (unit * unit), x[2] / (unit * unit * unit)]


def final_kernel(
    sums_ref, r_ref, v_ref, w_ref, d_ref, vel_ref, a_out, v_out, d_out, place, a_s, v_s, d_s, sems
):
    lane = iotas(1)[1]
    row = jnp.sum(sums_ref[...], axis=0, keepdims=True)
    mu = [
        jnp.broadcast_to(jnp.sum(jnp.where(lane == k, row, 0.0), axis=1, keepdims=True), (8, 128))
        for k in range(6)
    ]
    k0, k1, k2 = coefficients(mu)

    def copies(c):
        pairs = ((a_s, a_out), (v_s, v_out), (d_s, d_out))
        return [
            pltpu.make_async_copy(src.at[c], dst.at[c], sems.at[c, i])
            for i, (src, dst) in enumerate(pairs)
        ]

    def body(c, _):
        for x in range(3):
            for b in range(3):
                for g in range(3):
                    n = c * 9 + b * 3 + g
                    place[x, g, pl.ds(b, 8, stride=3), :] = (
                        k0 * r_ref[x, n] + k1 * v_ref[x, n] + k2 * w_ref[x, n]
                    )
            for s in range(3):
                rows = slice(8 * s, 8 * s + 8)
                for v, t in enumerate(join_lanes([place[x, g, rows, :] for g in range(3)])):
                    lanes = slice(128 * v, 128 * v + 128)
                    a_s[c, x, rows, lanes] = t
                    new = vel_ref[c, x, rows, lanes] + step_size * t
                    v_s[c, x, rows, lanes] = new
                    d_s[c, x, rows, lanes] = d_ref[c, x, rows, lanes] + step_size * new
        for copy in copies(c):
            copy.start()
        return 0

    lax.fori_loop(0, 3, body, 0)
    for c in range(3):
        for copy in copies(c):
            copy.wait()


def call(kernel, outs, scratch, name, flops=0, **more):
    def run(*args):
        moved = sum(a.size * 4 for a in args) + sum(4 * math.prod(s) for s in outs)
        return pl.pallas_call(
            kernel,
            out_shape=[jax.ShapeDtypeStruct(s, F32) for s in outs],
            scratch_shapes=[pltpu.VMEM(s, F32) if isinstance(s, tuple) else s for s in scratch],
            compiler_params=pltpu.CompilerParams(vmem_limit_bytes=VMEM_LIMIT),
            cost_estimate=pl.CostEstimate(flops=flops, bytes_accessed=moved, transcendentals=0),
            name=name,
            **more,
        )(*args)

    return run


T = (8, 128)
FACE = (232, 128)
PARTS = [FACE, FACE, (2, 27) + T, (2, 16, 128)]


def solution(mesh):
    gx, gy = mesh.shape["gx"], mesh.shape["gy"]

    def moved(value, by_x, by_y):
        pairs = [
            (i * gy + j, ((i + by_x) % gx) * gy + (j + by_y) % gy)
            for i in range(gx)
            for j in range(gy)
        ]
        return lax.ppermute(value, ("gx", "gy"), pairs)

    def complete(parts):
        minus, plus_face, inner, rim = parts
        low = moved(plus_face, 1, 0)
        high = moved(minus, -1, 0)
        down, up = call(rows_kernel, [(40, 128), (40, 128)], [], "rows")(
            minus, plus_face, inner, rim, low, high
        )
        from_up = moved(down, 0, -1)
        from_down = moved(up, 0, 1)
        return (minus, plus_face, inner, rim, low, high, from_down, from_up)

    def on_device(displacement, velocity, energy, mass_weight, pinned):
        weight = mass_weight.reshape((216,) + T)
        dofs = energy.reshape((27,) + T)
        flags = pinned.dtype
        face, row, corner = call(
            pack_kernel,
            [(9, 24, 384), (27, 384), (9, 384)],
            [
                (2, 3, 24, 384), pltpu.VMEM((3, 24, 384), flags), (2, 3, 3, 8, 384),
                pltpu.VMEM((3, 3, 8, 384), flags), pltpu.SemaphoreType.DMA((6,)),
            ],
            "pack",
            in_specs=[pl.BlockSpec(memory_space=pltpu.HBM)] * 3,
        )(displacement, velocity, pinned)
        hx = moved(face, -1, 0)
        hy = moved(row, 0, -1)
        hc = moved(corner, -1, -1)
        nodes, mask, heat, lump = call(
            prep_kernel,
            [(6, 27) + T, (3, 27) + T, (216,) + T, (27,) + T],
            [(9, 3, 24, 128), (6, 9) + T, (6, 3) + T],
            "prep",
            flops=4000 * 1024,
        )(displacement, velocity, pinned, dofs, weight)
        out = call(
            force_kernel,
            PARTS + [(27,) + T, (4, 16, 128), (216,) + T],
            [
                (9, 9) + T, (3, 40, 128), (6, 48) + T, (6, 6, 16) + T, (6, 6, 16) + T,
                (6, 3, 24) + T, (6, 3, 12) + T, (6, 3, 16) + T,
                (6, 3, 16) + T, (3, 48) + T, (3, 3, 24, 128),
            ],
            "force",
            flops=90000 * 1024,
        )(nodes, hx, hy, hc, heat, weight)
        parts, (face_mask, rim_mask, power) = out[:4], out[4:]
        (energy_new,) = call(
            energy_kernel, [(27,) + T], [(27,) + T, (6, 9) + T, (6, 3) + T], "energy",
            flops=2000 * 1024,
        )(power, lump, dofs)
        masks = (mask, face_mask, rim_mask)
        scratch = [
            (3, 48) + T, (6, 3, 16) + T, (3, 4, 6) + T, (6, 3, 16) + T, (3, 48) + T,
        ]
        apply = call(apply_kernel, [(3, 27) + T] + PARTS, scratch, "apply", flops=13000 * 1024)
        out = apply(*complete(parts), *masks, weight)
        r, parts = out[0], out[1:]
        out = apply(*complete(parts), *masks, weight)
        v, parts = out[0], out[1:]
        w, sums = call(
            moments_kernel, [(3, 27) + T, (gx * gy, 128)], scratch[:2], "moments", flops=8000 * 1024
        )(*complete(parts), *masks, weight, r, v)
        sums = sums.reshape(gx * gy, -1, 128)
        sums = lax.all_to_all(sums, ("gx", "gy"), 0, 0).reshape(-1, 128)
        shape = displacement.shape
        acceleration, velocity_new, displacement_new = call(
            final_kernel,
            [shape] * 3,
            [(3, 3, 24, 128), shape, shape, shape, pltpu.SemaphoreType.DMA((3, 3))],
            "final",
            flops=1000 * 1024,
            out_specs=[pl.BlockSpec(memory_space=pltpu.HBM)] * 3,
        )(sums, r, v, w, displacement, velocity)
        return acceleration, velocity_new, displacement_new, energy_new.reshape(energy.shape)

    spec = P(None, "gx", "gy", None)
    return jax.shard_map(
        on_device, mesh=mesh, in_specs=(spec,) * 5, out_specs=(spec,) * 4, check_vma=False
    )
```

```python
import math

import jax
import jax.numpy as jnp
import numpy as np
from jax import lax
from jax.experimental import pallas as pl
from jax.experimental.pallas import tpu as pltpu
from jax.sharding import PartitionSpec as P

step_size = 0.05
viscosity = 0.3
gamma_less = 0.4
F32 = jnp.float32
VMEM_LIMIT = 32 * 1024 * 1024


def tables():
    root_five = 1.0 / math.sqrt(5.0)
    lobatto = np.array([0.0, 0.5 - 0.5 * root_five, 0.5 + 0.5 * root_five, 1.0])
    legendre = np.array(
        [
            -0.932469514203152,
            -0.6612093864662645,
            -0.2386191860831909,
            0.2386191860831909,
            0.6612093864662645,
            0.932469514203152,
        ]
    )
    t = 0.5 + 0.5 * legendre
    values = np.ones((6, 4))
    slopes = np.zeros((6, 4))
    for a in range(4):
        for b in range(4):
            if b != a:
                values[:, a] *= (t - lobatto[b]) / (lobatto[a] - lobatto[b])
        for c in range(4):
            if c != a:
                term = np.ones(6) / (lobatto[a] - lobatto[c])
                for b in range(4):
                    if b != a and b != c:
                        term = term * (t - lobatto[b]) / (lobatto[a] - lobatto[b])
                slopes[:, a] += term
    thermo = np.stack([(1.0 - t) * (1.0 - t), 2.0 * t * (1.0 - t), t * t], axis=1)
    return values, slopes, thermo


def even_odd(matrix):
    even = [[float((matrix[q, a] + matrix[q, 3 - a]) / 2) for a in range(2)] for q in range(3)]
    odd = [[float((matrix[q, a] - matrix[q, 3 - a]) / 2) for a in range(2)] for q in range(3)]
    return even, odd


VALUES, SLOPES, THERMO = tables()
BE, BO = even_odd(VALUES)
DE, DO = even_odd(SLOPES)
TE = [float((THERMO[q, 0] + THERMO[q, 2]) / 2) for q in range(3)]
TO = [float((THERMO[q, 0] - THERMO[q, 2]) / 2) for q in range(3)]
TM = [float(THERMO[q, 1]) for q in range(3)]


def butterfly(u):
    return [u[0] + u[3], u[1] + u[2], u[0] - u[3], u[1] - u[2]]


def unbutterfly(r):
    return [r[0] + r[2], r[1] + r[3], r[1] - r[3], r[0] - r[2]]


def interp_pair(h, q):
    even = BE[q][0] * h[0] + BE[q][1] * h[1]
    odd = BO[q][0] * h[2] + BO[q][1] * h[3]
    return even + odd, even - odd


def slope_pair(h, q):
    even = DE[q][0] * h[0] + DE[q][1] * h[1]
    odd = DO[q][0] * h[2] + DO[q][1] * h[3]
    return odd + even, odd - even


def along(pair_fn, h):
    out = [None] * 6
    for q in range(3):
        out[q], out[5 - q] = pair_fn(h, q)
    return out


def plus(total, term):
    return term if total is None else total + term


def interp_back(f, h=None, sign=1.0):
    h = [None] * 4 if h is None else list(h)
    for q in range(3):
        even, odd = f[q] + f[5 - q], f[q] - f[5 - q]
        for a in range(2):
            h[a] = plus(h[a], (sign * BE[q][a]) * even)
            h[2 + a] = plus(h[2 + a], (sign * BO[q][a]) * odd)
    return h


def slope_back(f, h=None, sign=1.0):
    h = [None] * 4 if h is None else list(h)
    for q in range(3):
        even, odd = f[q] + f[5 - q], f[q] - f[5 - q]
        for a in range(2):
            h[a] = plus(h[a], (sign * DE[q][a]) * odd)
            h[2 + a] = plus(h[2 + a], (sign * DO[q][a]) * even)
    return h


def thermo_along(u):
    even, odd, mid = u[0] + u[2], u[0] - u[2], u[1]
    out = [None] * 6
    for q in range(3):
        both, one = TE[q] * even + TM[q] * mid, TO[q] * odd
        out[q], out[5 - q] = both + one, both - one
    return out


def thermo_back(f):
    even = mid = odd = None
    for q in range(3):
        both, one = f[q] + f[5 - q], f[q] - f[5 - q]
        even = plus(even, TE[q] * both)
        mid = plus(mid, TM[q] * both)
        odd = plus(odd, TO[q] * one)
    return [even + odd, mid, even - odd]


def iotas(rows=8):
    shape = (rows, 128)
    return lax.broadcasted_iota(jnp.int32, shape, 0), lax.broadcasted_iota(jnp.int32, shape, 1)


def gather_lanes(x, index):
    return jnp.take_along_axis(x, index, axis=1, mode="promise_in_bounds")


def split_lanes(parts, rows=8):
    lane = iotas(rows)[1]
    out = []
    for g in range(3):
        place = 3 * lane + g
        index = place & 127
        moved = [gather_lanes(p, index) for p in parts]
        out.append(
            jnp.where(place < 128, moved[0], jnp.where(place < 256, moved[1], moved[2]))
        )
    return out


def join_lanes(parts):
    lane = iotas()[1]
    out = []
    for v in range(3):
        place = lane + 128 * v
        index = place // 3
        g = place - 3 * index
        moved = [gather_lanes(p, index) for p in parts]
        out.append(jnp.where(g == 0, moved[0], jnp.where(g == 1, moved[1], moved[2])))
    return out


def next_lane(x):
    return pltpu.roll(x, 127, 1)


def previous_lane(x):
    return pltpu.roll(x, 1, 1)


def pack_kernel(d_ref, v_ref, f_ref, x_ref, y_ref, c_ref, face, face_f, low, low_f, sems):
    copies = []
    for n, ref in enumerate((d_ref, v_ref, f_ref)):
        to_face, to_low = (face.at[n], low.at[n]) if n < 2 else (face_f, low_f)
        copies.append(pltpu.make_async_copy(ref.at[:, 0], to_face, sems.at[2 * n]))
        copies.append(pltpu.make_async_copy(ref.at[:, :, 0:8], to_low, sems.at[2 * n + 1]))
    for copy in copies:
        copy.start()
    for copy in copies:
        copy.wait()
    for n in range(3):
        for c in range(3):
            k = 3 * n + c
            layer = (face[n, c] if n < 2 else face_f[c]).astype(F32)
            x_ref[k] = layer
            c_ref[k : k + 1, :] = layer[0:1]
            for x in range(3):
                r = 9 * x + k
                row = low[n, c, x, 0:1, :] if n < 2 else low_f[c, x, 0:1, :]
                y_ref[r : r + 1, :] = row.astype(F32)


def element_rows(load, place):
    for t in range(3):
        tiles = split_lanes([load(8 * t, 128 * v) for v in range(3)])
        for g in range(3):
            place[g, 8 * t : 8 * t + 8, :] = tiles[g]
    return [place[g, pl.ds(b, 8, stride=3), :] for b in range(3) for g in range(3)]


def prep_kernel(d_ref, v_ref, f_ref, e_ref, w_ref, u_ref, m_ref, eq_ref, lump_ref, place, ez_s, ey_s):
    def body(c, _):
        for x in range(3):
            for k, ref in enumerate((d_ref, v_ref, f_ref)):
                tiles = element_rows(
                    lambda s, l: ref[c, x, s : s + 8, l : l + 128].astype(F32), place.at[3 * x + k]
                )
                for n in range(9):
                    if k < 2:
                        u_ref[3 * k + c, x * 9 + n] = tiles[n]
                    else:
                        m_ref[x, c * 9 + n] = 1.0 - tiles[n]
        return 0

    lax.fori_loop(0, 3, body, 0)
    for n in range(9):
        for q, t in enumerate(thermo_along([gamma_less * e_ref[3 * n + g] for g in range(3)])):
            ez_s[q, n] = t

    def plane(z, _):
        for x in range(3):
            for q, t in enumerate(thermo_along([ez_s[z, 3 * x + y] for y in range(3)])):
                ey_s[q, x] = t
        for y in range(6):
            for q, t in enumerate(thermo_along([ey_s[y, x] for x in range(3)])):
                eq_ref[q * 36 + y * 6 + z] = t
        return 0

    lax.fori_loop(0, 6, plane, 0)
    project(w_ref, ez_s, ey_s, lump_ref)


def project(at_ref, z_s, x_s, out_ref):
    def plane(z, _):
        for y in range(6):
            for x, t in enumerate(thermo_back([at_ref[p * 36 + y * 6 + z] for p in range(6)])):
                x_s[y, x] = t
        for x in range(3):
            for y, t in enumerate(thermo_back([x_s[q, x] for q in range(6)])):
                z_s[z, 3 * x + y] = t
        return 0

    lax.fori_loop(0, 6, plane, 0)
    for n in range(9):
        for g, t in enumerate(thermo_back([z_s[q, n] for q in range(6)])):
            out_ref[3 * n + g] = t


def energy_kernel(power_ref, lump_ref, e_ref, out_ref, token_ref, sum_s, z_s, x_s):
    project(power_ref, z_s, x_s, sum_s)

    def body(n, _):
        out_ref[n] = e_ref[n] + step_size * (sum_s[n] / lump_ref[n])
        return 0

    lax.fori_loop(0, 27, body, 0)
    token_ref[...] = sum_s[0]


def point(jac, vel, energy, mass):
    cof = [
        [
            jac[(c + 1) % 3][(d + 1) % 3] * jac[(c + 2) % 3][(d + 2) % 3]
            - jac[(c + 1) % 3][(d + 2) % 3] * jac[(c + 2) % 3][(d + 1) % 3]
            for d in range(3)
        ]
        for c in range(3)
    ]
    det = jac[0][0] * cof[0][0] + jac[0][1] * cof[0][1] + jac[0][2] * cof[0][2]
    inv = pl.reciprocal(det, approx=True)
    inv = inv * (2.0 - det * inv)
    inv = inv * (2.0 - det * inv)
    scale = mass * inv
    shear = (viscosity * scale) * inv
    press = scale * energy
    rate = [
        [vel[c][0] * cof[e][0] + vel[c][1] * cof[e][1] + vel[c][2] * cof[e][2] for e in range(3)]
        for c in range(3)
    ]
    stress = [[None] * 3 for _ in range(3)]
    power = None
    for c in range(3):
        stress[c][c] = shear * (rate[c][c] + rate[c][c]) - press
        power = plus(power, stress[c][c] * rate[c][c])
        for d in range(c + 1, 3):
            both = rate[c][d] + rate[d][c]
            stress[c][d] = stress[d][c] = shear * both
            power = power + stress[c][d] * both
    flux = [
        [
            stress[c][0] * cof[0][f] + stress[c][1] * cof[1][f] + stress[c][2] * cof[2][f]
            for f in range(3)
        ]
        for c in range(3)
    ]
    return flux, power


def spread_y(first, row):
    sub = iotas()[0]
    return jnp.where(sub == 7, row, pltpu.roll(first, 7, 0))


def store_parts(nodes_of, minus_ref, plus_ref, inner_ref, rim_ref):
    sub = iotas()[0]

    def body(c, _):
        for g in range(3):
            nodes = nodes_of(c, g)
            for x in range(4):
                over = nodes[x][3]
                nodes[x][0] = nodes[x][0] + jnp.where(sub == 0, 0.0, pltpu.roll(over, 1, 0))
                r = c * 3 + g
                if x in (0, 3):
                    ref = minus_ref if x == 0 else plus_ref
                    ref[pl.ds(216 + r, 1), :] = over[7:8]
                    for b in range(3):
                        ref[pl.ds(pl.multiple_of((c * 9 + b * 3 + g) * 8, 8), 8), :] = nodes[x][b]
                else:
                    rim_ref[x - 1, pl.ds(r, 1), :] = over[7:8]
                    for b in range(3):
                        inner_ref[x - 1, c * 9 + b * 3 + g] = nodes[x][b]
        return 0

    lax.fori_loop(0, 3, body, 0)


def force_kernel(
    u_ref, hx_ref, hy_ref, hc_ref, eq_ref, w_ref,
    minus_ref, plus_ref, inner_ref, rim_ref, face_mask_ref, rim_mask_ref, power_ref,
    hx_s, hy_s, q_s, zv_s, zs_s, w_s, xt_s, ya_s, yb_s, zn_s, place,
):
    rows = [
        jnp.concatenate(
            [hy_ref[:, 128 * v : 128 * v + 128], hc_ref[:, 128 * v : 128 * v + 128]], axis=0
        )
        for v in range(3)
    ]
    rows = [jnp.concatenate([r, jnp.zeros((4, 128), F32)], axis=0) for r in rows]
    for t in range(5):
        for g, tile in enumerate(split_lanes([r[8 * t : 8 * t + 8] for r in rows])):
            hy_s[g, 8 * t : 8 * t + 8, :] = tile
    for x in range(4):
        for c in range(3):
            for g in range(3):
                r = 9 * x + 6 + c
                rim_mask_ref[x, c * 3 + g : c * 3 + g + 1, :] = 1.0 - hy_s[g, r : r + 1, :]

    def face(j, _):
        for i in range(3):
            k = 3 * j + i
            tiles = element_rows(lambda s, l: hx_ref[k, s : s + 8, l : l + 128], place.at[i])
            for n in range(9):
                hx_s[k, n] = tiles[n]
        return 0

    lax.fori_loop(0, 3, face, 0)
    for c in range(3):
        for n in range(9):
            face_mask_ref[c * 9 + n] = 1.0 - hx_s[6 + c, n]

    def gather_nodes(c, _):
        for g in range(3):
            cols = []
            for x in range(4):
                if x < 3:
                    u = [u_ref[c, x * 9 + b * 3 + g] for b in range(3)]
                else:
                    u = [hx_s[c, b * 3 + g] for b in range(3)]
                row = hy_s[g, pl.ds(9 * x + c, 1), :]
                u.append(spread_y(u[0], row))
                cols.append(butterfly(u))
            for y in range(4):
                for x, t in enumerate(butterfly([cols[x][y] for x in range(4)])):
                    q_s[c, (x * 4 + y) * 3 + g] = t
        return 0

    lax.fori_loop(0, 6, gather_nodes, 0)

    def along_z(c, _):
        for n in range(16):
            u = [q_s[c, 3 * n + g] for g in range(3)]
            u.append(next_lane(u[0]))
            h = butterfly(u)
            for q, t in enumerate(along(interp_pair, h)):
                zv_s[q, c, n] = t
            for q, t in enumerate(along(slope_pair, h)):
                zs_s[q, c, n] = t
        return 0

    lax.fori_loop(0, 6, along_z, 0)

    def plane(z, _):
        def along_y(c, _):
            for x in range(4):
                h = [zv_s[z, c, x * 4 + y] for y in range(4)]
                s = [zs_s[z, c, x * 4 + y] for y in range(4)]
                for q, t in enumerate(along(interp_pair, h)):
                    w_s[q, 0, c * 4 + x] = t
                for q, t in enumerate(along(slope_pair, h)):
                    w_s[q, 1, c * 4 + x] = t
                for q, t in enumerate(along(interp_pair, s)):
                    w_s[q, 2, c * 4 + x] = t
            return 0

        lax.fori_loop(0, 6, along_y, 0)

        def line(y, _):
            back = [[[None] * 4 for _ in range(3)] for _ in range(3)]
            for q in range(3):
                grads = [[[None] * 3 for _ in range(6)] for _ in range(2)]
                for c in range(6):
                    for d in range(3):
                        h = [w_s[y, d, c * 4 + x] for x in range(4)]
                        pair = slope_pair(h, q) if d == 0 else interp_pair(h, q)
                        for side in range(2):
                            t = pair[side]
                            grads[side][c][d] = t + 1.0 if c == d else t
                flux = []
                for side in range(2):
                    p = q if side == 0 else 5 - q
                    n = p * 36 + y * 6 + z
                    f, power_ref[n] = point(grads[side][:3], grads[side][3:], eq_ref[n], w_ref[n])
                    flux.append(f)
                for c in range(3):
                    for f in range(3):
                        even = flux[0][c][f] + flux[1][c][f]
                        odd = flux[0][c][f] - flux[1][c][f]
                        h = back[c][f]
                        for a in range(2):
                            if f == 0:
                                h[a] = plus(h[a], DE[q][a] * odd)
                                h[2 + a] = plus(h[2 + a], DO[q][a] * even)
                            else:
                                h[a] = plus(h[a], BE[q][a] * even)
                                h[2 + a] = plus(h[2 + a], BO[q][a] * odd)
            for c in range(3):
                for f in range(3):
                    for x in range(4):
                        xt_s[y, f, c * 4 + x] = back[c][f][x]
            return 0

        lax.fori_loop(0, 6, line, 0)

        def back_y(c, _):
            for x in range(4):
                f = [[xt_s[q, d, c * 4 + x] for q in range(6)] for d in range(3)]
                h = slope_back(f[1], interp_back(f[0]))
                s = interp_back(f[2])
                for y in range(4):
                    ya_s[z, c, x * 4 + y] = h[y]
                    yb_s[z, c, x * 4 + y] = s[y]
            return 0

        lax.fori_loop(0, 3, back_y, 0)
        return 0

    lax.fori_loop(0, 6, plane, 0)

    def back_z(c, _):
        for n in range(16):
            h = interp_back([ya_s[q, c, n] for q in range(6)], sign=-1.0)
            h = slope_back([yb_s[q, c, n] for q in range(6)], h, sign=-1.0)
            u = unbutterfly(h)
            zn_s[c, n * 3] = u[0] + previous_lane(u[3])
            zn_s[c, n * 3 + 1] = u[1]
            zn_s[c, n * 3 + 2] = u[2]
        return 0

    lax.fori_loop(0, 3, back_z, 0)
    store_parts(lambda c, g: nodes_from(zn_s, c, g), minus_ref, plus_ref, inner_ref, rim_ref)


def nodes_from(zn_s, c, g):
    cols = [unbutterfly([zn_s[c, (x * 4 + y) * 3 + g] for y in range(4)]) for x in range(4)]
    rows = [unbutterfly([cols[x][b] for x in range(4)]) for b in range(4)]
    return [[rows[b][x] for b in range(4)] for x in range(4)]


def rows_kernel(minus_ref, plus_ref, inner_ref, rim_ref, got_low_ref, got_high_ref, *rest):
    down_ref, up_ref = rest[-2:]
    for c in range(3):
        for g in range(3):
            r = c * 3 + g
            n = (c * 9 + g) * 8
            down_ref[r : r + 1, :] = minus_ref[n : n + 1, :] + got_low_ref[n : n + 1, :]
            down_ref[27 + r : 28 + r, :] = plus_ref[n : n + 1, :] + got_high_ref[n : n + 1, :]
            for x in range(2):
                down_ref[9 * (x + 1) + r : 9 * (x + 1) + r + 1, :] = inner_ref[x, c * 9 + g, 0:1, :]
    up_ref[0:9, :] = minus_ref[216:225, :] + got_low_ref[216:225, :]
    up_ref[27:36, :] = plus_ref[216:225, :] + got_high_ref[216:225, :]
    for x in range(2):
        up_ref[9 * (x + 1) : 9 * (x + 1) + 9, :] = rim_ref[x, 0:9, :]


def assemble(c, parts, mask_ref, face_mask_ref, rim_mask_ref, own_ref, q_s):
    minus_ref, plus_ref, inner_ref, rim_ref, low_ref, high_ref, from_down_ref, from_up_ref = parts
    sub = iotas()[0]
    for g in range(3):
        r = c * 3 + g
        cols = []
        for x in range(4):
            u = []
            for b in range(3):
                n = c * 9 + b * 3 + g
                tile = pl.ds(pl.multiple_of(n * 8, 8), 8)
                if x == 0:
                    t = minus_ref[tile, :] + low_ref[tile, :]
                elif x == 3:
                    t = plus_ref[tile, :] + high_ref[tile, :]
                else:
                    t = inner_ref[x - 1, n]
                if b == 0:
                    below = from_down_ref[pl.ds(9 * x + r, 1), :]
                    t = t + jnp.where(sub == 0, below, 0.0)
                t = t * (face_mask_ref[n] if x == 3 else mask_ref[x, n])
                u.append(t)
                if x < 3:
                    own_ref[x, n] = t
            edge = pl.ds(216 + r, 1)
            if x == 0:
                top = minus_ref[edge, :] + low_ref[edge, :]
            elif x == 3:
                top = plus_ref[edge, :] + high_ref[edge, :]
            else:
                top = rim_ref[x - 1, pl.ds(r, 1), :]
            top = (top + from_up_ref[pl.ds(9 * x + r, 1), :]) * rim_mask_ref[x, pl.ds(r, 1), :]
            u.append(spread_y(u[0], top))
            cols.append(butterfly(u))
        for y in range(4):
            for x, t in enumerate(butterfly([cols[x][y] for x in range(4)])):
                q_s[c, (x * 4 + y) * 3 + g] = t


def mass_along_z(c, q_s, zv_s):
    for n in range(16):
        u = [q_s[c, 3 * n + g] for g in range(3)]
        u.append(next_lane(u[0]))
        for q, t in enumerate(along(interp_pair, butterfly(u))):
            zv_s[q, c, n] = t


def apply_kernel(
    minus_ref, plus_ref, inner_ref, rim_ref, low_ref, high_ref, from_down_ref, from_up_ref,
    mask_ref, face_mask_ref, rim_mask_ref, w_ref,
    own_ref, out_minus_ref, out_plus_ref, out_inner_ref, out_rim_ref,
    q_s, zv_s, xt_s, ya_s, zn_s,
):
    parts = (
        minus_ref, plus_ref, inner_ref, rim_ref, low_ref, high_ref, from_down_ref, from_up_ref,
    )

    def first(c, _):
        assemble(c, parts, mask_ref, face_mask_ref, rim_mask_ref, own_ref, q_s)
        mass_along_z(c, q_s, zv_s)
        return 0

    lax.fori_loop(0, 3, first, 0)

    def plane(z, _):
        for c in range(3):
            lines = [along(interp_pair, [zv_s[z, c, x * 4 + y] for y in range(4)]) for x in range(4)]
            for y in range(6):
                h = [lines[x][y] for x in range(4)]
                at = along(interp_pair, h)
                at = [at[p] * w_ref[p * 36 + y * 6 + z] for p in range(6)]
                for x, t in enumerate(interp_back(at)):
                    xt_s[c, x, y] = t
            for x in range(4):
                for y, t in enumerate(interp_back([xt_s[c, x, q] for q in range(6)])):
                    ya_s[z, c, x * 4 + y] = t
        return 0

    lax.fori_loop(0, 6, plane, 0)

    def back_z(c, _):
        for n in range(16):
            u = unbutterfly(interp_back([ya_s[q, c, n] for q in range(6)]))
            zn_s[c, n * 3] = u[0] + previous_lane(u[3])
            zn_s[c, n * 3 + 1] = u[1]
            zn_s[c, n * 3 + 2] = u[2]
        return 0

    lax.fori_loop(0, 3, back_z, 0)
    store_parts(
        lambda c, g: nodes_from(zn_s, c, g), out_minus_ref, out_plus_ref, out_inner_ref, out_rim_ref
    )


def total(t):
    return jnp.sum(jnp.sum(t, axis=0, keepdims=True), axis=1, keepdims=True)


def moments_kernel(
    minus_ref, plus_ref, inner_ref, rim_ref, low_ref, high_ref, from_down_ref, from_up_ref,
    mask_ref, face_mask_ref, rim_mask_ref, w_ref, r_ref, v_ref,
    own_ref, sums_ref, q_s, zv_s,
):
    parts = (
        minus_ref, plus_ref, inner_ref, rim_ref, low_ref, high_ref, from_down_ref, from_up_ref,
    )

    def first(c, _):
        assemble(c, parts, mask_ref, face_mask_ref, rim_mask_ref, own_ref, q_s)
        mass_along_z(c, q_s, zv_s)
        return 0

    lax.fori_loop(0, 3, first, 0)
    zero = jnp.zeros((8, 128), F32)

    def dots(n, s):
        s = list(s)
        for x in range(3):
            r, v, w = r_ref[x, n], v_ref[x, n], own_ref[x, n]
            s = [
                s[0] + r * r, s[1] + r * v, s[2] + v * v, s[3] + v * w, s[4] + w * w,
            ]
        return tuple(s)

    sums = lax.fori_loop(0, 27, dots, (zero,) * 5)

    def plane(z, s):
        s = list(s)
        for c in range(3):
            lines = [along(interp_pair, [zv_s[z, c, x * 4 + y] for y in range(4)]) for x in range(4)]
            for y in range(6):
                at = along(interp_pair, [lines[x][y] for x in range(4)])
                for p in range(6):
                    s[c] = s[c] + (at[p] * at[p]) * w_ref[p * 36 + y * 6 + z]
        return tuple(s)

    last = lax.fori_loop(0, 6, plane, (zero,) * 3)
    sums = list(sums) + [last[0] + last[1] + last[2]]
    lane = iotas(1)[1]
    row = jnp.zeros((1, 128), F32)
    for k in range(6):
        row = row + jnp.where(lane == k, total(sums[k]), 0.0)
    sums_ref[...] = jnp.broadcast_to(row, sums_ref.shape)


def coefficients(mu):
    unit = mu[1] / mu[0]
    m = [None] * 6
    scale = 1.0 / mu[0]
    for k in range(6):
        m[k] = mu[k] * scale
        scale = scale / unit
    a0 = m[0] / m[1]
    rr1 = a0 * a0 * m[2] - 2.0 * a0 * m[1] + m[0]
    b0 = rr1 / m[0]
    d1 = [1.0 + b0, -a0]
    a1 = rr1 / (d1[0] * d1[0] * m[1] + 2.0 * d1[0] * d1[1] * m[2] + d1[1] * d1[1] * m[3])
    p1 = -(a0 + a1 * d1[0])
    p2 = -a1 * d1[1]
    rr2 = (
        m[0] + p1 * p1 * m[2] + p2 * p2 * m[4]
        + 2.0 * (p1 * m[1] + p2 * m[2] + p1 * p2 * m[3])
    )
    b1 = rr2 / rr1
    q = [1.0 + b1 * d1[0], p1 + b1 * d1[1], p2]
    a2 = rr2 / (
        q[0] * q[0] * m[1] + q[1] * q[1] * m[3] + q[2] * q[2] * m[5]
        + 2.0 * (q[0] * q[1] * m[2] + q[0] * q[2] * m[3] + q[1] * q[2] * m[4])
    )
    x = [a0 + a1 * d1[0] + a2 * q[0], a1 * d1[1] + a2 * q[1], a2 * q[2]]
    return [x[0] / unit, x[1] / (unit * unit), x[2] / (unit * unit * unit)]


def final_kernel(
    sums_ref, r_ref, v_ref, w_ref, d_ref, vel_ref, a_out, v_out, d_out, place, a_s, v_s, d_s, sems
):
    lane = iotas(1)[1]
    row = jnp.sum(sums_ref[...], axis=0, keepdims=True)
    mu = [
        jnp.broadcast_to(jnp.sum(jnp.where(lane == k, row, 0.0), axis=1, keepdims=True), (8, 128))
        for k in range(6)
    ]
    k0, k1, k2 = coefficients(mu)

    def copies(c):
        pairs = ((a_s, a_out), (v_s, v_out), (d_s, d_out))
        return [
            pltpu.make_async_copy(src.at[c], dst.at[c], sems.at[c, i])
            for i, (src, dst) in enumerate(pairs)
        ]

    def body(c, _):
        for x in range(3):
            for b in range(3):
                for g in range(3):
                    n = c * 9 + b * 3 + g
                    place[x, g, pl.ds(b, 8, stride=3), :] = (
                        k0 * r_ref[x, n] + k1 * v_ref[x, n] + k2 * w_ref[x, n]
                    )
            for s in range(3):
                rows = slice(8 * s, 8 * s + 8)
                for v, t in enumerate(join_lanes([place[x, g, rows, :] for g in range(3)])):
                    lanes = slice(128 * v, 128 * v + 128)
                    a_s[c, x, rows, lanes] = t
                    new = vel_ref[c, x, rows, lanes] + step_size * t
                    v_s[c, x, rows, lanes] = new
                    d_s[c, x, rows, lanes] = d_ref[c, x, rows, lanes] + step_size * new
        for copy in copies(c):
            copy.start()
        return 0

    lax.fori_loop(0, 3, body, 0)
    for c in range(3):
        for copy in copies(c):
            copy.wait()


def call(kernel, outs, scratch, name, flops=0, limit=VMEM_LIMIT, **more):
    def run(*args):
        moved = sum(a.size * 4 for a in args) + sum(4 * math.prod(s) for s in outs)
        return pl.pallas_call(
            kernel,
            out_shape=[jax.ShapeDtypeStruct(s, F32) for s in outs],
            scratch_shapes=[pltpu.VMEM(s, F32) if isinstance(s, tuple) else s for s in scratch],
            compiler_params=pltpu.CompilerParams(vmem_limit_bytes=limit),
            cost_estimate=pl.CostEstimate(flops=flops, bytes_accessed=moved, transcendentals=0),
            name=name,
            **more,
        )(*args)

    return run


T = (8, 128)
FACE = (232, 128)
PARTS = [FACE, FACE, (2, 27) + T, (2, 16, 128)]


def solution(mesh):
    gx, gy = mesh.shape["gx"], mesh.shape["gy"]

    def moved(value, by_x, by_y):
        pairs = [
            (i * gy + j, ((i + by_x) % gx) * gy + (j + by_y) % gy)
            for i in range(gx)
            for j in range(gy)
        ]
        return lax.ppermute(value, ("gx", "gy"), pairs)

    def complete(parts, *done):
        minus, plus_face, inner, rim = parts
        low = moved(plus_face, 1, 0)
        high = moved(minus, -1, 0)
        specs = [pl.BlockSpec(memory_space=pltpu.VMEM)] * 6
        specs += [pl.BlockSpec(memory_space=pltpu.VMEM)] * len(done)
        down, up = call(rows_kernel, [(40, 128), (40, 128)], [], "rows", in_specs=specs)(
            minus, plus_face, inner, rim, low, high, *done
        )
        from_up = moved(down, 0, -1)
        from_down = moved(up, 0, 1)
        return (minus, plus_face, inner, rim, low, high, from_down, from_up)

    def on_device(displacement, velocity, energy, mass_weight, pinned):
        weight = mass_weight.reshape((216,) + T)
        dofs = energy.reshape((27,) + T)
        flags = pinned.dtype
        face, row, corner = call(
            pack_kernel,
            [(9, 24, 384), (27, 384), (9, 384)],
            [
                (2, 3, 24, 384), pltpu.VMEM((3, 24, 384), flags), (2, 3, 3, 8, 384),
                pltpu.VMEM((3, 3, 8, 384), flags), pltpu.SemaphoreType.DMA((6,)),
            ],
            "pack",
            limit=62 * 1024 * 1024,
            in_specs=[pl.BlockSpec(memory_space=pltpu.HBM)] * 3,
        )(displacement, velocity, pinned)
        hx = moved(face, -1, 0)
        hy = moved(row, 0, -1)
        hc = moved(corner, -1, -1)
        nodes, mask, heat, lump = call(
            prep_kernel,
            [(6, 27) + T, (3, 27) + T, (216,) + T, (27,) + T],
            [(9, 3, 24, 128), (6, 9) + T, (6, 3) + T],
            "prep",
            flops=4000 * 1024,
        )(displacement, velocity, pinned, dofs, weight)
        out = call(
            force_kernel,
            PARTS + [(27,) + T, (4, 16, 128), (216,) + T],
            [
                (9, 9) + T, (3, 40, 128), (6, 48) + T, (6, 6, 16) + T, (6, 6, 16) + T,
                (6, 3, 24) + T, (6, 3, 12) + T, (6, 3, 16) + T,
                (6, 3, 16) + T, (3, 48) + T, (3, 3, 24, 128),
            ],
            "force",
            flops=90000 * 1024,
        )(nodes, hx, hy, hc, heat, weight)
        parts, (face_mask, rim_mask, power) = out[:4], out[4:]
        energy_new, token = call(
            energy_kernel, [(27,) + T, T], [(27,) + T, (6, 9) + T, (6, 3) + T], "energy",
            flops=2000 * 1024,
        )(power, lump, dofs)
        masks = (mask, face_mask, rim_mask)
        scratch = [
            (3, 48) + T, (6, 3, 16) + T, (3, 4, 6) + T, (6, 3, 16) + T, (3, 48) + T,
        ]
        apply = call(apply_kernel, [(3, 27) + T] + PARTS, scratch, "apply", flops=13000 * 1024)
        out = apply(*complete(parts, token), *masks, weight)
        r, parts = out[0], out[1:]
        out = apply(*complete(parts), *masks, weight)
        v, parts = out[0], out[1:]
        w, sums = call(
            moments_kernel, [(3, 27) + T, (gx * gy, 128)], scratch[:2], "moments", flops=8000 * 1024
        )(*complete(parts), *masks, weight, r, v)
        sums = sums.reshape(gx * gy, -1, 128)
        sums = lax.all_to_all(sums, ("gx", "gy"), 0, 0).reshape(-1, 128)
        shape = displacement.shape
        acceleration, velocity_new, displacement_new = call(
            final_kernel,
            [shape] * 3,
            [(3, 3, 24, 128), shape, shape, shape, pltpu.SemaphoreType.DMA((3, 3))],
            "final",
            flops=1000 * 1024,
            out_specs=[pl.BlockSpec(memory_space=pltpu.HBM)] * 3,
        )(sums, r, v, w, displacement, velocity)
        return acceleration, velocity_new, displacement_new, energy_new.reshape(energy.shape)

    spec = P(None, "gx", "gy", None)
    return jax.shard_map(
        on_device, mesh=mesh, in_specs=(spec,) * 5, out_specs=(spec,) * 4, check_vma=False
    )
```

```python
import math

import jax
import jax.numpy as jnp
import numpy as np
from jax import lax
from jax.experimental import pallas as pl
from jax.experimental.pallas import tpu as pltpu
from jax.sharding import PartitionSpec as P

step_size = 0.05
viscosity = 0.3
gamma_less = 0.4
F32 = jnp.float32
VMEM_LIMIT = 32 * 1024 * 1024


def tables():
    root_five = 1.0 / math.sqrt(5.0)
    lobatto = np.array([0.0, 0.5 - 0.5 * root_five, 0.5 + 0.5 * root_five, 1.0])
    legendre = np.array(
        [
            -0.932469514203152,
            -0.6612093864662645,
            -0.2386191860831909,
            0.2386191860831909,
            0.6612093864662645,
            0.932469514203152,
        ]
    )
    t = 0.5 + 0.5 * legendre
    values = np.ones((6, 4))
    slopes = np.zeros((6, 4))
    for a in range(4):
        for b in range(4):
            if b != a:
                values[:, a] *= (t - lobatto[b]) / (lobatto[a] - lobatto[b])
        for c in range(4):
            if c != a:
                term = np.ones(6) / (lobatto[a] - lobatto[c])
                for b in range(4):
                    if b != a and b != c:
                        term = term * (t - lobatto[b]) / (lobatto[a] - lobatto[b])
                slopes[:, a] += term
    thermo = np.stack([(1.0 - t) * (1.0 - t), 2.0 * t * (1.0 - t), t * t], axis=1)
    return values, slopes, thermo


VALUES, SLOPES, THERMO = tables()
LOBATTO = np.array([0.0, 0.5 - 0.5 / math.sqrt(5.0), 0.5 + 0.5 / math.sqrt(5.0), 1.0]) - 0.5
ABSCISSA = VALUES @ LOBATTO
INVERSE = float(0.5 / LOBATTO[1])
RATIO = float(LOBATTO[0] / LOBATTO[1])
BK = [float((VALUES[q, 0] + VALUES[q, 3]) / 2) for q in range(3)]
BM = [float((VALUES[q, 0] - VALUES[q, 3]) / 2) for q in range(3)]
BL = [float(ABSCISSA[q]) for q in range(3)]
DK = [float((SLOPES[q, 0] + SLOPES[q, 3]) / 2) for q in range(3)]
DM = [float((SLOPES[q, 0] - SLOPES[q, 3]) / 2) for q in range(3)]
TE = [float((THERMO[q, 0] + THERMO[q, 2]) / 2) for q in range(3)]
TO = [float((THERMO[q, 0] - THERMO[q, 2]) / 2) for q in range(3)]
TM = [float(THERMO[q, 1]) for q in range(3)]


def butterfly(u):
    e0, e1, o0, o1 = u[0] + u[3], u[1] + u[2], u[0] - u[3], u[1] - u[2]
    return [0.5 * e1, e0 - e1, INVERSE * o1, o0 - RATIO * o1]


def unbutterfly(r):
    e0, e1, o0, o1 = r[1], 0.5 * r[0] - r[1], r[3], INVERSE * r[2] - RATIO * r[3]
    return [e0 + o0, e1 + o1, e1 - o1, e0 - o0]


def interp_pair(h, q):
    even = h[0] + BK[q] * h[1]
    odd = BL[q] * h[2] + BM[q] * h[3]
    return even + odd, even - odd


def slope_pair(h, q):
    even = h[2] + DM[q] * h[3]
    odd = DK[q] * h[1]
    return even + odd, even - odd


def along(pair_fn, h):
    out = [None] * 6
    for q in range(3):
        out[q], out[5 - q] = pair_fn(h, q)
    return out


def plus(total, term):
    return term if total is None else total + term


def interp_back_pair(h, q, even, odd):
    h[0] = plus(h[0], even)
    h[1] = plus(h[1], BK[q] * even)
    h[2] = plus(h[2], BL[q] * odd)
    h[3] = plus(h[3], BM[q] * odd)


def slope_back_pair(h, q, even, odd):
    h[1] = plus(h[1], DK[q] * odd)
    h[2] = plus(h[2], even)
    h[3] = plus(h[3], DM[q] * even)


def interp_back(f, h=None):
    h = [None] * 4 if h is None else list(h)
    for q in range(3):
        interp_back_pair(h, q, f[q] + f[5 - q], f[q] - f[5 - q])
    return h


def slope_back(f, h=None):
    h = [None] * 4 if h is None else list(h)
    for q in range(3):
        slope_back_pair(h, q, f[q] + f[5 - q], f[q] - f[5 - q])
    return h


def thermo_along(u):
    even, odd, mid = u[0] + u[2], u[0] - u[2], u[1]
    out = [None] * 6
    for q in range(3):
        both, one = TE[q] * even + TM[q] * mid, TO[q] * odd
        out[q], out[5 - q] = both + one, both - one
    return out


def thermo_back(f):
    even = mid = odd = None
    for q in range(3):
        both, one = f[q] + f[5 - q], f[q] - f[5 - q]
        even = plus(even, TE[q] * both)
        mid = plus(mid, TM[q] * both)
        odd = plus(odd, TO[q] * one)
    return [even + odd, mid, even - odd]


def iotas(rows=8):
    shape = (rows, 128)
    return lax.broadcasted_iota(jnp.int32, shape, 0), lax.broadcasted_iota(jnp.int32, shape, 1)


def gather_lanes(x, index):
    return jnp.take_along_axis(x, index, axis=1, mode="promise_in_bounds")


def split_lanes(parts, rows=8):
    lane = iotas(rows)[1]
    out = []
    for g in range(3):
        place = 3 * lane + g
        index = place & 127
        moved = [gather_lanes(p, index) for p in parts]
        out.append(
            jnp.where(place < 128, moved[0], jnp.where(place < 256, moved[1], moved[2]))
        )
    return out


def join_lanes(parts):
    lane = iotas()[1]
    out = []
    for v in range(3):
        place = lane + 128 * v
        index = place // 3
        g = place - 3 * index
        moved = [gather_lanes(p, index) for p in parts]
        out.append(jnp.where(g == 0, moved[0], jnp.where(g == 1, moved[1], moved[2])))
    return out


def next_lane(x):
    return pltpu.roll(x, 127, 1)


def previous_lane(x):
    return pltpu.roll(x, 1, 1)


def pack_kernel(d_ref, v_ref, f_ref, x_ref, y_ref, c_ref, face, face_f, low, low_f, sems):
    copies = []
    for n, ref in enumerate((d_ref, v_ref, f_ref)):
        to_face, to_low = (face.at[n], low.at[n]) if n < 2 else (face_f, low_f)
        copies.append(pltpu.make_async_copy(ref.at[:, 0], to_face, sems.at[2 * n]))
        copies.append(pltpu.make_async_copy(ref.at[:, :, 0:8], to_low, sems.at[2 * n + 1]))
    for copy in copies:
        copy.start()
    for copy in copies:
        copy.wait()
    for n in range(3):
        for c in range(3):
            k = 3 * n + c
            layer = (face[n, c] if n < 2 else face_f[c]).astype(F32)
            x_ref[k] = layer
            c_ref[k : k + 1, :] = layer[0:1]
            for x in range(3):
                r = 9 * x + k
                row = low[n, c, x, 0:1, :] if n < 2 else low_f[c, x, 0:1, :]
                y_ref[r : r + 1, :] = row.astype(F32)


def element_rows(load, place):
    for t in range(3):
        tiles = split_lanes([load(8 * t, 128 * v) for v in range(3)])
        for g in range(3):
            place[g, 8 * t : 8 * t + 8, :] = tiles[g]
    return [place[g, pl.ds(b, 8, stride=3), :] for b in range(3) for g in range(3)]


def prep_kernel(d_ref, v_ref, f_ref, e_ref, w_ref, u_ref, m_ref, eq_ref, lump_ref, place, ez_s, ey_s):
    def body(c, _):
        for x in range(3):
            for k, ref in enumerate((d_ref, v_ref, f_ref)):
                tiles = element_rows(
                    lambda s, l: ref[c, x, s : s + 8, l : l + 128].astype(F32), place.at[3 * x + k]
                )
                for n in range(9):
                    if k < 2:
                        u_ref[3 * k + c, x * 9 + n] = tiles[n]
                    else:
                        m_ref[x, c * 9 + n] = 1.0 - tiles[n]
        return 0

    lax.fori_loop(0, 3, body, 0)
    for n in range(9):
        for q, t in enumerate(thermo_along([gamma_less * e_ref[3 * n + g] for g in range(3)])):
            ez_s[q, n] = t

    def plane(z, _):
        for x in range(3):
            for q, t in enumerate(thermo_along([ez_s[z, 3 * x + y] for y in range(3)])):
                ey_s[q, x] = t
        for y in range(6):
            for q, t in enumerate(thermo_along([ey_s[y, x] for x in range(3)])):
                eq_ref[q * 36 + y * 6 + z] = t
        return 0

    lax.fori_loop(0, 6, plane, 0)
    project(w_ref, ez_s, ey_s, lump_ref)


def project(at_ref, z_s, x_s, out_ref):
    def plane(z, _):
        for y in range(6):
            for x, t in enumerate(thermo_back([at_ref[p * 36 + y * 6 + z] for p in range(6)])):
                x_s[y, x] = t
        for x in range(3):
            for y, t in enumerate(thermo_back([x_s[q, x] for q in range(6)])):
                z_s[z, 3 * x + y] = t
        return 0

    lax.fori_loop(0, 6, plane, 0)
    for n in range(9):
        for g, t in enumerate(thermo_back([z_s[q, n] for q in range(6)])):
            out_ref[3 * n + g] = t


def energy_kernel(power_ref, lump_ref, e_ref, out_ref, token_ref, sum_s, z_s, x_s):
    project(power_ref, z_s, x_s, sum_s)

    def body(n, _):
        out_ref[n] = e_ref[n] + step_size * (sum_s[n] / lump_ref[n])
        return 0

    lax.fori_loop(0, 27, body, 0)
    token_ref[...] = sum_s[0]


def point(jac, vel, energy, mass):
    cof = [
        [
            jac[(c + 1) % 3][(d + 1) % 3] * jac[(c + 2) % 3][(d + 2) % 3]
            - jac[(c + 1) % 3][(d + 2) % 3] * jac[(c + 2) % 3][(d + 1) % 3]
            for d in range(3)
        ]
        for c in range(3)
    ]
    det = jac[0][0] * cof[0][0] + jac[0][1] * cof[0][1] + jac[0][2] * cof[0][2]
    inv = pl.reciprocal(det, approx=True)
    inv = inv * (2.0 - det * inv)
    scale = mass * inv
    shear = (viscosity * scale) * inv
    twice = shear + shear
    press = scale * energy
    rate = [
        [vel[c][0] * cof[e][0] + vel[c][1] * cof[e][1] + vel[c][2] * cof[e][2] for e in range(3)]
        for c in range(3)
    ]
    stress = [[None] * 3 for _ in range(3)]
    power = None
    for c in range(3):
        stress[c][c] = twice * rate[c][c] - press
        power = plus(power, stress[c][c] * rate[c][c])
        for d in range(c + 1, 3):
            both = rate[c][d] + rate[d][c]
            stress[c][d] = stress[d][c] = shear * both
            power = power + stress[c][d] * both
    flux = [
        [
            stress[c][0] * cof[0][f] + stress[c][1] * cof[1][f] + stress[c][2] * cof[2][f]
            for f in range(3)
        ]
        for c in range(3)
    ]
    return flux, power


def spread_y(first, row):
    sub = iotas()[0]
    return jnp.where(sub == 7, row, pltpu.roll(first, 7, 0))


def store_parts(nodes_of, minus_ref, plus_ref, inner_ref, rim_ref):
    sub = iotas()[0]

    def body(c, _):
        for g in range(3):
            nodes = nodes_of(c, g)
            for x in range(4):
                over = nodes[x][3]
                nodes[x][0] = nodes[x][0] + jnp.where(sub == 0, 0.0, pltpu.roll(over, 1, 0))
                r = c * 3 + g
                if x in (0, 3):
                    ref = minus_ref if x == 0 else plus_ref
                    ref[pl.ds(216 + r, 1), :] = over[7:8]
                    for b in range(3):
                        ref[pl.ds(pl.multiple_of((c * 9 + b * 3 + g) * 8, 8), 8), :] = nodes[x][b]
                else:
                    rim_ref[x - 1, pl.ds(r, 1), :] = over[7:8]
                    for b in range(3):
                        inner_ref[x - 1, c * 9 + b * 3 + g] = nodes[x][b]
        return 0

    lax.fori_loop(0, 3, body, 0)


def rim_rows(hy_ref, hc_ref, hy_s):
    rows = [
        jnp.concatenate(
            [hy_ref[:, 128 * v : 128 * v + 128], hc_ref[:, 128 * v : 128 * v + 128]], axis=0
        )
        for v in range(3)
    ]
    rows = [jnp.concatenate([r, jnp.zeros((4, 128), F32)], axis=0) for r in rows]
    for t in range(5):
        for g, tile in enumerate(split_lanes([r[8 * t : 8 * t + 8] for r in rows])):
            hy_s[g, 8 * t : 8 * t + 8, :] = tile


def mask_kernel(hx_ref, hy_ref, hc_ref, face_mask_ref, rim_mask_ref, hy_s, place):
    rim_rows(hy_ref, hc_ref, hy_s)
    for x in range(4):
        for c in range(3):
            for g in range(3):
                r = 9 * x + 6 + c
                rim_mask_ref[x, c * 3 + g : c * 3 + g + 1, :] = 1.0 - hy_s[g, r : r + 1, :]
    for c in range(3):
        tiles = element_rows(lambda s, l: hx_ref[6 + c, s : s + 8, l : l + 128], place.at[c])
        for n in range(9):
            face_mask_ref[c * 9 + n] = 1.0 - tiles[n]


def force_kernel(
    u_ref, hx_ref, hy_ref, hc_ref, eq_ref, w_ref,
    minus_ref, plus_ref, inner_ref, rim_ref, power_ref,
    hx_s, hy_s, q_s, zv_s, zs_s, w_s, xt_s, ya_s, yb_s, zn_s, place,
):
    rim_rows(hy_ref, hc_ref, hy_s)
    for k in range(6):
        tiles = element_rows(lambda s, l: hx_ref[k, s : s + 8, l : l + 128], place.at[k])
        for n in range(9):
            hx_s[k, n] = tiles[n]
    def gather_nodes(c, _):
        for g in range(3):
            cols = []
            for x in range(4):
                if x < 3:
                    u = [u_ref[c, x * 9 + b * 3 + g] for b in range(3)]
                else:
                    u = [hx_s[c, b * 3 + g] for b in range(3)]
                row = hy_s[g, pl.ds(9 * x + c, 1), :]
                u.append(spread_y(u[0], row))
                cols.append(butterfly(u))
            for y in range(4):
                for x, t in enumerate(butterfly([cols[x][y] for x in range(4)])):
                    q_s[c, (x * 4 + y) * 3 + g] = t
        return 0

    lax.fori_loop(0, 6, gather_nodes, 0)
    for c, n in ((0, 2 * 4), (1, 2)):
        for g in range(3):
            q_s[c, n * 3 + g] = q_s[c, n * 3 + g] + 1.0

    def along_z(c, _):
        for n in range(16):
            u = [q_s[c, 3 * n + g] for g in range(3)]
            u.append(next_lane(u[0]))
            h = butterfly(u)
            if n == 0:
                h[2] = h[2] + jnp.where(c == 2, 1.0, 0.0)
            for q, t in enumerate(along(interp_pair, h)):
                zv_s[q, c, n] = t
            for q, t in enumerate(along(slope_pair, h)):
                zs_s[q, c, n] = t
        return 0

    lax.fori_loop(0, 6, along_z, 0)

    def plane(z, _):
        def along_y(c, _):
            for x in range(4):
                h = [zv_s[z, c, x * 4 + y] for y in range(4)]
                s = [zs_s[z, c, x * 4 + y] for y in range(4)]
                for q, t in enumerate(along(interp_pair, h)):
                    w_s[q, 0, c * 4 + x] = t
                for q, t in enumerate(along(slope_pair, h)):
                    w_s[q, 1, c * 4 + x] = t
                for q, t in enumerate(along(interp_pair, s)):
                    w_s[q, 2, c * 4 + x] = t
            return 0

        lax.fori_loop(0, 6, along_y, 0)

        def line(y, _):
            back = [[[None] * 4 for _ in range(3)] for _ in range(3)]
            for q in range(3):
                grads = [[[None] * 3 for _ in range(6)] for _ in range(2)]
                for c in range(6):
                    for d in range(3):
                        h = [w_s[y, d, c * 4 + x] for x in range(4)]
                        pair = slope_pair(h, q) if d == 0 else interp_pair(h, q)
                        for side in range(2):
                            grads[side][c][d] = pair[side]
                flux = []
                for side in range(2):
                    p = q if side == 0 else 5 - q
                    n = p * 36 + y * 6 + z
                    f, power_ref[n] = point(grads[side][:3], grads[side][3:], eq_ref[n], w_ref[n])
                    flux.append(f)
                for c in range(3):
                    for f in range(3):
                        even = flux[0][c][f] + flux[1][c][f]
                        odd = flux[0][c][f] - flux[1][c][f]
                        (slope_back_pair if f == 0 else interp_back_pair)(back[c][f], q, even, odd)
            for c in range(3):
                for f in range(3):
                    for x in range(4):
                        if back[c][f][x] is not None:
                            xt_s[y, f, c * 4 + x] = back[c][f][x]
            return 0

        lax.fori_loop(0, 6, line, 0)

        def back_y(c, _):
            for x in range(4):
                f = [
                    [xt_s[q, d, c * 4 + x] for q in range(6)] if d or x else None
                    for d in range(3)
                ]
                h = slope_back(f[1], interp_back(f[0]) if x else None)
                s = interp_back(f[2])
                for y in range(4):
                    ya_s[z, c, x * 4 + y] = jnp.zeros((8, 128), F32) if h[y] is None else h[y]
                    yb_s[z, c, x * 4 + y] = s[y]
            return 0

        lax.fori_loop(0, 3, back_y, 0)
        return 0

    lax.fori_loop(0, 6, plane, 0)

    def back_z(c, _):
        for n in range(16):
            h = interp_back([ya_s[q, c, n] for q in range(6)])
            h = slope_back([yb_s[q, c, n] for q in range(6)], h)
            u = unbutterfly(h)
            zn_s[c, n * 3] = -(u[0] + previous_lane(u[3]))
            zn_s[c, n * 3 + 1] = -u[1]
            zn_s[c, n * 3 + 2] = -u[2]
        return 0

    lax.fori_loop(0, 3, back_z, 0)
    store_parts(lambda c, g: nodes_from(zn_s, c, g), minus_ref, plus_ref, inner_ref, rim_ref)


def nodes_from(zn_s, c, g):
    cols = [unbutterfly([zn_s[c, (x * 4 + y) * 3 + g] for y in range(4)]) for x in range(4)]
    rows = [unbutterfly([cols[x][b] for x in range(4)]) for b in range(4)]
    return [[rows[b][x] for b in range(4)] for x in range(4)]


def rows_kernel(minus_ref, plus_ref, inner_ref, rim_ref, got_low_ref, got_high_ref, *rest):
    down_ref, up_ref = rest[-2:]
    for c in range(3):
        for g in range(3):
            r = c * 3 + g
            n = (c * 9 + g) * 8
            down_ref[r : r + 1, :] = minus_ref[n : n + 1, :] + got_low_ref[n : n + 1, :]
            down_ref[27 + r : 28 + r, :] = plus_ref[n : n + 1, :] + got_high_ref[n : n + 1, :]
            for x in range(2):
                down_ref[9 * (x + 1) + r : 9 * (x + 1) + r + 1, :] = inner_ref[x, c * 9 + g, 0:1, :]
    up_ref[0:9, :] = minus_ref[216:225, :] + got_low_ref[216:225, :]
    up_ref[27:36, :] = plus_ref[216:225, :] + got_high_ref[216:225, :]
    for x in range(2):
        up_ref[9 * (x + 1) : 9 * (x + 1) + 9, :] = rim_ref[x, 0:9, :]


def assemble(c, parts, mask_ref, face_mask_ref, rim_mask_ref, own_ref, q_s):
    minus_ref, plus_ref, inner_ref, rim_ref, low_ref, high_ref, from_down_ref, from_up_ref = parts
    sub = iotas()[0]
    for g in range(3):
        r = c * 3 + g
        cols = []
        for x in range(4):
            u = []
            for b in range(3):
                n = c * 9 + b * 3 + g
                tile = pl.ds(pl.multiple_of(n * 8, 8), 8)
                if x == 0:
                    t = minus_ref[tile, :] + low_ref[tile, :]
                elif x == 3:
                    t = plus_ref[tile, :] + high_ref[tile, :]
                else:
                    t = inner_ref[x - 1, n]
                if b == 0:
                    below = from_down_ref[pl.ds(9 * x + r, 1), :]
                    t = t + jnp.where(sub == 0, below, 0.0)
                t = t * (face_mask_ref[n] if x == 3 else mask_ref[x, n])
                u.append(t)
                if x < 3:
                    own_ref[x, n] = t
            edge = pl.ds(216 + r, 1)
            if x == 0:
                top = minus_ref[edge, :] + low_ref[edge, :]
            elif x == 3:
                top = plus_ref[edge, :] + high_ref[edge, :]
            else:
                top = rim_ref[x - 1, pl.ds(r, 1), :]
            top = (top + from_up_ref[pl.ds(9 * x + r, 1), :]) * rim_mask_ref[x, pl.ds(r, 1), :]
            u.append(spread_y(u[0], top))
            cols.append(butterfly(u))
        for y in range(4):
            for x, t in enumerate(butterfly([cols[x][y] for x in range(4)])):
                q_s[c, (x * 4 + y) * 3 + g] = t


def mass_along_z(c, q_s, zv_s):
    for n in range(16):
        u = [q_s[c, 3 * n + g] for g in range(3)]
        u.append(next_lane(u[0]))
        for q, t in enumerate(along(interp_pair, butterfly(u))):
            zv_s[q, c, n] = t


def apply_kernel(
    minus_ref, plus_ref, inner_ref, rim_ref, low_ref, high_ref, from_down_ref, from_up_ref,
    mask_ref, face_mask_ref, rim_mask_ref, w_ref,
    own_ref, out_minus_ref, out_plus_ref, out_inner_ref, out_rim_ref,
    q_s, zv_s, xt_s, ya_s, zn_s,
):
    parts = (
        minus_ref, plus_ref, inner_ref, rim_ref, low_ref, high_ref, from_down_ref, from_up_ref,
    )

    def first(c, _):
        assemble(c, parts, mask_ref, face_mask_ref, rim_mask_ref, own_ref, q_s)
        mass_along_z(c, q_s, zv_s)
        return 0

    lax.fori_loop(0, 3, first, 0)

    def plane(z, _):
        for c in range(3):
            lines = [along(interp_pair, [zv_s[z, c, x * 4 + y] for y in range(4)]) for x in range(4)]
            for y in range(6):
                h = [lines[x][y] for x in range(4)]
                at = along(interp_pair, h)
                at = [at[p] * w_ref[p * 36 + y * 6 + z] for p in range(6)]
                for x, t in enumerate(interp_back(at)):
                    xt_s[c, x, y] = t
            for x in range(4):
                for y, t in enumerate(interp_back([xt_s[c, x, q] for q in range(6)])):
                    ya_s[z, c, x * 4 + y] = t
        return 0

    lax.fori_loop(0, 6, plane, 0)

    def back_z(c, _):
        for n in range(16):
            u = unbutterfly(interp_back([ya_s[q, c, n] for q in range(6)]))
            zn_s[c, n * 3] = u[0] + previous_lane(u[3])
            zn_s[c, n * 3 + 1] = u[1]
            zn_s[c, n * 3 + 2] = u[2]
        return 0

    lax.fori_loop(0, 3, back_z, 0)
    store_parts(
        lambda c, g: nodes_from(zn_s, c, g), out_minus_ref, out_plus_ref, out_inner_ref, out_rim_ref
    )


def total(t):
    return jnp.sum(jnp.sum(t, axis=0, keepdims=True), axis=1, keepdims=True)


def moments_kernel(
    minus_ref, plus_ref, inner_ref, rim_ref, low_ref, high_ref, from_down_ref, from_up_ref,
    mask_ref, face_mask_ref, rim_mask_ref, w_ref, r_ref, v_ref,
    own_ref, sums_ref, q_s, zv_s,
):
    parts = (
        minus_ref, plus_ref, inner_ref, rim_ref, low_ref, high_ref, from_down_ref, from_up_ref,
    )

    def first(c, _):
        assemble(c, parts, mask_ref, face_mask_ref, rim_mask_ref, own_ref, q_s)
        mass_along_z(c, q_s, zv_s)
        return 0

    lax.fori_loop(0, 3, first, 0)
    zero = jnp.zeros((8, 128), F32)

    def dots(n, s):
        s = list(s)
        for x in range(3):
            r, v, w = r_ref[x, n], v_ref[x, n], own_ref[x, n]
            s = [
                s[0] + r * r, s[1] + r * v, s[2] + v * v, s[3] + v * w, s[4] + w * w,
            ]
        return tuple(s)

    sums = lax.fori_loop(0, 27, dots, (zero,) * 5)

    def plane(z, s):
        s = list(s)
        for c in range(3):
            lines = [along(interp_pair, [zv_s[z, c, x * 4 + y] for y in range(4)]) for x in range(4)]
            for y in range(6):
                at = along(interp_pair, [lines[x][y] for x in range(4)])
                for p in range(6):
                    s[c] = s[c] + (at[p] * at[p]) * w_ref[p * 36 + y * 6 + z]
        return tuple(s)

    last = lax.fori_loop(0, 6, plane, (zero,) * 3)
    sums = list(sums) + [last[0] + last[1] + last[2]]
    lane = iotas(1)[1]
    row = jnp.zeros((1, 128), F32)
    for k in range(6):
        row = row + jnp.where(lane == k, total(sums[k]), 0.0)
    sums_ref[...] = jnp.broadcast_to(row, sums_ref.shape)


def coefficients(mu):
    unit = mu[1] / mu[0]
    m = [None] * 6
    scale = 1.0 / mu[0]
    for k in range(6):
        m[k] = mu[k] * scale
        scale = scale / unit
    a0 = m[0] / m[1]
    rr1 = a0 * a0 * m[2] - 2.0 * a0 * m[1] + m[0]
    b0 = rr1 / m[0]
    d1 = [1.0 + b0, -a0]
    a1 = rr1 / (d1[0] * d1[0] * m[1] + 2.0 * d1[0] * d1[1] * m[2] + d1[1] * d1[1] * m[3])
    p1 = -(a0 + a1 * d1[0])
    p2 = -a1 * d1[1]
    rr2 = (
        m[0] + p1 * p1 * m[2] + p2 * p2 * m[4]
        + 2.0 * (p1 * m[1] + p2 * m[2] + p1 * p2 * m[3])
    )
    b1 = rr2 / rr1
    q = [1.0 + b1 * d1[0], p1 + b1 * d1[1], p2]
    a2 = rr2 / (
        q[0] * q[0] * m[1] + q[1] * q[1] * m[3] + q[2] * q[2] * m[5]
        + 2.0 * (q[0] * q[1] * m[2] + q[0] * q[2] * m[3] + q[1] * q[2] * m[4])
    )
    x = [a0 + a1 * d1[0] + a2 * q[0], a1 * d1[1] + a2 * q[1], a2 * q[2]]
    return [x[0] / unit, x[1] / (unit * unit), x[2] / (unit * unit * unit)]


def final_kernel(
    sums_ref, r_ref, v_ref, w_ref, d_ref, vel_ref, a_out, v_out, d_out, place, a_s, v_s, d_s, sems
):
    lane = iotas(1)[1]
    row = jnp.sum(sums_ref[...], axis=0, keepdims=True)
    mu = [
        jnp.broadcast_to(jnp.sum(jnp.where(lane == k, row, 0.0), axis=1, keepdims=True), (8, 128))
        for k in range(6)
    ]
    k0, k1, k2 = coefficients(mu)

    def copies(c):
        pairs = ((a_s, a_out), (v_s, v_out), (d_s, d_out))
        return [
            pltpu.make_async_copy(src.at[c], dst.at[c], sems.at[c, i])
            for i, (src, dst) in enumerate(pairs)
        ]

    def body(c, _):
        for x in range(3):
            for b in range(3):
                for g in range(3):
                    n = c * 9 + b * 3 + g
                    place[x, g, pl.ds(b, 8, stride=3), :] = (
                        k0 * r_ref[x, n] + k1 * v_ref[x, n] + k2 * w_ref[x, n]
                    )
            for s in range(3):
                rows = slice(8 * s, 8 * s + 8)
                for v, t in enumerate(join_lanes([place[x, g, rows, :] for g in range(3)])):
                    lanes = slice(128 * v, 128 * v + 128)
                    a_s[c, x, rows, lanes] = t
                    new = vel_ref[c, x, rows, lanes] + step_size * t
                    v_s[c, x, rows, lanes] = new
                    d_s[c, x, rows, lanes] = d_ref[c, x, rows, lanes] + step_size * new
        for copy in copies(c):
            copy.start()
        return 0

    lax.fori_loop(0, 3, body, 0)
    for c in range(3):
        for copy in copies(c):
            copy.wait()


def call(kernel, outs, scratch, name, flops=0, limit=VMEM_LIMIT, **more):
    def run(*args):
        moved = sum(a.size * 4 for a in args) + sum(4 * math.prod(s) for s in outs)
        return pl.pallas_call(
            kernel,
            out_shape=[jax.ShapeDtypeStruct(s, F32) for s in outs],
            scratch_shapes=[pltpu.VMEM(s, F32) if isinstance(s, tuple) else s for s in scratch],
            compiler_params=pltpu.CompilerParams(vmem_limit_bytes=limit),
            cost_estimate=pl.CostEstimate(flops=flops, bytes_accessed=moved, transcendentals=0),
            name=name,
            **more,
        )(*args)

    return run


T = (8, 128)
FACE = (232, 128)
PARTS = [FACE, FACE, (2, 27) + T, (2, 16, 128)]


def solution(mesh):
    gx, gy = mesh.shape["gx"], mesh.shape["gy"]

    def moved(value, by_x, by_y):
        pairs = [
            (i * gy + j, ((i + by_x) % gx) * gy + (j + by_y) % gy)
            for i in range(gx)
            for j in range(gy)
        ]
        return lax.ppermute(value, ("gx", "gy"), pairs)

    def complete(parts, *done):
        minus, plus_face, inner, rim = parts
        low = moved(plus_face, 1, 0)
        high = moved(minus, -1, 0)
        specs = [pl.BlockSpec(memory_space=pltpu.VMEM)] * 6
        specs += [pl.BlockSpec(memory_space=pltpu.VMEM)] * len(done)
        down, up = call(rows_kernel, [(40, 128), (40, 128)], [], "rows", in_specs=specs)(
            minus, plus_face, inner, rim, low, high, *done
        )
        from_up = moved(down, 0, -1)
        from_down = moved(up, 0, 1)
        return (minus, plus_face, inner, rim, low, high, from_down, from_up)

    def on_device(displacement, velocity, energy, mass_weight, pinned):
        weight = mass_weight.reshape((216,) + T)
        dofs = energy.reshape((27,) + T)
        flags = pinned.dtype
        face, row, corner = call(
            pack_kernel,
            [(9, 24, 384), (27, 384), (9, 384)],
            [
                (2, 3, 24, 384), pltpu.VMEM((3, 24, 384), flags), (2, 3, 3, 8, 384),
                pltpu.VMEM((3, 3, 8, 384), flags), pltpu.SemaphoreType.DMA((6,)),
            ],
            "pack",
            limit=62 * 1024 * 1024,
            in_specs=[pl.BlockSpec(memory_space=pltpu.HBM)] * 3,
        )(displacement, velocity, pinned)
        hx = moved(face, -1, 0)
        hy = moved(row, 0, -1)
        hc = moved(corner, -1, -1)
        nodes, mask, heat, lump = call(
            prep_kernel,
            [(6, 27) + T, (3, 27) + T, (216,) + T, (27,) + T],
            [(9, 3, 24, 128), (6, 9) + T, (6, 3) + T],
            "prep",
            flops=4000 * 1024,
        )(displacement, velocity, pinned, dofs, weight)
        out = call(
            force_kernel,
            PARTS + [(216,) + T],
            [
                (6, 9) + T, (3, 40, 128), (6, 48) + T, (6, 6, 16) + T, (6, 6, 16) + T,
                (6, 3, 24) + T, (6, 3, 12) + T, (6, 3, 16) + T,
                (6, 3, 16) + T, (3, 48) + T, (6, 3, 24, 128),
            ],
            "force",
            flops=90000 * 1024,
        )(nodes, hx, hy, hc, heat, weight)
        parts, power = out[:4], out[4]
        face_mask, rim_mask = call(
            mask_kernel, [(27,) + T, (4, 16, 128)], [(3, 40, 128), (3, 3, 24, 128)], "masks",
            flops=100 * 1024,
        )(hx, hy, hc)
        energy_new, token = call(
            energy_kernel, [(27,) + T, T], [(27,) + T, (6, 9) + T, (6, 3) + T], "energy",
            flops=2000 * 1024,
        )(power, lump, dofs)
        masks = (mask, face_mask, rim_mask)
        scratch = [
            (3, 48) + T, (6, 3, 16) + T, (3, 4, 6) + T, (6, 3, 16) + T, (3, 48) + T,
        ]
        apply = call(apply_kernel, [(3, 27) + T] + PARTS, scratch, "apply", flops=13000 * 1024)
        out = apply(*complete(parts, token), *masks, weight)
        r, parts = out[0], out[1:]
        out = apply(*complete(parts), *masks, weight)
        v, parts = out[0], out[1:]
        w, sums = call(
            moments_kernel, [(3, 27) + T, (gx * gy, 128)], scratch[:2], "moments", flops=8000 * 1024
        )(*complete(parts), *masks, weight, r, v)
        sums = sums.reshape(gx * gy, -1, 128)
        sums = lax.all_to_all(sums, ("gx", "gy"), 0, 0).reshape(-1, 128)
        shape = displacement.shape
        acceleration, velocity_new, displacement_new = call(
            final_kernel,
            [shape] * 3,
            [(3, 3, 24, 128), shape, shape, shape, pltpu.SemaphoreType.DMA((3, 3))],
            "final",
            flops=1000 * 1024,
            out_specs=[pl.BlockSpec(memory_space=pltpu.HBM)] * 3,
        )(sums, r, v, w, displacement, velocity)
        return acceleration, velocity_new, displacement_new, energy_new.reshape(energy.shape)

    spec = P(None, "gx", "gy", None)
    return jax.shard_map(
        on_device, mesh=mesh, in_specs=(spec,) * 5, out_specs=(spec,) * 4, check_vma=False
    )
```

```python
import math

import jax
import jax.numpy as jnp
import numpy as np
from jax import lax
from jax.experimental import pallas as pl
from jax.experimental.pallas import tpu as pltpu
from jax.sharding import PartitionSpec as P

step_size = 0.05
viscosity = 0.3
gamma_less = 0.4
F32 = jnp.float32
VMEM_LIMIT = 32 * 1024 * 1024


def tables():
    root_five = 1.0 / math.sqrt(5.0)
    lobatto = np.array([0.0, 0.5 - 0.5 * root_five, 0.5 + 0.5 * root_five, 1.0])
    legendre = np.array(
        [
            -0.932469514203152,
            -0.6612093864662645,
            -0.2386191860831909,
            0.2386191860831909,
            0.6612093864662645,
            0.932469514203152,
        ]
    )
    t = 0.5 + 0.5 * legendre
    values = np.ones((6, 4))
    slopes = np.zeros((6, 4))
    for a in range(4):
        for b in range(4):
            if b != a:
                values[:, a] *= (t - lobatto[b]) / (lobatto[a] - lobatto[b])
        for c in range(4):
            if c != a:
                term = np.ones(6) / (lobatto[a] - lobatto[c])
                for b in range(4):
                    if b != a and b != c:
                        term = term * (t - lobatto[b]) / (lobatto[a] - lobatto[b])
                slopes[:, a] += term
    thermo = np.stack([(1.0 - t) * (1.0 - t), 2.0 * t * (1.0 - t), t * t], axis=1)
    return values, slopes, thermo


VALUES, SLOPES, THERMO = tables()
LOBATTO = np.array([0.0, 0.5 - 0.5 / math.sqrt(5.0), 0.5 + 0.5 / math.sqrt(5.0), 1.0]) - 0.5
ABSCISSA = VALUES @ LOBATTO
INVERSE = float(0.5 / LOBATTO[1])
RATIO = float(LOBATTO[0] / LOBATTO[1])
BK = [float((VALUES[q, 0] + VALUES[q, 3]) / 2) for q in range(3)]
BM = [float((VALUES[q, 0] - VALUES[q, 3]) / 2) for q in range(3)]
BL = [float(ABSCISSA[q]) for q in range(3)]
DK = [float((SLOPES[q, 0] + SLOPES[q, 3]) / 2) for q in range(3)]
DM = [float((SLOPES[q, 0] - SLOPES[q, 3]) / 2) for q in range(3)]
TE = [float((THERMO[q, 0] + THERMO[q, 2]) / 2) for q in range(3)]
TO = [float((THERMO[q, 0] - THERMO[q, 2]) / 2) for q in range(3)]
TM = [float(THERMO[q, 1]) for q in range(3)]


def butterfly(u):
    e0, e1, o0, o1 = u[0] + u[3], u[1] + u[2], u[0] - u[3], u[1] - u[2]
    return [0.5 * e1, e0 - e1, INVERSE * o1, o0 - RATIO * o1]


def unbutterfly(r):
    e0, e1, o0, o1 = r[1], 0.5 * r[0] - r[1], r[3], INVERSE * r[2] - RATIO * r[3]
    return [e0 + o0, e1 + o1, e1 - o1, e0 - o0]


def interp_pair(h, q):
    even = h[0] + BK[q] * h[1]
    odd = BL[q] * h[2] + BM[q] * h[3]
    return even + odd, even - odd


def slope_pair(h, q):
    even = h[2] + DM[q] * h[3]
    odd = DK[q] * h[1]
    return even + odd, even - odd


def along(pair_fn, h):
    out = [None] * 6
    for q in range(3):
        out[q], out[5 - q] = pair_fn(h, q)
    return out


def plus(total, term):
    return term if total is None else total + term


def interp_back_pair(h, q, even, odd):
    h[0] = plus(h[0], even)
    h[1] = plus(h[1], BK[q] * even)
    h[2] = plus(h[2], BL[q] * odd)
    h[3] = plus(h[3], BM[q] * odd)


def slope_back_pair(h, q, even, odd):
    h[1] = plus(h[1], DK[q] * odd)
    h[2] = plus(h[2], even)
    h[3] = plus(h[3], DM[q] * even)


def interp_back(f, h=None):
    h = [None] * 4 if h is None else list(h)
    for q in range(3):
        interp_back_pair(h, q, f[q] + f[5 - q], f[q] - f[5 - q])
    return h


def slope_back(f, h=None):
    h = [None] * 4 if h is None else list(h)
    for q in range(3):
        slope_back_pair(h, q, f[q] + f[5 - q], f[q] - f[5 - q])
    return h


def thermo_along(u):
    even, odd, mid = u[0] + u[2], u[0] - u[2], u[1]
    out = [None] * 6
    for q in range(3):
        both, one = TE[q] * even + TM[q] * mid, TO[q] * odd
        out[q], out[5 - q] = both + one, both - one
    return out


def thermo_back(f):
    even = mid = odd = None
    for q in range(3):
        both, one = f[q] + f[5 - q], f[q] - f[5 - q]
        even = plus(even, TE[q] * both)
        mid = plus(mid, TM[q] * both)
        odd = plus(odd, TO[q] * one)
    return [even + odd, mid, even - odd]


def iotas(rows=8):
    shape = (rows, 128)
    return lax.broadcasted_iota(jnp.int32, shape, 0), lax.broadcasted_iota(jnp.int32, shape, 1)


def gather_lanes(x, index):
    return jnp.take_along_axis(x, index, axis=1, mode="promise_in_bounds")


def split_lanes(parts, rows=8):
    lane = iotas(rows)[1]
    out = []
    for g in range(3):
        place = 3 * lane + g
        index = place & 127
        moved = [gather_lanes(p, index) for p in parts]
        out.append(
            jnp.where(place < 128, moved[0], jnp.where(place < 256, moved[1], moved[2]))
        )
    return out


def join_lanes(parts):
    lane = iotas()[1]
    out = []
    for v in range(3):
        place = lane + 128 * v
        index = place // 3
        g = place - 3 * index
        moved = [gather_lanes(p, index) for p in parts]
        out.append(jnp.where(g == 0, moved[0], jnp.where(g == 1, moved[1], moved[2])))
    return out


def next_lane(x):
    return pltpu.roll(x, 127, 1)


def previous_lane(x):
    return pltpu.roll(x, 1, 1)


def pack_kernel(d_ref, v_ref, f_ref, x_ref, y_ref, c_ref, face, face_f, low, low_f, sems):
    copies = []
    for n, ref in enumerate((d_ref, v_ref, f_ref)):
        to_face, to_low = (face.at[n], low.at[n]) if n < 2 else (face_f, low_f)
        copies.append(pltpu.make_async_copy(ref.at[:, 0], to_face, sems.at[2 * n]))
        copies.append(pltpu.make_async_copy(ref.at[:, :, 0:8], to_low, sems.at[2 * n + 1]))
    for copy in copies:
        copy.start()
    for copy in copies:
        copy.wait()
    for n in range(3):
        for c in range(3):
            k = 3 * n + c
            layer = (face[n, c] if n < 2 else face_f[c]).astype(F32)
            x_ref[k] = layer
            c_ref[k : k + 1, :] = layer[0:1]
            for x in range(3):
                r = 9 * x + k
                row = low[n, c, x, 0:1, :] if n < 2 else low_f[c, x, 0:1, :]
                y_ref[r : r + 1, :] = row.astype(F32)


def element_rows(load, place):
    for t in range(3):
        tiles = split_lanes([load(8 * t, 128 * v) for v in range(3)])
        for g in range(3):
            place[g, 8 * t : 8 * t + 8, :] = tiles[g]
    return [place[g, pl.ds(b, 8, stride=3), :] for b in range(3) for g in range(3)]


def prep_kernel(d_ref, v_ref, f_ref, e_ref, w_ref, u_ref, m_ref, eq_ref, lump_ref, place, ez_s, ey_s):
    def body(c, _):
        for x in range(3):
            for k, ref in enumerate((d_ref, v_ref, f_ref)):
                tiles = element_rows(
                    lambda s, l: ref[c, x, s : s + 8, l : l + 128].astype(F32), place.at[3 * x + k]
                )
                for n in range(9):
                    if k < 2:
                        u_ref[3 * k + c, x * 9 + n] = tiles[n]
                    else:
                        m_ref[x, c * 9 + n] = 1.0 - tiles[n]
        return 0

    lax.fori_loop(0, 3, body, 0)
    for n in range(9):
        for q, t in enumerate(thermo_along([gamma_less * e_ref[3 * n + g] for g in range(3)])):
            ez_s[q, n] = t

    def plane(z, _):
        for x in range(3):
            for q, t in enumerate(thermo_along([ez_s[z, 3 * x + y] for y in range(3)])):
                ey_s[q, x] = t
        for y in range(6):
            for q, t in enumerate(thermo_along([ey_s[y, x] for x in range(3)])):
                eq_ref[q * 36 + y * 6 + z] = t
        return 0

    lax.fori_loop(0, 6, plane, 0)
    project(w_ref, ez_s, ey_s, lump_ref)


def project(at_ref, z_s, x_s, out_ref):
    def plane(z, _):
        for y in range(6):
            for x, t in enumerate(thermo_back([at_ref[p * 36 + y * 6 + z] for p in range(6)])):
                x_s[y, x] = t
        for x in range(3):
            for y, t in enumerate(thermo_back([x_s[q, x] for q in range(6)])):
                z_s[z, 3 * x + y] = t
        return 0

    lax.fori_loop(0, 6, plane, 0)
    for n in range(9):
        for g, t in enumerate(thermo_back([z_s[q, n] for q in range(6)])):
            out_ref[3 * n + g] = t


def energy_kernel(
    power_ref, lump_ref, e_ref, hx_ref, hy_ref, hc_ref,
    out_ref, token_ref, face_mask_ref, rim_mask_ref, sum_s, z_s, x_s, hy_s, place,
):
    masks(hx_ref, hy_ref, hc_ref, face_mask_ref, rim_mask_ref, hy_s, place)
    project(power_ref, z_s, x_s, sum_s)

    def body(n, _):
        out_ref[n] = e_ref[n] + step_size * (sum_s[n] / lump_ref[n])
        return 0

    lax.fori_loop(0, 27, body, 0)
    token_ref[...] = sum_s[0]


def point(jac, vel, energy, mass):
    cof = [
        [
            jac[(c + 1) % 3][(d + 1) % 3] * jac[(c + 2) % 3][(d + 2) % 3]
            - jac[(c + 1) % 3][(d + 2) % 3] * jac[(c + 2) % 3][(d + 1) % 3]
            for d in range(3)
        ]
        for c in range(3)
    ]
    det = jac[0][0] * cof[0][0] + jac[0][1] * cof[0][1] + jac[0][2] * cof[0][2]
    inv = pl.reciprocal(det, approx=True)
    inv = inv * (2.0 - det * inv)
    scale = mass * inv
    shear = (viscosity * scale) * inv
    twice = shear + shear
    press = scale * energy
    rate = [
        [vel[c][0] * cof[e][0] + vel[c][1] * cof[e][1] + vel[c][2] * cof[e][2] for e in range(3)]
        for c in range(3)
    ]
    stress = [[None] * 3 for _ in range(3)]
    power = None
    for c in range(3):
        stress[c][c] = twice * rate[c][c] - press
        power = plus(power, stress[c][c] * rate[c][c])
        for d in range(c + 1, 3):
            both = rate[c][d] + rate[d][c]
            stress[c][d] = stress[d][c] = shear * both
            power = power + stress[c][d] * both
    flux = [
        [
            stress[c][0] * cof[0][f] + stress[c][1] * cof[1][f] + stress[c][2] * cof[2][f]
            for f in range(3)
        ]
        for c in range(3)
    ]
    return flux, power


def spread_y(first, row):
    sub = iotas()[0]
    return jnp.where(sub == 7, row, pltpu.roll(first, 7, 0))


def store_parts(nodes_of, minus_ref, plus_ref, inner_ref, rim_ref):
    sub = iotas()[0]

    def body(c, _):
        for g in range(3):
            nodes = nodes_of(c, g)
            for x in range(4):
                over = nodes[x][3]
                nodes[x][0] = nodes[x][0] + jnp.where(sub == 0, 0.0, pltpu.roll(over, 1, 0))
                r = c * 3 + g
                if x in (0, 3):
                    ref = minus_ref if x == 0 else plus_ref
                    ref[pl.ds(216 + r, 1), :] = over[7:8]
                    for b in range(3):
                        ref[pl.ds(pl.multiple_of((c * 9 + b * 3 + g) * 8, 8), 8), :] = nodes[x][b]
                else:
                    rim_ref[x - 1, pl.ds(r, 1), :] = over[7:8]
                    for b in range(3):
                        inner_ref[x - 1, c * 9 + b * 3 + g] = nodes[x][b]
        return 0

    lax.fori_loop(0, 3, body, 0)


def rim_rows(hy_ref, hc_ref, hy_s):
    rows = [
        jnp.concatenate(
            [hy_ref[:, 128 * v : 128 * v + 128], hc_ref[:, 128 * v : 128 * v + 128]], axis=0
        )
        for v in range(3)
    ]
    rows = [jnp.concatenate([r, jnp.zeros((4, 128), F32)], axis=0) for r in rows]
    for t in range(5):
        for g, tile in enumerate(split_lanes([r[8 * t : 8 * t + 8] for r in rows])):
            hy_s[g, 8 * t : 8 * t + 8, :] = tile


def masks(hx_ref, hy_ref, hc_ref, face_mask_ref, rim_mask_ref, hy_s, place):
    rim_rows(hy_ref, hc_ref, hy_s)
    for x in range(4):
        for c in range(3):
            for g in range(3):
                r = 9 * x + 6 + c
                rim_mask_ref[x, c * 3 + g : c * 3 + g + 1, :] = 1.0 - hy_s[g, r : r + 1, :]
    for c in range(3):
        tiles = element_rows(lambda s, l: hx_ref[6 + c, s : s + 8, l : l + 128], place.at[c])
        for n in range(9):
            face_mask_ref[c * 9 + n] = 1.0 - tiles[n]


def force_kernel(
    u_ref, hx_ref, hy_ref, hc_ref, eq_ref, w_ref,
    minus_ref, plus_ref, inner_ref, rim_ref, power_ref,
    hx_s, hy_s, q_s, zv_s, zs_s, w_s, xt_s, ya_s, yb_s, zn_s, place,
):
    rim_rows(hy_ref, hc_ref, hy_s)
    for k in range(6):
        tiles = element_rows(lambda s, l: hx_ref[k, s : s + 8, l : l + 128], place.at[k])
        for n in range(9):
            hx_s[k, n] = tiles[n]
    def gather_nodes(c, _):
        for g in range(3):
            cols = []
            for x in range(4):
                if x < 3:
                    u = [u_ref[c, x * 9 + b * 3 + g] for b in range(3)]
                else:
                    u = [hx_s[c, b * 3 + g] for b in range(3)]
                row = hy_s[g, pl.ds(9 * x + c, 1), :]
                u.append(spread_y(u[0], row))
                cols.append(butterfly(u))
            for y in range(4):
                for x, t in enumerate(butterfly([cols[x][y] for x in range(4)])):
                    q_s[c, (x * 4 + y) * 3 + g] = t
        return 0

    lax.fori_loop(0, 6, gather_nodes, 0)
    for c, n in ((0, 2 * 4), (1, 2)):
        for g in range(3):
            q_s[c, n * 3 + g] = q_s[c, n * 3 + g] + 1.0

    def along_z(c, _):
        for n in range(16):
            u = [q_s[c, 3 * n + g] for g in range(3)]
            u.append(next_lane(u[0]))
            h = butterfly(u)
            if n == 0:
                h[2] = h[2] + jnp.where(c == 2, 1.0, 0.0)
            for q, t in enumerate(along(interp_pair, h)):
                zv_s[q, c, n] = t
            for q, t in enumerate(along(slope_pair, h)):
                zs_s[q, c, n] = t
        return 0

    lax.fori_loop(0, 6, along_z, 0)

    def plane(z, _):
        def along_y(c, _):
            for x in range(4):
                h = [zv_s[z, c, x * 4 + y] for y in range(4)]
                s = [zs_s[z, c, x * 4 + y] for y in range(4)]
                for q, t in enumerate(along(interp_pair, h)):
                    w_s[q, 0, c * 4 + x] = t
                for q, t in enumerate(along(slope_pair, h)):
                    w_s[q, 1, c * 4 + x] = t
                for q, t in enumerate(along(interp_pair, s)):
                    w_s[q, 2, c * 4 + x] = t
            return 0

        lax.fori_loop(0, 6, along_y, 0)

        def line(y, _):
            back = [[[None] * 4 for _ in range(3)] for _ in range(3)]
            for q in range(3):
                grads = [[[None] * 3 for _ in range(6)] for _ in range(2)]
                for c in range(6):
                    for d in range(3):
                        h = [w_s[y, d, c * 4 + x] for x in range(4)]
                        pair = slope_pair(h, q) if d == 0 else interp_pair(h, q)
                        for side in range(2):
                            grads[side][c][d] = pair[side]
                flux = []
                for side in range(2):
                    p = q if side == 0 else 5 - q
                    n = p * 36 + y * 6 + z
                    f, power_ref[n] = point(grads[side][:3], grads[side][3:], eq_ref[n], w_ref[n])
                    flux.append(f)
                for c in range(3):
                    for f in range(3):
                        even = flux[0][c][f] + flux[1][c][f]
                        odd = flux[0][c][f] - flux[1][c][f]
                        (slope_back_pair if f == 0 else interp_back_pair)(back[c][f], q, even, odd)
            for c in range(3):
                for f in range(3):
                    for x in range(4):
                        if back[c][f][x] is not None:
                            xt_s[y, f, c * 4 + x] = back[c][f][x]
            return 0

        lax.fori_loop(0, 6, line, 0)

        def back_y(c, _):
            for x in range(4):
                f = [
                    [xt_s[q, d, c * 4 + x] for q in range(6)] if d or x else None
                    for d in range(3)
                ]
                h = slope_back(f[1], interp_back(f[0]) if x else None)
                s = interp_back(f[2])
                for y in range(4):
                    ya_s[z, c, x * 4 + y] = jnp.zeros((8, 128), F32) if h[y] is None else h[y]
                    yb_s[z, c, x * 4 + y] = s[y]
            return 0

        lax.fori_loop(0, 3, back_y, 0)
        return 0

    lax.fori_loop(0, 6, plane, 0)

    def back_z(c, _):
        for n in range(16):
            h = interp_back([ya_s[q, c, n] for q in range(6)])
            h = slope_back([yb_s[q, c, n] for q in range(6)], h)
            u = unbutterfly(h)
            zn_s[c, n * 3] = -(u[0] + previous_lane(u[3]))
            zn_s[c, n * 3 + 1] = -u[1]
            zn_s[c, n * 3 + 2] = -u[2]
        return 0

    lax.fori_loop(0, 3, back_z, 0)
    store_parts(lambda c, g: nodes_from(zn_s, c, g), minus_ref, plus_ref, inner_ref, rim_ref)


def nodes_from(zn_s, c, g):
    cols = [unbutterfly([zn_s[c, (x * 4 + y) * 3 + g] for y in range(4)]) for x in range(4)]
    rows = [unbutterfly([cols[x][b] for x in range(4)]) for b in range(4)]
    return [[rows[b][x] for b in range(4)] for x in range(4)]


def rows_kernel(minus_ref, plus_ref, inner_ref, rim_ref, got_low_ref, got_high_ref, *rest):
    down_ref, up_ref = rest[-2:]
    for c in range(3):
        for g in range(3):
            r = c * 3 + g
            n = (c * 9 + g) * 8
            down_ref[r : r + 1, :] = minus_ref[n : n + 1, :] + got_low_ref[n : n + 1, :]
            down_ref[27 + r : 28 + r, :] = plus_ref[n : n + 1, :] + got_high_ref[n : n + 1, :]
            for x in range(2):
                down_ref[9 * (x + 1) + r : 9 * (x + 1) + r + 1, :] = inner_ref[x, c * 9 + g, 0:1, :]
    up_ref[0:9, :] = minus_ref[216:225, :] + got_low_ref[216:225, :]
    up_ref[27:36, :] = plus_ref[216:225, :] + got_high_ref[216:225, :]
    for x in range(2):
        up_ref[9 * (x + 1) : 9 * (x + 1) + 9, :] = rim_ref[x, 0:9, :]


def assemble(c, parts, mask_ref, face_mask_ref, rim_mask_ref, own_ref, q_s):
    minus_ref, plus_ref, inner_ref, rim_ref, low_ref, high_ref, from_down_ref, from_up_ref = parts
    sub = iotas()[0]
    for g in range(3):
        r = c * 3 + g
        cols = []
        for x in range(4):
            u = []
            for b in range(3):
                n = c * 9 + b * 3 + g
                tile = pl.ds(pl.multiple_of(n * 8, 8), 8)
                if x == 0:
                    t = minus_ref[tile, :] + low_ref[tile, :]
                elif x == 3:
                    t = plus_ref[tile, :] + high_ref[tile, :]
                else:
                    t = inner_ref[x - 1, n]
                if b == 0:
                    below = from_down_ref[pl.ds(9 * x + r, 1), :]
                    t = t + jnp.where(sub == 0, below, 0.0)
                t = t * (face_mask_ref[n] if x == 3 else mask_ref[x, n])
                u.append(t)
                if x < 3:
                    own_ref[x, n] = t
            edge = pl.ds(216 + r, 1)
            if x == 0:
                top = minus_ref[edge, :] + low_ref[edge, :]
            elif x == 3:
                top = plus_ref[edge, :] + high_ref[edge, :]
            else:
                top = rim_ref[x - 1, pl.ds(r, 1), :]
            top = (top + from_up_ref[pl.ds(9 * x + r, 1), :]) * rim_mask_ref[x, pl.ds(r, 1), :]
            u.append(spread_y(u[0], top))
            cols.append(butterfly(u))
        for y in range(4):
            for x, t in enumerate(butterfly([cols[x][y] for x in range(4)])):
                q_s[c, (x * 4 + y) * 3 + g] = t


def mass_along_z(c, q_s, zv_s):
    for n in range(16):
        u = [q_s[c, 3 * n + g] for g in range(3)]
        u.append(next_lane(u[0]))
        for q, t in enumerate(along(interp_pair, butterfly(u))):
            zv_s[q, c, n] = t


def apply_kernel(
    minus_ref, plus_ref, inner_ref, rim_ref, low_ref, high_ref, from_down_ref, from_up_ref,
    mask_ref, face_mask_ref, rim_mask_ref, w_ref,
    own_ref, out_minus_ref, out_plus_ref, out_inner_ref, out_rim_ref,
    q_s, zv_s, xt_s, ya_s, zn_s,
):
    parts = (
        minus_ref, plus_ref, inner_ref, rim_ref, low_ref, high_ref, from_down_ref, from_up_ref,
    )

    def first(c, _):
        assemble(c, parts, mask_ref, face_mask_ref, rim_mask_ref, own_ref, q_s)
        mass_along_z(c, q_s, zv_s)
        return 0

    lax.fori_loop(0, 3, first, 0)

    def plane(z, _):
        for c in range(3):
            lines = [along(interp_pair, [zv_s[z, c, x * 4 + y] for y in range(4)]) for x in range(4)]
            for y in range(6):
                h = [lines[x][y] for x in range(4)]
                at = along(interp_pair, h)
                at = [at[p] * w_ref[p * 36 + y * 6 + z] for p in range(6)]
                for x, t in enumerate(interp_back(at)):
                    xt_s[c, x, y] = t
            for x in range(4):
                for y, t in enumerate(interp_back([xt_s[c, x, q] for q in range(6)])):
                    ya_s[z, c, x * 4 + y] = t
        return 0

    lax.fori_loop(0, 6, plane, 0)

    def back_z(c, _):
        for n in range(16):
            u = unbutterfly(interp_back([ya_s[q, c, n] for q in range(6)]))
            zn_s[c, n * 3] = u[0] + previous_lane(u[3])
            zn_s[c, n * 3 + 1] = u[1]
            zn_s[c, n * 3 + 2] = u[2]
        return 0

    lax.fori_loop(0, 3, back_z, 0)
    store_parts(
        lambda c, g: nodes_from(zn_s, c, g), out_minus_ref, out_plus_ref, out_inner_ref, out_rim_ref
    )


def total(t):
    return jnp.sum(jnp.sum(t, axis=0, keepdims=True), axis=1, keepdims=True)


def moments_kernel(
    minus_ref, plus_ref, inner_ref, rim_ref, low_ref, high_ref, from_down_ref, from_up_ref,
    mask_ref, face_mask_ref, rim_mask_ref, w_ref, r_ref, v_ref,
    own_ref, sums_ref, q_s, zv_s,
):
    parts = (
        minus_ref, plus_ref, inner_ref, rim_ref, low_ref, high_ref, from_down_ref, from_up_ref,
    )

    def first(c, _):
        assemble(c, parts, mask_ref, face_mask_ref, rim_mask_ref, own_ref, q_s)
        mass_along_z(c, q_s, zv_s)
        return 0

    lax.fori_loop(0, 3, first, 0)
    zero = jnp.zeros((8, 128), F32)

    def dots(n, s):
        s = list(s)
        for x in range(3):
            r, v, w = r_ref[x, n], v_ref[x, n], own_ref[x, n]
            s = [
                s[0] + r * r, s[1] + r * v, s[2] + v * v, s[3] + v * w, s[4] + w * w,
            ]
        return tuple(s)

    sums = lax.fori_loop(0, 27, dots, (zero,) * 5)

    def plane(z, s):
        s = list(s)
        for c in range(3):
            lines = [along(interp_pair, [zv_s[z, c, x * 4 + y] for y in range(4)]) for x in range(4)]
            for y in range(6):
                at = along(interp_pair, [lines[x][y] for x in range(4)])
                for p in range(6):
                    s[c] = s[c] + (at[p] * at[p]) * w_ref[p * 36 + y * 6 + z]
        return tuple(s)

    last = lax.fori_loop(0, 6, plane, (zero,) * 3)
    sums = list(sums) + [last[0] + last[1] + last[2]]
    lane = iotas(1)[1]
    row = jnp.zeros((1, 128), F32)
    for k in range(6):
        row = row + jnp.where(lane == k, total(sums[k]), 0.0)
    sums_ref[...] = jnp.broadcast_to(row, sums_ref.shape)


def coefficients(mu):
    unit = mu[1] / mu[0]
    m = [None] * 6
    scale = 1.0 / mu[0]
    for k in range(6):
        m[k] = mu[k] * scale
        scale = scale / unit
    a0 = m[0] / m[1]
    rr1 = a0 * a0 * m[2] - 2.0 * a0 * m[1] + m[0]
    b0 = rr1 / m[0]
    d1 = [1.0 + b0, -a0]
    a1 = rr1 / (d1[0] * d1[0] * m[1] + 2.0 * d1[0] * d1[1] * m[2] + d1[1] * d1[1] * m[3])
    p1 = -(a0 + a1 * d1[0])
    p2 = -a1 * d1[1]
    rr2 = (
        m[0] + p1 * p1 * m[2] + p2 * p2 * m[4]
        + 2.0 * (p1 * m[1] + p2 * m[2] + p1 * p2 * m[3])
    )
    b1 = rr2 / rr1
    q = [1.0 + b1 * d1[0], p1 + b1 * d1[1], p2]
    a2 = rr2 / (
        q[0] * q[0] * m[1] + q[1] * q[1] * m[3] + q[2] * q[2] * m[5]
        + 2.0 * (q[0] * q[1] * m[2] + q[0] * q[2] * m[3] + q[1] * q[2] * m[4])
    )
    x = [a0 + a1 * d1[0] + a2 * q[0], a1 * d1[1] + a2 * q[1], a2 * q[2]]
    return [x[0] / unit, x[1] / (unit * unit), x[2] / (unit * unit * unit)]


def final_kernel(
    sums_ref, r_ref, v_ref, w_ref, d_ref, vel_ref, a_out, v_out, d_out, place, a_s, v_s, d_s, sems
):
    lane = iotas(1)[1]
    row = jnp.sum(sums_ref[...], axis=0, keepdims=True)
    mu = [
        jnp.broadcast_to(jnp.sum(jnp.where(lane == k, row, 0.0), axis=1, keepdims=True), (8, 128))
        for k in range(6)
    ]
    k0, k1, k2 = coefficients(mu)

    def copies(c):
        pairs = ((a_s, a_out), (v_s, v_out), (d_s, d_out))
        return [
            pltpu.make_async_copy(src.at[c], dst.at[c], sems.at[c, i])
            for i, (src, dst) in enumerate(pairs)
        ]

    def body(c, _):
        for x in range(3):
            for b in range(3):
                for g in range(3):
                    n = c * 9 + b * 3 + g
                    place[x, g, pl.ds(b, 8, stride=3), :] = (
                        k0 * r_ref[x, n] + k1 * v_ref[x, n] + k2 * w_ref[x, n]
                    )
            for s in range(3):
                rows = slice(8 * s, 8 * s + 8)
                for v, t in enumerate(join_lanes([place[x, g, rows, :] for g in range(3)])):
                    lanes = slice(128 * v, 128 * v + 128)
                    a_s[c, x, rows, lanes] = t
                    new = vel_ref[c, x, rows, lanes] + step_size * t
                    v_s[c, x, rows, lanes] = new
                    d_s[c, x, rows, lanes] = d_ref[c, x, rows, lanes] + step_size * new
        for copy in copies(c):
            copy.start()
        return 0

    lax.fori_loop(0, 3, body, 0)
    for c in range(3):
        for copy in copies(c):
            copy.wait()


def call(kernel, outs, scratch, name, flops=0, limit=VMEM_LIMIT, **more):
    def run(*args):
        moved = sum(a.size * 4 for a in args) + sum(4 * math.prod(s) for s in outs)
        return pl.pallas_call(
            kernel,
            out_shape=[jax.ShapeDtypeStruct(s, F32) for s in outs],
            scratch_shapes=[pltpu.VMEM(s, F32) if isinstance(s, tuple) else s for s in scratch],
            compiler_params=pltpu.CompilerParams(vmem_limit_bytes=limit),
            cost_estimate=pl.CostEstimate(flops=flops, bytes_accessed=moved, transcendentals=0),
            name=name,
            **more,
        )(*args)

    return run


T = (8, 128)
FACE = (232, 128)
PARTS = [FACE, FACE, (2, 27) + T, (2, 16, 128)]


def solution(mesh):
    gx, gy = mesh.shape["gx"], mesh.shape["gy"]

    def moved(value, by_x, by_y):
        pairs = [
            (i * gy + j, ((i + by_x) % gx) * gy + (j + by_y) % gy)
            for i in range(gx)
            for j in range(gy)
        ]
        return lax.ppermute(value, ("gx", "gy"), pairs)

    def complete(parts, *done):
        minus, plus_face, inner, rim = parts
        low = moved(plus_face, 1, 0)
        high = moved(minus, -1, 0)
        specs = [pl.BlockSpec(memory_space=pltpu.VMEM)] * 6
        specs += [pl.BlockSpec(memory_space=pltpu.VMEM)] * len(done)
        down, up = call(rows_kernel, [(40, 128), (40, 128)], [], "rows", in_specs=specs)(
            minus, plus_face, inner, rim, low, high, *done
        )
        from_up = moved(down, 0, -1)
        from_down = moved(up, 0, 1)
        return (minus, plus_face, inner, rim, low, high, from_down, from_up)

    def on_device(displacement, velocity, energy, mass_weight, pinned):
        weight = mass_weight.reshape((216,) + T)
        dofs = energy.reshape((27,) + T)
        flags = pinned.dtype
        face, row, corner = call(
            pack_kernel,
            [(9, 24, 384), (27, 384), (9, 384)],
            [
                (2, 3, 24, 384), pltpu.VMEM((3, 24, 384), flags), (2, 3, 3, 8, 384),
                pltpu.VMEM((3, 3, 8, 384), flags), pltpu.SemaphoreType.DMA((6,)),
            ],
            "pack",
            limit=62 * 1024 * 1024,
            in_specs=[pl.BlockSpec(memory_space=pltpu.HBM)] * 3,
        )(displacement, velocity, pinned)
        hx = moved(face, -1, 0)
        hy = moved(row, 0, -1)
        hc = moved(corner, -1, -1)
        nodes, mask, heat, lump = call(
            prep_kernel,
            [(6, 27) + T, (3, 27) + T, (216,) + T, (27,) + T],
            [(9, 3, 24, 128), (6, 9) + T, (6, 3) + T],
            "prep",
            flops=4000 * 1024,
        )(displacement, velocity, pinned, dofs, weight)
        out = call(
            force_kernel,
            PARTS + [(216,) + T],
            [
                (6, 9) + T, (3, 40, 128), (6, 48) + T, (6, 6, 16) + T, (6, 6, 16) + T,
                (6, 3, 24) + T, (6, 3, 12) + T, (6, 3, 16) + T,
                (6, 3, 16) + T, (3, 48) + T, (6, 3, 24, 128),
            ],
            "force",
            flops=90000 * 1024,
        )(nodes, hx, hy, hc, heat, weight)
        parts, power = out[:4], out[4]
        energy_new, token, face_mask, rim_mask = call(
            energy_kernel,
            [(27,) + T, T, (27,) + T, (4, 16, 128)],
            [(27,) + T, (6, 9) + T, (6, 3) + T, (3, 40, 128), (3, 3, 24, 128)],
            "energy",
            flops=2000 * 1024,
        )(power, lump, dofs, hx, hy, hc)
        free = (mask, face_mask, rim_mask)
        scratch = [
            (3, 48) + T, (6, 3, 16) + T, (3, 4, 6) + T, (6, 3, 16) + T, (3, 48) + T,
        ]
        apply = call(apply_kernel, [(3, 27) + T] + PARTS, scratch, "apply", flops=13000 * 1024)
        out = apply(*complete(parts, token), *free, weight)
        r, parts = out[0], out[1:]
        out = apply(*complete(parts), *free, weight)
        v, parts = out[0], out[1:]
        w, sums = call(
            moments_kernel, [(3, 27) + T, (gx * gy, 128)], scratch[:2], "moments", flops=8000 * 1024
        )(*complete(parts), *free, weight, r, v)
        sums = sums.reshape(gx * gy, -1, 128)
        sums = lax.all_to_all(sums, ("gx", "gy"), 0, 0).reshape(-1, 128)
        shape = displacement.shape
        acceleration, velocity_new, displacement_new = call(
            final_kernel,
            [shape] * 3,
            [(3, 3, 24, 128), shape, shape, shape, pltpu.SemaphoreType.DMA((3, 3))],
            "final",
            flops=1000 * 1024,
            out_specs=[pl.BlockSpec(memory_space=pltpu.HBM)] * 3,
        )(sums, r, v, w, displacement, velocity)
        return acceleration, velocity_new, displacement_new, energy_new.reshape(energy.shape)

    spec = P(None, "gx", "gy", None)
    return jax.shard_map(
        on_device, mesh=mesh, in_specs=(spec,) * 5, out_specs=(spec,) * 4, check_vma=False
    )
```

```python
import math

import jax
import jax.numpy as jnp
import numpy as np
from jax import lax
from jax.experimental import pallas as pl
from jax.experimental.pallas import tpu as pltpu
from jax.sharding import PartitionSpec as P

step_size = 0.05
viscosity = 0.3
gamma_less = 0.4
F32 = jnp.float32
VMEM_LIMIT = 32 * 1024 * 1024


def tables():
    root_five = 1.0 / math.sqrt(5.0)
    lobatto = np.array([0.0, 0.5 - 0.5 * root_five, 0.5 + 0.5 * root_five, 1.0])
    legendre = np.array(
        [
            -0.932469514203152,
            -0.6612093864662645,
            -0.2386191860831909,
            0.2386191860831909,
            0.6612093864662645,
            0.932469514203152,
        ]
    )
    t = 0.5 + 0.5 * legendre
    values = np.ones((6, 4))
    slopes = np.zeros((6, 4))
    for a in range(4):
        for b in range(4):
            if b != a:
                values[:, a] *= (t - lobatto[b]) / (lobatto[a] - lobatto[b])
        for c in range(4):
            if c != a:
                term = np.ones(6) / (lobatto[a] - lobatto[c])
                for b in range(4):
                    if b != a and b != c:
                        term = term * (t - lobatto[b]) / (lobatto[a] - lobatto[b])
                slopes[:, a] += term
    thermo = np.stack([(1.0 - t) * (1.0 - t), 2.0 * t * (1.0 - t), t * t], axis=1)
    return values, slopes, thermo


VALUES, SLOPES, THERMO = tables()
LOBATTO = np.array([0.0, 0.5 - 0.5 / math.sqrt(5.0), 0.5 + 0.5 / math.sqrt(5.0), 1.0]) - 0.5
ABSCISSA = VALUES @ LOBATTO
INVERSE = float(0.5 / LOBATTO[1])
RATIO = float(LOBATTO[0] / LOBATTO[1])
BK = [float((VALUES[q, 0] + VALUES[q, 3]) / 2) for q in range(3)]
BM = [float((VALUES[q, 0] - VALUES[q, 3]) / 2) for q in range(3)]
BL = [float(ABSCISSA[q]) for q in range(3)]
DK = [float((SLOPES[q, 0] + SLOPES[q, 3]) / 2) for q in range(3)]
DM = [float((SLOPES[q, 0] - SLOPES[q, 3]) / 2) for q in range(3)]
TE = [float((THERMO[q, 0] + THERMO[q, 2]) / 2) for q in range(3)]
TO = [float((THERMO[q, 0] - THERMO[q, 2]) / 2) for q in range(3)]
TM = [float(THERMO[q, 1]) for q in range(3)]


def butterfly(u):
    e0, e1, o0, o1 = u[0] + u[3], u[1] + u[2], u[0] - u[3], u[1] - u[2]
    return [0.5 * e1, e0 - e1, INVERSE * o1, o0 - RATIO * o1]


def unbutterfly(r):
    e0, e1, o0, o1 = r[1], 0.5 * r[0] - r[1], r[3], INVERSE * r[2] - RATIO * r[3]
    return [e0 + o0, e1 + o1, e1 - o1, e0 - o0]


def interp_pair(h, q):
    even = h[0] + BK[q] * h[1]
    odd = BL[q] * h[2] + BM[q] * h[3]
    return even + odd, even - odd


def slope_pair(h, q):
    even = h[2] + DM[q] * h[3]
    odd = DK[q] * h[1]
    return even + odd, even - odd


def along(pair_fn, h):
    out = [None] * 6
    for q in range(3):
        out[q], out[5 - q] = pair_fn(h, q)
    return out


def plus(total, term):
    return term if total is None else total + term


def interp_back_pair(h, q, even, odd):
    h[0] = plus(h[0], even)
    h[1] = plus(h[1], BK[q] * even)
    h[2] = plus(h[2], BL[q] * odd)
    h[3] = plus(h[3], BM[q] * odd)


def slope_back_pair(h, q, even, odd):
    h[1] = plus(h[1], DK[q] * odd)
    h[2] = plus(h[2], even)
    h[3] = plus(h[3], DM[q] * even)


def interp_back(f, h=None):
    h = [None] * 4 if h is None else list(h)
    for q in range(3):
        interp_back_pair(h, q, f[q] + f[5 - q], f[q] - f[5 - q])
    return h


def slope_back(f, h=None):
    h = [None] * 4 if h is None else list(h)
    for q in range(3):
        slope_back_pair(h, q, f[q] + f[5 - q], f[q] - f[5 - q])
    return h


def thermo_along(u):
    even, odd, mid = u[0] + u[2], u[0] - u[2], u[1]
    out = [None] * 6
    for q in range(3):
        both, one = TE[q] * even + TM[q] * mid, TO[q] * odd
        out[q], out[5 - q] = both + one, both - one
    return out


def thermo_back(f):
    even = mid = odd = None
    for q in range(3):
        both, one = f[q] + f[5 - q], f[q] - f[5 - q]
        even = plus(even, TE[q] * both)
        mid = plus(mid, TM[q] * both)
        odd = plus(odd, TO[q] * one)
    return [even + odd, mid, even - odd]


def iotas(rows=8):
    shape = (rows, 128)
    return lax.broadcasted_iota(jnp.int32, shape, 0), lax.broadcasted_iota(jnp.int32, shape, 1)


def gather_lanes(x, index):
    return jnp.take_along_axis(x, index, axis=1, mode="promise_in_bounds")


def split_lanes(parts, rows=8):
    lane = iotas(rows)[1]
    out = []
    for g in range(3):
        place = 3 * lane + g
        index = place & 127
        moved = [gather_lanes(p, index) for p in parts]
        out.append(
            jnp.where(place < 128, moved[0], jnp.where(place < 256, moved[1], moved[2]))
        )
    return out


def join_lanes(parts):
    lane = iotas()[1]
    out = []
    for v in range(3):
        place = lane + 128 * v
        index = place // 3
        g = place - 3 * index
        moved = [gather_lanes(p, index) for p in parts]
        out.append(jnp.where(g == 0, moved[0], jnp.where(g == 1, moved[1], moved[2])))
    return out


def next_lane(x):
    return pltpu.roll(x, 127, 1)


def previous_lane(x):
    return pltpu.roll(x, 1, 1)


def pack_kernel(d_ref, v_ref, f_ref, x_ref, y_ref, c_ref, face, face_f, low, low_f, sems):
    copies = []
    for n, ref in enumerate((d_ref, v_ref, f_ref)):
        to_face, to_low = (face.at[n], low.at[n]) if n < 2 else (face_f, low_f)
        copies.append(pltpu.make_async_copy(ref.at[:, 0], to_face, sems.at[2 * n]))
        copies.append(pltpu.make_async_copy(ref.at[:, :, 0:8], to_low, sems.at[2 * n + 1]))
    for copy in copies:
        copy.start()
    for copy in copies:
        copy.wait()
    for n in range(3):
        for c in range(3):
            k = 3 * n + c
            layer = (face[n, c] if n < 2 else face_f[c]).astype(F32)
            x_ref[k] = layer
            c_ref[k : k + 1, :] = layer[0:1]
            for x in range(3):
                r = 9 * x + k
                row = low[n, c, x, 0:1, :] if n < 2 else low_f[c, x, 0:1, :]
                y_ref[r : r + 1, :] = row.astype(F32)


def element_rows(load, place):
    for t in range(3):
        tiles = split_lanes([load(8 * t, 128 * v) for v in range(3)])
        for g in range(3):
            place[g, 8 * t : 8 * t + 8, :] = tiles[g]
    return [place[g, pl.ds(b, 8, stride=3), :] for b in range(3) for g in range(3)]


def prep_kernel(d_ref, v_ref, e_ref, u_ref, eq_ref, place, ez_s, ey_s):
    def body(c, _):
        for x in range(3):
            for k, ref in enumerate((d_ref, v_ref)):
                tiles = element_rows(
                    lambda s, l: ref[c, x, s : s + 8, l : l + 128], place.at[2 * x + k]
                )
                for n in range(9):
                    u_ref[3 * k + c, x * 9 + n] = tiles[n]
        return 0

    lax.fori_loop(0, 3, body, 0)
    for n in range(9):
        for q, t in enumerate(thermo_along([gamma_less * e_ref[3 * n + g] for g in range(3)])):
            ez_s[q, n] = t

    def plane(z, _):
        for x in range(3):
            for q, t in enumerate(thermo_along([ez_s[z, 3 * x + y] for y in range(3)])):
                ey_s[q, x] = t
        for y in range(6):
            for q, t in enumerate(thermo_along([ey_s[y, x] for x in range(3)])):
                eq_ref[q * 36 + y * 6 + z] = t
        return 0

    lax.fori_loop(0, 6, plane, 0)


def project(at_ref, z_s, x_s, out_ref):
    def plane(z, _):
        for y in range(6):
            for x, t in enumerate(thermo_back([at_ref[p * 36 + y * 6 + z] for p in range(6)])):
                x_s[y, x] = t
        for x in range(3):
            for y, t in enumerate(thermo_back([x_s[q, x] for q in range(6)])):
                z_s[z, 3 * x + y] = t
        return 0

    lax.fori_loop(0, 6, plane, 0)
    for n in range(9):
        for g, t in enumerate(thermo_back([z_s[q, n] for q in range(6)])):
            out_ref[3 * n + g] = t


def energy_kernel(
    power_ref, w_ref, e_ref, f_ref, hx_ref, hy_ref, hc_ref,
    out_ref, token_ref, mask_ref, face_mask_ref, rim_mask_ref,
    lump_ref, sum_s, z_s, x_s, hy_s, place,
):
    masks(hx_ref, hy_ref, hc_ref, face_mask_ref, rim_mask_ref, hy_s, place)

    def own(c, _):
        for x in range(3):
            tiles = element_rows(
                lambda s, l: f_ref[c, x, s : s + 8, l : l + 128].astype(F32), place.at[x]
            )
            for n in range(9):
                mask_ref[x, c * 9 + n] = 1.0 - tiles[n]
        return 0

    lax.fori_loop(0, 3, own, 0)
    project(w_ref, z_s, x_s, lump_ref)
    project(power_ref, z_s, x_s, sum_s)

    def body(n, _):
        out_ref[n] = e_ref[n] + step_size * (sum_s[n] / lump_ref[n])
        return 0

    lax.fori_loop(0, 27, body, 0)
    token_ref[...] = sum_s[0]


def point(jac, vel, energy, mass):
    cof = [
        [
            jac[(c + 1) % 3][(d + 1) % 3] * jac[(c + 2) % 3][(d + 2) % 3]
            - jac[(c + 1) % 3][(d + 2) % 3] * jac[(c + 2) % 3][(d + 1) % 3]
            for d in range(3)
        ]
        for c in range(3)
    ]
    det = jac[0][0] * cof[0][0] + jac[0][1] * cof[0][1] + jac[0][2] * cof[0][2]
    inv = pl.reciprocal(det, approx=True)
    inv = inv * (2.0 - det * inv)
    scale = mass * inv
    shear = (viscosity * scale) * inv
    twice = shear + shear
    press = scale * energy
    rate = [
        [vel[c][0] * cof[e][0] + vel[c][1] * cof[e][1] + vel[c][2] * cof[e][2] for e in range(3)]
        for c in range(3)
    ]
    stress = [[None] * 3 for _ in range(3)]
    power = None
    for c in range(3):
        stress[c][c] = twice * rate[c][c] - press
        power = plus(power, stress[c][c] * rate[c][c])
        for d in range(c + 1, 3):
            both = rate[c][d] + rate[d][c]
            stress[c][d] = stress[d][c] = shear * both
            power = power + stress[c][d] * both
    flux = [
        [
            stress[c][0] * cof[0][f] + stress[c][1] * cof[1][f] + stress[c][2] * cof[2][f]
            for f in range(3)
        ]
        for c in range(3)
    ]
    return flux, power


def spread_y(first, row):
    sub = iotas()[0]
    return jnp.where(sub == 7, row, pltpu.roll(first, 7, 0))


def store_parts(nodes_of, minus_ref, plus_ref, inner_ref, rim_ref):
    sub = iotas()[0]

    def body(c, _):
        for g in range(3):
            nodes = nodes_of(c, g)
            for x in range(4):
                over = nodes[x][3]
                nodes[x][0] = nodes[x][0] + jnp.where(sub == 0, 0.0, pltpu.roll(over, 1, 0))
                r = c * 3 + g
                if x in (0, 3):
                    ref = minus_ref if x == 0 else plus_ref
                    ref[pl.ds(216 + r, 1), :] = over[7:8]
                    for b in range(3):
                        ref[pl.ds(pl.multiple_of((c * 9 + b * 3 + g) * 8, 8), 8), :] = nodes[x][b]
                else:
                    rim_ref[x - 1, pl.ds(r, 1), :] = over[7:8]
                    for b in range(3):
                        inner_ref[x - 1, c * 9 + b * 3 + g] = nodes[x][b]
        return 0

    lax.fori_loop(0, 3, body, 0)


def rim_rows(hy_ref, hc_ref, hy_s):
    rows = [
        jnp.concatenate(
            [hy_ref[:, 128 * v : 128 * v + 128], hc_ref[:, 128 * v : 128 * v + 128]], axis=0
        )
        for v in range(3)
    ]
    rows = [jnp.concatenate([r, jnp.zeros((4, 128), F32)], axis=0) for r in rows]
    for t in range(5):
        for g, tile in enumerate(split_lanes([r[8 * t : 8 * t + 8] for r in rows])):
            hy_s[g, 8 * t : 8 * t + 8, :] = tile


def masks(hx_ref, hy_ref, hc_ref, face_mask_ref, rim_mask_ref, hy_s, place):
    rim_rows(hy_ref, hc_ref, hy_s)
    for x in range(4):
        for c in range(3):
            for g in range(3):
                r = 9 * x + 6 + c
                rim_mask_ref[x, c * 3 + g : c * 3 + g + 1, :] = 1.0 - hy_s[g, r : r + 1, :]
    for c in range(3):
        tiles = element_rows(lambda s, l: hx_ref[6 + c, s : s + 8, l : l + 128], place.at[c])
        for n in range(9):
            face_mask_ref[c * 9 + n] = 1.0 - tiles[n]


def force_kernel(
    u_ref, hx_ref, hy_ref, hc_ref, eq_ref, w_ref,
    minus_ref, plus_ref, inner_ref, rim_ref, power_ref,
    hx_s, hy_s, q_s, zv_s, zs_s, w_s, xt_s, ya_s, yb_s, zn_s, place,
):
    rim_rows(hy_ref, hc_ref, hy_s)
    for k in range(6):
        tiles = element_rows(lambda s, l: hx_ref[k, s : s + 8, l : l + 128], place.at[k])
        for n in range(9):
            hx_s[k, n] = tiles[n]
    def gather_nodes(c, _):
        for g in range(3):
            cols = []
            for x in range(4):
                if x < 3:
                    u = [u_ref[c, x * 9 + b * 3 + g] for b in range(3)]
                else:
                    u = [hx_s[c, b * 3 + g] for b in range(3)]
                row = hy_s[g, pl.ds(9 * x + c, 1), :]
                u.append(spread_y(u[0], row))
                cols.append(butterfly(u))
            for y in range(4):
                for x, t in enumerate(butterfly([cols[x][y] for x in range(4)])):
                    q_s[c, (x * 4 + y) * 3 + g] = t
        return 0

    lax.fori_loop(0, 6, gather_nodes, 0)
    for c, n in ((0, 2 * 4), (1, 2)):
        for g in range(3):
            q_s[c, n * 3 + g] = q_s[c, n * 3 + g] + 1.0

    def along_z(c, _):
        for n in range(16):
            u = [q_s[c, 3 * n + g] for g in range(3)]
            u.append(next_lane(u[0]))
            h = butterfly(u)
            if n == 0:
                h[2] = h[2] + jnp.where(c == 2, 1.0, 0.0)
            for q, t in enumerate(along(interp_pair, h)):
                zv_s[q, c, n] = t
            for q, t in enumerate(along(slope_pair, h)):
                zs_s[q, c, n] = t
        return 0

    lax.fori_loop(0, 6, along_z, 0)

    def plane(z, _):
        def along_y(c, _):
            for x in range(4):
                h = [zv_s[z, c, x * 4 + y] for y in range(4)]
                s = [zs_s[z, c, x * 4 + y] for y in range(4)]
                for q, t in enumerate(along(interp_pair, h)):
                    w_s[q, 0, c * 4 + x] = t
                for q, t in enumerate(along(slope_pair, h)):
                    w_s[q, 1, c * 4 + x] = t
                for q, t in enumerate(along(interp_pair, s)):
                    w_s[q, 2, c * 4 + x] = t
            return 0

        lax.fori_loop(0, 6, along_y, 0)

        def line(y, _):
            back = [[[None] * 4 for _ in range(3)] for _ in range(3)]
            for q in range(3):
                grads = [[[None] * 3 for _ in range(6)] for _ in range(2)]
                for c in range(6):
                    for d in range(3):
                        h = [w_s[y, d, c * 4 + x] for x in range(4)]
                        pair = slope_pair(h, q) if d == 0 else interp_pair(h, q)
                        for side in range(2):
                            grads[side][c][d] = pair[side]
                flux = []
                for side in range(2):
                    p = q if side == 0 else 5 - q
                    n = p * 36 + y * 6 + z
                    f, power_ref[n] = point(grads[side][:3], grads[side][3:], eq_ref[n], w_ref[n])
                    flux.append(f)
                for c in range(3):
                    for f in range(3):
                        even = flux[0][c][f] + flux[1][c][f]
                        odd = flux[0][c][f] - flux[1][c][f]
                        (slope_back_pair if f == 0 else interp_back_pair)(back[c][f], q, even, odd)
            for c in range(3):
                for f in range(3):
                    for x in range(4):
                        if back[c][f][x] is not None:
                            xt_s[y, f, c * 4 + x] = back[c][f][x]
            return 0

        lax.fori_loop(0, 6, line, 0)

        def back_y(c, _):
            for x in range(4):
                f = [
                    [xt_s[q, d, c * 4 + x] for q in range(6)] if d or x else None
                    for d in range(3)
                ]
                h = slope_back(f[1], interp_back(f[0]) if x else None)
                s = interp_back(f[2])
                for y in range(4):
                    ya_s[z, c, x * 4 + y] = jnp.zeros((8, 128), F32) if h[y] is None else h[y]
                    yb_s[z, c, x * 4 + y] = s[y]
            return 0

        lax.fori_loop(0, 3, back_y, 0)
        return 0

    lax.fori_loop(0, 6, plane, 0)

    def back_z(c, _):
        for n in range(16):
            h = interp_back([ya_s[q, c, n] for q in range(6)])
            h = slope_back([yb_s[q, c, n] for q in range(6)], h)
            u = unbutterfly(h)
            zn_s[c, n * 3] = -(u[0] + previous_lane(u[3]))
            zn_s[c, n * 3 + 1] = -u[1]
            zn_s[c, n * 3 + 2] = -u[2]
        return 0

    lax.fori_loop(0, 3, back_z, 0)
    store_parts(lambda c, g: nodes_from(zn_s, c, g), minus_ref, plus_ref, inner_ref, rim_ref)


def nodes_from(zn_s, c, g):
    cols = [unbutterfly([zn_s[c, (x * 4 + y) * 3 + g] for y in range(4)]) for x in range(4)]
    rows = [unbutterfly([cols[x][b] for x in range(4)]) for b in range(4)]
    return [[rows[b][x] for b in range(4)] for x in range(4)]


def rows_kernel(minus_ref, plus_ref, inner_ref, rim_ref, got_low_ref, got_high_ref, *rest):
    down_ref, up_ref = rest[-2:]
    for c in range(3):
        for g in range(3):
            r = c * 3 + g
            n = (c * 9 + g) * 8
            down_ref[r : r + 1, :] = minus_ref[n : n + 1, :] + got_low_ref[n : n + 1, :]
            down_ref[27 + r : 28 + r, :] = plus_ref[n : n + 1, :] + got_high_ref[n : n + 1, :]
            for x in range(2):
                down_ref[9 * (x + 1) + r : 9 * (x + 1) + r + 1, :] = inner_ref[x, c * 9 + g, 0:1, :]
    up_ref[0:9, :] = minus_ref[216:225, :] + got_low_ref[216:225, :]
    up_ref[27:36, :] = plus_ref[216:225, :] + got_high_ref[216:225, :]
    for x in range(2):
        up_ref[9 * (x + 1) : 9 * (x + 1) + 9, :] = rim_ref[x, 0:9, :]


def assemble(c, parts, mask_ref, face_mask_ref, rim_mask_ref, own_ref, q_s):
    minus_ref, plus_ref, inner_ref, rim_ref, low_ref, high_ref, from_down_ref, from_up_ref = parts
    sub = iotas()[0]
    for g in range(3):
        r = c * 3 + g
        cols = []
        for x in range(4):
            u = []
            for b in range(3):
                n = c * 9 + b * 3 + g
                tile = pl.ds(pl.multiple_of(n * 8, 8), 8)
                if x == 0:
                    t = minus_ref[tile, :] + low_ref[tile, :]
                elif x == 3:
                    t = plus_ref[tile, :] + high_ref[tile, :]
                else:
                    t = inner_ref[x - 1, n]
                if b == 0:
                    below = from_down_ref[pl.ds(9 * x + r, 1), :]
                    t = t + jnp.where(sub == 0, below, 0.0)
                t = t * (face_mask_ref[n] if x == 3 else mask_ref[x, n])
                u.append(t)
                if x < 3:
                    own_ref[x, n] = t
            edge = pl.ds(216 + r, 1)
            if x == 0:
                top = minus_ref[edge, :] + low_ref[edge, :]
            elif x == 3:
                top = plus_ref[edge, :] + high_ref[edge, :]
            else:
                top = rim_ref[x - 1, pl.ds(r, 1), :]
            top = (top + from_up_ref[pl.ds(9 * x + r, 1), :]) * rim_mask_ref[x, pl.ds(r, 1), :]
            u.append(spread_y(u[0], top))
            cols.append(butterfly(u))
        for y in range(4):
            for x, t in enumerate(butterfly([cols[x][y] for x in range(4)])):
                q_s[c, (x * 4 + y) * 3 + g] = t


def mass_along_z(c, q_s, zv_s):
    for n in range(16):
        u = [q_s[c, 3 * n + g] for g in range(3)]
        u.append(next_lane(u[0]))
        for q, t in enumerate(along(interp_pair, butterfly(u))):
            zv_s[q, c, n] = t


def apply_kernel(
    minus_ref, plus_ref, inner_ref, rim_ref, low_ref, high_ref, from_down_ref, from_up_ref,
    mask_ref, face_mask_ref, rim_mask_ref, w_ref,
    own_ref, out_minus_ref, out_plus_ref, out_inner_ref, out_rim_ref,
    q_s, zv_s, xt_s, ya_s, zn_s,
):
    parts = (
        minus_ref, plus_ref, inner_ref, rim_ref, low_ref, high_ref, from_down_ref, from_up_ref,
    )

    def first(c, _):
        assemble(c, parts, mask_ref, face_mask_ref, rim_mask_ref, own_ref, q_s)
        mass_along_z(c, q_s, zv_s)
        return 0

    lax.fori_loop(0, 3, first, 0)

    def plane(z, _):
        for c in range(3):
            lines = [along(interp_pair, [zv_s[z, c, x * 4 + y] for y in range(4)]) for x in range(4)]
            for y in range(6):
                h = [lines[x][y] for x in range(4)]
                at = along(interp_pair, h)
                at = [at[p] * w_ref[p * 36 + y * 6 + z] for p in range(6)]
                for x, t in enumerate(interp_back(at)):
                    xt_s[c, x, y] = t
            for x in range(4):
                for y, t in enumerate(interp_back([xt_s[c, x, q] for q in range(6)])):
                    ya_s[z, c, x * 4 + y] = t
        return 0

    lax.fori_loop(0, 6, plane, 0)

    def back_z(c, _):
        for n in range(16):
            u = unbutterfly(interp_back([ya_s[q, c, n] for q in range(6)]))
            zn_s[c, n * 3] = u[0] + previous_lane(u[3])
            zn_s[c, n * 3 + 1] = u[1]
            zn_s[c, n * 3 + 2] = u[2]
        return 0

    lax.fori_loop(0, 3, back_z, 0)
    store_parts(
        lambda c, g: nodes_from(zn_s, c, g), out_minus_ref, out_plus_ref, out_inner_ref, out_rim_ref
    )


def total(t):
    return jnp.sum(jnp.sum(t, axis=0, keepdims=True), axis=1, keepdims=True)


def moments_kernel(
    minus_ref, plus_ref, inner_ref, rim_ref, low_ref, high_ref, from_down_ref, from_up_ref,
    mask_ref, face_mask_ref, rim_mask_ref, w_ref, r_ref, v_ref,
    own_ref, sums_ref, q_s, zv_s,
):
    parts = (
        minus_ref, plus_ref, inner_ref, rim_ref, low_ref, high_ref, from_down_ref, from_up_ref,
    )

    def first(c, _):
        assemble(c, parts, mask_ref, face_mask_ref, rim_mask_ref, own_ref, q_s)
        mass_along_z(c, q_s, zv_s)
        return 0

    lax.fori_loop(0, 3, first, 0)
    zero = jnp.zeros((8, 128), F32)

    def dots(n, s):
        s = list(s)
        for x in range(3):
            r, v, w = r_ref[x, n], v_ref[x, n], own_ref[x, n]
            s = [
                s[0] + r * r, s[1] + r * v, s[2] + v * v, s[3] + v * w, s[4] + w * w,
            ]
        return tuple(s)

    sums = lax.fori_loop(0, 27, dots, (zero,) * 5)

    def plane(z, s):
        s = list(s)
        for c in range(3):
            lines = [along(interp_pair, [zv_s[z, c, x * 4 + y] for y in range(4)]) for x in range(4)]
            for y in range(6):
                at = along(interp_pair, [lines[x][y] for x in range(4)])
                for p in range(6):
                    s[c] = s[c] + (at[p] * at[p]) * w_ref[p * 36 + y * 6 + z]
        return tuple(s)

    last = lax.fori_loop(0, 6, plane, (zero,) * 3)
    sums = list(sums) + [last[0] + last[1] + last[2]]
    lane = iotas(1)[1]
    row = jnp.zeros((1, 128), F32)
    for k in range(6):
        row = row + jnp.where(lane == k, total(sums[k]), 0.0)
    sums_ref[...] = jnp.broadcast_to(row, sums_ref.shape)


def coefficients(mu):
    unit = mu[1] / mu[0]
    m = [None] * 6
    scale = 1.0 / mu[0]
    for k in range(6):
        m[k] = mu[k] * scale
        scale = scale / unit
    a0 = m[0] / m[1]
    rr1 = a0 * a0 * m[2] - 2.0 * a0 * m[1] + m[0]
    b0 = rr1 / m[0]
    d1 = [1.0 + b0, -a0]
    a1 = rr1 / (d1[0] * d1[0] * m[1] + 2.0 * d1[0] * d1[1] * m[2] + d1[1] * d1[1] * m[3])
    p1 = -(a0 + a1 * d1[0])
    p2 = -a1 * d1[1]
    rr2 = (
        m[0] + p1 * p1 * m[2] + p2 * p2 * m[4]
        + 2.0 * (p1 * m[1] + p2 * m[2] + p1 * p2 * m[3])
    )
    b1 = rr2 / rr1
    q = [1.0 + b1 * d1[0], p1 + b1 * d1[1], p2]
    a2 = rr2 / (
        q[0] * q[0] * m[1] + q[1] * q[1] * m[3] + q[2] * q[2] * m[5]
        + 2.0 * (q[0] * q[1] * m[2] + q[0] * q[2] * m[3] + q[1] * q[2] * m[4])
    )
    x = [a0 + a1 * d1[0] + a2 * q[0], a1 * d1[1] + a2 * q[1], a2 * q[2]]
    return [x[0] / unit, x[1] / (unit * unit), x[2] / (unit * unit * unit)]


def final_kernel(
    sums_ref, r_ref, v_ref, w_ref, d_ref, vel_ref, a_out, v_out, d_out, place, a_s, v_s, d_s, sems
):
    lane = iotas(1)[1]
    row = jnp.sum(sums_ref[...], axis=0, keepdims=True)
    mu = [
        jnp.broadcast_to(jnp.sum(jnp.where(lane == k, row, 0.0), axis=1, keepdims=True), (8, 128))
        for k in range(6)
    ]
    k0, k1, k2 = coefficients(mu)

    def copies(c):
        pairs = ((a_s, a_out), (v_s, v_out), (d_s, d_out))
        return [
            pltpu.make_async_copy(src.at[c], dst.at[c], sems.at[c, i])
            for i, (src, dst) in enumerate(pairs)
        ]

    def body(c, _):
        for x in range(3):
            for b in range(3):
                for g in range(3):
                    n = c * 9 + b * 3 + g
                    place[x, g, pl.ds(b, 8, stride=3), :] = (
                        k0 * r_ref[x, n] + k1 * v_ref[x, n] + k2 * w_ref[x, n]
                    )
            for s in range(3):
                rows = slice(8 * s, 8 * s + 8)
                for v, t in enumerate(join_lanes([place[x, g, rows, :] for g in range(3)])):
                    lanes = slice(128 * v, 128 * v + 128)
                    a_s[c, x, rows, lanes] = t
                    new = vel_ref[c, x, rows, lanes] + step_size * t
                    v_s[c, x, rows, lanes] = new
                    d_s[c, x, rows, lanes] = d_ref[c, x, rows, lanes] + step_size * new
        for copy in copies(c):
            copy.start()
        return 0

    lax.fori_loop(0, 3, body, 0)
    for c in range(3):
        for copy in copies(c):
            copy.wait()


def call(kernel, outs, scratch, name, flops=0, limit=VMEM_LIMIT, **more):
    def run(*args):
        moved = sum(a.size * 4 for a in args) + sum(4 * math.prod(s) for s in outs)
        return pl.pallas_call(
            kernel,
            out_shape=[jax.ShapeDtypeStruct(s, F32) for s in outs],
            scratch_shapes=[pltpu.VMEM(s, F32) if isinstance(s, tuple) else s for s in scratch],
            compiler_params=pltpu.CompilerParams(vmem_limit_bytes=limit),
            cost_estimate=pl.CostEstimate(flops=flops, bytes_accessed=moved, transcendentals=0),
            name=name,
            **more,
        )(*args)

    return run


T = (8, 128)
FACE = (232, 128)
PARTS = [FACE, FACE, (2, 27) + T, (2, 16, 128)]


def solution(mesh):
    gx, gy = mesh.shape["gx"], mesh.shape["gy"]

    def moved(value, by_x, by_y):
        pairs = [
            (i * gy + j, ((i + by_x) % gx) * gy + (j + by_y) % gy)
            for i in range(gx)
            for j in range(gy)
        ]
        return lax.ppermute(value, ("gx", "gy"), pairs)

    def complete(parts, *done):
        minus, plus_face, inner, rim = parts
        low = moved(plus_face, 1, 0)
        high = moved(minus, -1, 0)
        specs = [pl.BlockSpec(memory_space=pltpu.VMEM)] * 6
        specs += [pl.BlockSpec(memory_space=pltpu.VMEM)] * len(done)
        down, up = call(rows_kernel, [(40, 128), (40, 128)], [], "rows", in_specs=specs)(
            minus, plus_face, inner, rim, low, high, *done
        )
        from_up = moved(down, 0, -1)
        from_down = moved(up, 0, 1)
        return (minus, plus_face, inner, rim, low, high, from_down, from_up)

    def on_device(displacement, velocity, energy, mass_weight, pinned):
        weight = mass_weight.reshape((216,) + T)
        dofs = energy.reshape((27,) + T)
        flags = pinned.dtype
        face, row, corner = call(
            pack_kernel,
            [(9, 24, 384), (27, 384), (9, 384)],
            [
                (2, 3, 24, 384), pltpu.VMEM((3, 24, 384), flags), (2, 3, 3, 8, 384),
                pltpu.VMEM((3, 3, 8, 384), flags), pltpu.SemaphoreType.DMA((6,)),
            ],
            "pack",
            limit=62 * 1024 * 1024,
            in_specs=[pl.BlockSpec(memory_space=pltpu.HBM)] * 3,
        )(displacement, velocity, pinned)
        hx = moved(face, -1, 0)
        hy = moved(row, 0, -1)
        hc = moved(corner, -1, -1)
        nodes, heat = call(
            prep_kernel,
            [(6, 27) + T, (216,) + T],
            [(6, 3, 24, 128), (6, 9) + T, (6, 3) + T],
            "prep",
            flops=4000 * 1024,
        )(displacement, velocity, dofs)
        out = call(
            force_kernel,
            PARTS + [(216,) + T],
            [
                (6, 9) + T, (3, 40, 128), (6, 48) + T, (6, 6, 16) + T, (6, 6, 16) + T,
                (6, 3, 24) + T, (6, 3, 12) + T, (6, 3, 16) + T,
                (6, 3, 16) + T, (3, 48) + T, (6, 3, 24, 128),
            ],
            "force",
            flops=90000 * 1024,
        )(nodes, hx, hy, hc, heat, weight)
        parts, power = out[:4], out[4]
        energy_new, token, mask, face_mask, rim_mask = call(
            energy_kernel,
            [(27,) + T, T, (3, 27) + T, (27,) + T, (4, 16, 128)],
            [(27,) + T, (27,) + T, (6, 9) + T, (6, 3) + T, (3, 40, 128), (3, 3, 24, 128)],
            "energy",
            flops=2000 * 1024,
        )(power, weight, dofs, pinned, hx, hy, hc)
        free = (mask, face_mask, rim_mask)
        scratch = [
            (3, 48) + T, (6, 3, 16) + T, (3, 4, 6) + T, (6, 3, 16) + T, (3, 48) + T,
        ]
        apply = call(apply_kernel, [(3, 27) + T] + PARTS, scratch, "apply", flops=13000 * 1024)
        out = apply(*complete(parts, token), *free, weight)
        r, parts = out[0], out[1:]
        out = apply(*complete(parts), *free, weight)
        v, parts = out[0], out[1:]
        w, sums = call(
            moments_kernel, [(3, 27) + T, (gx * gy, 128)], scratch[:2], "moments", flops=8000 * 1024
        )(*complete(parts), *free, weight, r, v)
        sums = sums.reshape(gx * gy, -1, 128)
        sums = lax.all_to_all(sums, ("gx", "gy"), 0, 0).reshape(-1, 128)
        shape = displacement.shape
        acceleration, velocity_new, displacement_new = call(
            final_kernel,
            [shape] * 3,
            [(3, 3, 24, 128), shape, shape, shape, pltpu.SemaphoreType.DMA((3, 3))],
            "final",
            flops=1000 * 1024,
            out_specs=[pl.BlockSpec(memory_space=pltpu.HBM)] * 3,
        )(sums, r, v, w, displacement, velocity)
        return acceleration, velocity_new, displacement_new, energy_new.reshape(energy.shape)

    spec = P(None, "gx", "gy", None)
    return jax.shard_map(
        on_device, mesh=mesh, in_specs=(spec,) * 5, out_specs=(spec,) * 4, check_vma=False
    )
```

```python
import math

import jax
import jax.numpy as jnp
import numpy as np
from jax import lax
from jax.experimental import pallas as pl
from jax.experimental.pallas import tpu as pltpu
from jax.sharding import PartitionSpec as P

step_size = 0.05
viscosity = 0.3
gamma_less = 0.4
F32 = jnp.float32
VMEM_LIMIT = 32 * 1024 * 1024


def tables():
    root_five = 1.0 / math.sqrt(5.0)
    lobatto = np.array([0.0, 0.5 - 0.5 * root_five, 0.5 + 0.5 * root_five, 1.0])
    legendre = np.array(
        [
            -0.932469514203152,
            -0.6612093864662645,
            -0.2386191860831909,
            0.2386191860831909,
            0.6612093864662645,
            0.932469514203152,
        ]
    )
    t = 0.5 + 0.5 * legendre
    values = np.ones((6, 4))
    slopes = np.zeros((6, 4))
    for a in range(4):
        for b in range(4):
            if b != a:
                values[:, a] *= (t - lobatto[b]) / (lobatto[a] - lobatto[b])
        for c in range(4):
            if c != a:
                term = np.ones(6) / (lobatto[a] - lobatto[c])
                for b in range(4):
                    if b != a and b != c:
                        term = term * (t - lobatto[b]) / (lobatto[a] - lobatto[b])
                slopes[:, a] += term
    thermo = np.stack([(1.0 - t) * (1.0 - t), 2.0 * t * (1.0 - t), t * t], axis=1)
    return values, slopes, thermo


VALUES, SLOPES, THERMO = tables()
LOBATTO = np.array([0.0, 0.5 - 0.5 / math.sqrt(5.0), 0.5 + 0.5 / math.sqrt(5.0), 1.0]) - 0.5
ABSCISSA = VALUES @ LOBATTO
INVERSE = float(0.5 / LOBATTO[1])
RATIO = float(LOBATTO[0] / LOBATTO[1])
BK = [float((VALUES[q, 0] + VALUES[q, 3]) / 2) for q in range(3)]
BM = [float((VALUES[q, 0] - VALUES[q, 3]) / 2) for q in range(3)]
BL = [float(ABSCISSA[q]) for q in range(3)]
DK = [float((SLOPES[q, 0] + SLOPES[q, 3]) / 2) for q in range(3)]
DM = [float((SLOPES[q, 0] - SLOPES[q, 3]) / 2) for q in range(3)]
TE = [float((THERMO[q, 0] + THERMO[q, 2]) / 2) for q in range(3)]
TO = [float((THERMO[q, 0] - THERMO[q, 2]) / 2) for q in range(3)]
TM = [float(THERMO[q, 1]) for q in range(3)]


def butterfly(u):
    e0, e1, o0, o1 = u[0] + u[3], u[1] + u[2], u[0] - u[3], u[1] - u[2]
    return [0.5 * e1, e0 - e1, INVERSE * o1, o0 - RATIO * o1]


def unbutterfly(r):
    e0, e1, o0, o1 = r[1], 0.5 * r[0] - r[1], r[3], INVERSE * r[2] - RATIO * r[3]
    return [e0 + o0, e1 + o1, e1 - o1, e0 - o0]


def interp_pair(h, q):
    even = h[0] + BK[q] * h[1]
    odd = BL[q] * h[2] + BM[q] * h[3]
    return even + odd, even - odd


def slope_pair(h, q):
    even = h[2] + DM[q] * h[3]
    odd = DK[q] * h[1]
    return even + odd, even - odd


def along(pair_fn, h):
    out = [None] * 6
    for q in range(3):
        out[q], out[5 - q] = pair_fn(h, q)
    return out


def plus(total, term):
    return term if total is None else total + term


def interp_back_pair(h, q, even, odd):
    h[0] = plus(h[0], even)
    h[1] = plus(h[1], BK[q] * even)
    h[2] = plus(h[2], BL[q] * odd)
    h[3] = plus(h[3], BM[q] * odd)


def slope_back_pair(h, q, even, odd):
    h[1] = plus(h[1], DK[q] * odd)
    h[2] = plus(h[2], even)
    h[3] = plus(h[3], DM[q] * even)


def interp_back(f, h=None):
    h = [None] * 4 if h is None else list(h)
    for q in range(3):
        interp_back_pair(h, q, f[q] + f[5 - q], f[q] - f[5 - q])
    return h


def slope_back(f, h=None):
    h = [None] * 4 if h is None else list(h)
    for q in range(3):
        slope_back_pair(h, q, f[q] + f[5 - q], f[q] - f[5 - q])
    return h


def thermo_along(u):
    even, odd, mid = u[0] + u[2], u[0] - u[2], u[1]
    out = [None] * 6
    for q in range(3):
        both, one = TE[q] * even + TM[q] * mid, TO[q] * odd
        out[q], out[5 - q] = both + one, both - one
    return out


def thermo_back(f):
    even = mid = odd = None
    for q in range(3):
        both, one = f[q] + f[5 - q], f[q] - f[5 - q]
        even = plus(even, TE[q] * both)
        mid = plus(mid, TM[q] * both)
        odd = plus(odd, TO[q] * one)
    return [even + odd, mid, even - odd]


def iotas(rows=8):
    shape = (rows, 128)
    return lax.broadcasted_iota(jnp.int32, shape, 0), lax.broadcasted_iota(jnp.int32, shape, 1)


def gather_lanes(x, index):
    return jnp.take_along_axis(x, index, axis=1, mode="promise_in_bounds")


def split_lanes(parts, rows=8):
    lane = iotas(rows)[1]
    out = []
    for g in range(3):
        place = 3 * ((43 * (lane - g)) & 127) + g
        held = jnp.where(place < 128, parts[0], jnp.where(place < 256, parts[1], parts[2]))
        out.append(gather_lanes(held, (3 * lane + g) & 127))
    return out


def join_lanes(parts):
    lane = iotas()[1]
    moved = [gather_lanes(p, (43 * (lane - g)) & 127) for g, p in enumerate(parts)]
    out = []
    for v in range(3):
        g = (lane + 128 * v) % 3
        out.append(jnp.where(g == 0, moved[0], jnp.where(g == 1, moved[1], moved[2])))
    return out


def next_lane(x):
    return pltpu.roll(x, 127, 1)


def previous_lane(x):
    return pltpu.roll(x, 1, 1)


def pack_kernel(d_ref, v_ref, f_ref, x_ref, y_ref, c_ref, face, face_f, low, low_f, sems):
    copies = []
    for n, ref in enumerate((d_ref, v_ref, f_ref)):
        to_face, to_low = (face.at[n], low.at[n]) if n < 2 else (face_f, low_f)
        copies.append(pltpu.make_async_copy(ref.at[:, 0], to_face, sems.at[2 * n]))
        copies.append(pltpu.make_async_copy(ref.at[:, :, 0:8], to_low, sems.at[2 * n + 1]))
    for copy in copies:
        copy.start()
    for copy in copies:
        copy.wait()
    for n in range(3):
        for c in range(3):
            k = 3 * n + c
            layer = (face[n, c] if n < 2 else face_f[c]).astype(F32)
            x_ref[k] = layer
            c_ref[k : k + 1, :] = layer[0:1]
            for x in range(3):
                r = 9 * x + k
                row = low[n, c, x, 0:1, :] if n < 2 else low_f[c, x, 0:1, :]
                y_ref[r : r + 1, :] = row.astype(F32)


def element_rows(load, place):
    for t in range(3):
        tiles = split_lanes([load(8 * t, 128 * v) for v in range(3)])
        for g in range(3):
            place[g, 8 * t : 8 * t + 8, :] = tiles[g]
    return [place[g, pl.ds(b, 8, stride=3), :] for b in range(3) for g in range(3)]


def prep_kernel(d_ref, v_ref, e_ref, u_ref, eq_ref, place, ez_s, ey_s):
    def body(c, _):
        for x in range(3):
            for k, ref in enumerate((d_ref, v_ref)):
                tiles = element_rows(
                    lambda s, l: ref[c, x, s : s + 8, l : l + 128], place.at[2 * x + k]
                )
                for n in range(9):
                    u_ref[3 * k + c, x * 9 + n] = tiles[n]
        return 0

    lax.fori_loop(0, 3, body, 0)
    for n in range(9):
        for q, t in enumerate(thermo_along([gamma_less * e_ref[3 * n + g] for g in range(3)])):
            ez_s[q, n] = t

    def plane(z, _):
        for x in range(3):
            for q, t in enumerate(thermo_along([ez_s[z, 3 * x + y] for y in range(3)])):
                ey_s[q, x] = t
        for y in range(6):
            for q, t in enumerate(thermo_along([ey_s[y, x] for x in range(3)])):
                eq_ref[q * 36 + y * 6 + z] = t
        return 0

    lax.fori_loop(0, 6, plane, 0)


def project(at_ref, z_s, x_s, out_ref):
    def plane(z, _):
        for y in range(6):
            for x, t in enumerate(thermo_back([at_ref[p * 36 + y * 6 + z] for p in range(6)])):
                x_s[y, x] = t
        for x in range(3):
            for y, t in enumerate(thermo_back([x_s[q, x] for q in range(6)])):
                z_s[z, 3 * x + y] = t
        return 0

    lax.fori_loop(0, 6, plane, 0)
    for n in range(9):
        for g, t in enumerate(thermo_back([z_s[q, n] for q in range(6)])):
            out_ref[3 * n + g] = t


def energy_kernel(
    power_ref, w_ref, e_ref, f_ref, hx_ref, hy_ref, hc_ref,
    out_ref, token_ref, mask_ref, face_mask_ref, rim_mask_ref,
    lump_ref, sum_s, z_s, x_s, hy_s, place,
):
    masks(hx_ref, hy_ref, hc_ref, face_mask_ref, rim_mask_ref, hy_s, place)

    def own(c, _):
        for x in range(3):
            tiles = element_rows(
                lambda s, l: f_ref[c, x, s : s + 8, l : l + 128].astype(F32), place.at[x]
            )
            for n in range(9):
                mask_ref[x, c * 9 + n] = 1.0 - tiles[n]
        return 0

    lax.fori_loop(0, 3, own, 0)
    project(w_ref, z_s, x_s, lump_ref)
    project(power_ref, z_s, x_s, sum_s)

    def body(n, _):
        out_ref[n] = e_ref[n] + step_size * (sum_s[n] / lump_ref[n])
        return 0

    lax.fori_loop(0, 27, body, 0)
    token_ref[...] = sum_s[0]


def point(jac, vel, energy, mass):
    cof = [
        [
            jac[(c + 1) % 3][(d + 1) % 3] * jac[(c + 2) % 3][(d + 2) % 3]
            - jac[(c + 1) % 3][(d + 2) % 3] * jac[(c + 2) % 3][(d + 1) % 3]
            for d in range(3)
        ]
        for c in range(3)
    ]
    det = jac[0][0] * cof[0][0] + jac[0][1] * cof[0][1] + jac[0][2] * cof[0][2]
    inv = pl.reciprocal(det, approx=True)
    inv = inv * (2.0 - det * inv)
    scale = mass * inv
    shear = (viscosity * scale) * inv
    twice = shear + shear
    press = scale * energy
    rate = [
        [vel[c][0] * cof[e][0] + vel[c][1] * cof[e][1] + vel[c][2] * cof[e][2] for e in range(3)]
        for c in range(3)
    ]
    stress = [[None] * 3 for _ in range(3)]
    power = None
    for c in range(3):
        stress[c][c] = twice * rate[c][c] - press
        power = plus(power, stress[c][c] * rate[c][c])
        for d in range(c + 1, 3):
            both = rate[c][d] + rate[d][c]
            stress[c][d] = stress[d][c] = shear * both
            power = power + stress[c][d] * both
    flux = [
        [
            stress[c][0] * cof[0][f] + stress[c][1] * cof[1][f] + stress[c][2] * cof[2][f]
            for f in range(3)
        ]
        for c in range(3)
    ]
    return flux, power


def spread_y(first, row):
    sub = iotas()[0]
    return jnp.where(sub == 7, row, pltpu.roll(first, 7, 0))


def store_parts(nodes_of, minus_ref, plus_ref, inner_ref, rim_ref):
    sub = iotas()[0]

    def body(c, _):
        for g in range(3):
            nodes = nodes_of(c, g)
            for x in range(4):
                over = nodes[x][3]
                nodes[x][0] = nodes[x][0] + jnp.where(sub == 0, 0.0, pltpu.roll(over, 1, 0))
                r = c * 3 + g
                if x in (0, 3):
                    ref = minus_ref if x == 0 else plus_ref
                    ref[pl.ds(216 + r, 1), :] = over[7:8]
                    for b in range(3):
                        ref[pl.ds(pl.multiple_of((c * 9 + b * 3 + g) * 8, 8), 8), :] = nodes[x][b]
                else:
                    rim_ref[x - 1, pl.ds(r, 1), :] = over[7:8]
                    for b in range(3):
                        inner_ref[x - 1, c * 9 + b * 3 + g] = nodes[x][b]
        return 0

    lax.fori_loop(0, 3, body, 0)


def rim_rows(hy_ref, hc_ref, hy_s):
    rows = [
        jnp.concatenate(
            [hy_ref[:, 128 * v : 128 * v + 128], hc_ref[:, 128 * v : 128 * v + 128]], axis=0
        )
        for v in range(3)
    ]
    rows = [jnp.concatenate([r, jnp.zeros((4, 128), F32)], axis=0) for r in rows]
    for t in range(5):
        for g, tile in enumerate(split_lanes([r[8 * t : 8 * t + 8] for r in rows])):
            hy_s[g, 8 * t : 8 * t + 8, :] = tile


def masks(hx_ref, hy_ref, hc_ref, face_mask_ref, rim_mask_ref, hy_s, place):
    rim_rows(hy_ref, hc_ref, hy_s)
    for x in range(4):
        for c in range(3):
            for g in range(3):
                r = 9 * x + 6 + c
                rim_mask_ref[x, c * 3 + g : c * 3 + g + 1, :] = 1.0 - hy_s[g, r : r + 1, :]
    for c in range(3):
        tiles = element_rows(lambda s, l: hx_ref[6 + c, s : s + 8, l : l + 128], place.at[c])
        for n in range(9):
            face_mask_ref[c * 9 + n] = 1.0 - tiles[n]


def force_kernel(
    u_ref, hx_ref, hy_ref, hc_ref, eq_ref, w_ref,
    minus_ref, plus_ref, inner_ref, rim_ref, power_ref,
    hx_s, hy_s, q_s, zv_s, zs_s, w_s, xt_s, ya_s, yb_s, zn_s, place,
):
    rim_rows(hy_ref, hc_ref, hy_s)
    for k in range(6):
        tiles = element_rows(lambda s, l: hx_ref[k, s : s + 8, l : l + 128], place.at[k])
        for n in range(9):
            hx_s[k, n] = tiles[n]
    def gather_nodes(c, _):
        for g in range(3):
            cols = []
            for x in range(4):
                if x < 3:
                    u = [u_ref[c, x * 9 + b * 3 + g] for b in range(3)]
                else:
                    u = [hx_s[c, b * 3 + g] for b in range(3)]
                row = hy_s[g, pl.ds(9 * x + c, 1), :]
                u.append(spread_y(u[0], row))
                cols.append(butterfly(u))
            for y in range(4):
                for x, t in enumerate(butterfly([cols[x][y] for x in range(4)])):
                    q_s[c, (x * 4 + y) * 3 + g] = t
        return 0

    lax.fori_loop(0, 6, gather_nodes, 0)
    for c, n in ((0, 2 * 4), (1, 2)):
        for g in range(3):
            q_s[c, n * 3 + g] = q_s[c, n * 3 + g] + 1.0

    def along_z(c, _):
        for n in range(16):
            u = [q_s[c, 3 * n + g] for g in range(3)]
            u.append(next_lane(u[0]))
            h = butterfly(u)
            if n == 0:
                h[2] = h[2] + jnp.where(c == 2, 1.0, 0.0)
            for q, t in enumerate(along(interp_pair, h)):
                zv_s[q, c, n] = t
            for q, t in enumerate(along(slope_pair, h)):
                zs_s[q, c, n] = t
        return 0

    lax.fori_loop(0, 6, along_z, 0)

    def plane(z, _):
        def along_y(c, _):
            for x in range(4):
                h = [zv_s[z, c, x * 4 + y] for y in range(4)]
                s = [zs_s[z, c, x * 4 + y] for y in range(4)]
                for q, t in enumerate(along(interp_pair, h)):
                    w_s[q, 0, c * 4 + x] = t
                for q, t in enumerate(along(slope_pair, h)):
                    w_s[q, 1, c * 4 + x] = t
                for q, t in enumerate(along(interp_pair, s)):
                    w_s[q, 2, c * 4 + x] = t
            return 0

        lax.fori_loop(0, 6, along_y, 0)

        def line(y, _):
            back = [[[None] * 4 for _ in range(3)] for _ in range(3)]
            for q in range(3):
                grads = [[[None] * 3 for _ in range(6)] for _ in range(2)]
                for c in range(6):
                    for d in range(3):
                        h = [w_s[y, d, c * 4 + x] for x in range(4)]
                        pair = slope_pair(h, q) if d == 0 else interp_pair(h, q)
                        for side in range(2):
                            grads[side][c][d] = pair[side]
                flux = []
                for side in range(2):
                    p = q if side == 0 else 5 - q
                    n = p * 36 + y * 6 + z
                    f, power_ref[n] = point(grads[side][:3], grads[side][3:], eq_ref[n], w_ref[n])
                    flux.append(f)
                for c in range(3):
                    for f in range(3):
                        even = flux[0][c][f] + flux[1][c][f]
                        odd = flux[0][c][f] - flux[1][c][f]
                        (slope_back_pair if f == 0 else interp_back_pair)(back[c][f], q, even, odd)
            for c in range(3):
                for f in range(3):
                    for x in range(4):
                        if back[c][f][x] is not None:
                            xt_s[y, f, c * 4 + x] = back[c][f][x]
            return 0

        lax.fori_loop(0, 6, line, 0)

        def back_y(c, _):
            for x in range(4):
                f = [
                    [xt_s[q, d, c * 4 + x] for q in range(6)] if d or x else None
                    for d in range(3)
                ]
                h = slope_back(f[1], interp_back(f[0]) if x else None)
                s = interp_back(f[2])
                for y in range(4):
                    ya_s[z, c, x * 4 + y] = jnp.zeros((8, 128), F32) if h[y] is None else h[y]
                    yb_s[z, c, x * 4 + y] = s[y]
            return 0

        lax.fori_loop(0, 3, back_y, 0)
        return 0

    lax.fori_loop(0, 6, plane, 0)

    def back_z(c, _):
        for n in range(16):
            h = interp_back([ya_s[q, c, n] for q in range(6)])
            h = slope_back([yb_s[q, c, n] for q in range(6)], h)
            u = unbutterfly(h)
            zn_s[c, n * 3] = -(u[0] + previous_lane(u[3]))
            zn_s[c, n * 3 + 1] = -u[1]
            zn_s[c, n * 3 + 2] = -u[2]
        return 0

    lax.fori_loop(0, 3, back_z, 0)
    store_parts(lambda c, g: nodes_from(zn_s, c, g), minus_ref, plus_ref, inner_ref, rim_ref)


def nodes_from(zn_s, c, g):
    cols = [unbutterfly([zn_s[c, (x * 4 + y) * 3 + g] for y in range(4)]) for x in range(4)]
    rows = [unbutterfly([cols[x][b] for x in range(4)]) for b in range(4)]
    return [[rows[b][x] for b in range(4)] for x in range(4)]


def rows_kernel(minus_ref, plus_ref, inner_ref, rim_ref, got_low_ref, got_high_ref, *rest):
    down_ref, up_ref = rest[-2:]
    for c in range(3):
        for g in range(3):
            r = c * 3 + g
            n = (c * 9 + g) * 8
            down_ref[r : r + 1, :] = minus_ref[n : n + 1, :] + got_low_ref[n : n + 1, :]
            down_ref[27 + r : 28 + r, :] = plus_ref[n : n + 1, :] + got_high_ref[n : n + 1, :]
            for x in range(2):
                down_ref[9 * (x + 1) + r : 9 * (x + 1) + r + 1, :] = inner_ref[x, c * 9 + g, 0:1, :]
    up_ref[0:9, :] = minus_ref[216:225, :] + got_low_ref[216:225, :]
    up_ref[27:36, :] = plus_ref[216:225, :] + got_high_ref[216:225, :]
    for x in range(2):
        up_ref[9 * (x + 1) : 9 * (x + 1) + 9, :] = rim_ref[x, 0:9, :]


def assemble(c, parts, mask_ref, face_mask_ref, rim_mask_ref, own_ref, q_s):
    minus_ref, plus_ref, inner_ref, rim_ref, low_ref, high_ref, from_down_ref, from_up_ref = parts
    sub = iotas()[0]
    for g in range(3):
        r = c * 3 + g
        cols = []
        for x in range(4):
            u = []
            for b in range(3):
                n = c * 9 + b * 3 + g
                tile = pl.ds(pl.multiple_of(n * 8, 8), 8)
                if x == 0:
                    t = minus_ref[tile, :] + low_ref[tile, :]
                elif x == 3:
                    t = plus_ref[tile, :] + high_ref[tile, :]
                else:
                    t = inner_ref[x - 1, n]
                if b == 0:
                    below = from_down_ref[pl.ds(9 * x + r, 1), :]
                    t = t + jnp.where(sub == 0, below, 0.0)
                t = t * (face_mask_ref[n] if x == 3 else mask_ref[x, n])
                u.append(t)
                if x < 3:
                    own_ref[x, n] = t
            edge = pl.ds(216 + r, 1)
            if x == 0:
                top = minus_ref[edge, :] + low_ref[edge, :]
            elif x == 3:
                top = plus_ref[edge, :] + high_ref[edge, :]
            else:
                top = rim_ref[x - 1, pl.ds(r, 1), :]
            top = (top + from_up_ref[pl.ds(9 * x + r, 1), :]) * rim_mask_ref[x, pl.ds(r, 1), :]
            u.append(spread_y(u[0], top))
            cols.append(butterfly(u))
        for y in range(4):
            for x, t in enumerate(butterfly([cols[x][y] for x in range(4)])):
                q_s[c, (x * 4 + y) * 3 + g] = t


def mass_along_z(c, q_s, zv_s):
    for n in range(16):
        u = [q_s[c, 3 * n + g] for g in range(3)]
        u.append(next_lane(u[0]))
        for q, t in enumerate(along(interp_pair, butterfly(u))):
            zv_s[q, c, n] = t


def apply_kernel(
    minus_ref, plus_ref, inner_ref, rim_ref, low_ref, high_ref, from_down_ref, from_up_ref,
    mask_ref, face_mask_ref, rim_mask_ref, w_ref,
    own_ref, out_minus_ref, out_plus_ref, out_inner_ref, out_rim_ref,
    q_s, zv_s, xt_s, ya_s, zn_s,
):
    parts = (
        minus_ref, plus_ref, inner_ref, rim_ref, low_ref, high_ref, from_down_ref, from_up_ref,
    )

    def first(c, _):
        assemble(c, parts, mask_ref, face_mask_ref, rim_mask_ref, own_ref, q_s)
        mass_along_z(c, q_s, zv_s)
        return 0

    lax.fori_loop(0, 3, first, 0)

    def plane(z, _):
        for c in range(3):
            lines = [along(interp_pair, [zv_s[z, c, x * 4 + y] for y in range(4)]) for x in range(4)]
            for y in range(6):
                h = [lines[x][y] for x in range(4)]
                at = along(interp_pair, h)
                at = [at[p] * w_ref[p * 36 + y * 6 + z] for p in range(6)]
                for x, t in enumerate(interp_back(at)):
                    xt_s[c, x, y] = t
            for x in range(4):
                for y, t in enumerate(interp_back([xt_s[c, x, q] for q in range(6)])):
                    ya_s[z, c, x * 4 + y] = t
        return 0

    lax.fori_loop(0, 6, plane, 0)

    def back_z(c, _):
        for n in range(16):
            u = unbutterfly(interp_back([ya_s[q, c, n] for q in range(6)]))
            zn_s[c, n * 3] = u[0] + previous_lane(u[3])
            zn_s[c, n * 3 + 1] = u[1]
            zn_s[c, n * 3 + 2] = u[2]
        return 0

    lax.fori_loop(0, 3, back_z, 0)
    store_parts(
        lambda c, g: nodes_from(zn_s, c, g), out_minus_ref, out_plus_ref, out_inner_ref, out_rim_ref
    )


def total(t):
    return jnp.sum(jnp.sum(t, axis=0, keepdims=True), axis=1, keepdims=True)


def moments_kernel(
    minus_ref, plus_ref, inner_ref, rim_ref, low_ref, high_ref, from_down_ref, from_up_ref,
    mask_ref, face_mask_ref, rim_mask_ref, w_ref, r_ref, v_ref,
    own_ref, sums_ref, q_s, zv_s,
):
    parts = (
        minus_ref, plus_ref, inner_ref, rim_ref, low_ref, high_ref, from_down_ref, from_up_ref,
    )

    def first(c, _):
        assemble(c, parts, mask_ref, face_mask_ref, rim_mask_ref, own_ref, q_s)
        mass_along_z(c, q_s, zv_s)
        return 0

    lax.fori_loop(0, 3, first, 0)
    zero = jnp.zeros((8, 128), F32)

    def dots(n, s):
        s = list(s)
        for x in range(3):
            r, v, w = r_ref[x, n], v_ref[x, n], own_ref[x, n]
            s = [
                s[0] + r * r, s[1] + r * v, s[2] + v * v, s[3] + v * w, s[4] + w * w,
            ]
        return tuple(s)

    sums = lax.fori_loop(0, 27, dots, (zero,) * 5)

    def plane(z, s):
        s = list(s)
        for c in range(3):
            lines = [along(interp_pair, [zv_s[z, c, x * 4 + y] for y in range(4)]) for x in range(4)]
            for y in range(6):
                at = along(interp_pair, [lines[x][y] for x in range(4)])
                for p in range(6):
                    s[c] = s[c] + (at[p] * at[p]) * w_ref[p * 36 + y * 6 + z]
        return tuple(s)

    last = lax.fori_loop(0, 6, plane, (zero,) * 3)
    sums = list(sums) + [last[0] + last[1] + last[2]]
    lane = iotas(1)[1]
    row = jnp.zeros((1, 128), F32)
    for k in range(6):
        row = row + jnp.where(lane == k, total(sums[k]), 0.0)
    sums_ref[...] = jnp.broadcast_to(row, sums_ref.shape)


def coefficients(mu):
    unit = mu[1] / mu[0]
    m = [None] * 6
    scale = 1.0 / mu[0]
    for k in range(6):
        m[k] = mu[k] * scale
        scale = scale / unit
    a0 = m[0] / m[1]
    rr1 = a0 * a0 * m[2] - 2.0 * a0 * m[1] + m[0]
    b0 = rr1 / m[0]
    d1 = [1.0 + b0, -a0]
    a1 = rr1 / (d1[0] * d1[0] * m[1] + 2.0 * d1[0] * d1[1] * m[2] + d1[1] * d1[1] * m[3])
    p1 = -(a0 + a1 * d1[0])
    p2 = -a1 * d1[1]
    rr2 = (
        m[0] + p1 * p1 * m[2] + p2 * p2 * m[4]
        + 2.0 * (p1 * m[1] + p2 * m[2] + p1 * p2 * m[3])
    )
    b1 = rr2 / rr1
    q = [1.0 + b1 * d1[0], p1 + b1 * d1[1], p2]
    a2 = rr2 / (
        q[0] * q[0] * m[1] + q[1] * q[1] * m[3] + q[2] * q[2] * m[5]
        + 2.0 * (q[0] * q[1] * m[2] + q[0] * q[2] * m[3] + q[1] * q[2] * m[4])
    )
    x = [a0 + a1 * d1[0] + a2 * q[0], a1 * d1[1] + a2 * q[1], a2 * q[2]]
    return [x[0] / unit, x[1] / (unit * unit), x[2] / (unit * unit * unit)]


def final_kernel(
    sums_ref, r_ref, v_ref, w_ref, d_ref, vel_ref, a_out, v_out, d_out, place, a_s, v_s, d_s, sems
):
    lane = iotas(1)[1]
    row = jnp.sum(sums_ref[...], axis=0, keepdims=True)
    mu = [
        jnp.broadcast_to(jnp.sum(jnp.where(lane == k, row, 0.0), axis=1, keepdims=True), (8, 128))
        for k in range(6)
    ]
    k0, k1, k2 = coefficients(mu)

    def copies(c):
        pairs = ((a_s, a_out), (v_s, v_out), (d_s, d_out))
        return [
            pltpu.make_async_copy(src.at[c], dst.at[c], sems.at[c, i])
            for i, (src, dst) in enumerate(pairs)
        ]

    def body(c, _):
        for x in range(3):
            for b in range(3):
                for g in range(3):
                    n = c * 9 + b * 3 + g
                    place[x, g, pl.ds(b, 8, stride=3), :] = (
                        k0 * r_ref[x, n] + k1 * v_ref[x, n] + k2 * w_ref[x, n]
                    )
            for s in range(3):
                rows = slice(8 * s, 8 * s + 8)
                for v, t in enumerate(join_lanes([place[x, g, rows, :] for g in range(3)])):
                    lanes = slice(128 * v, 128 * v + 128)
                    a_s[c, x, rows, lanes] = t
                    new = vel_ref[c, x, rows, lanes] + step_size * t
                    v_s[c, x, rows, lanes] = new
                    d_s[c, x, rows, lanes] = d_ref[c, x, rows, lanes] + step_size * new
        for copy in copies(c):
            copy.start()
        return 0

    lax.fori_loop(0, 3, body, 0)
    for c in range(3):
        for copy in copies(c):
            copy.wait()


def call(kernel, outs, scratch, name, flops=0, limit=VMEM_LIMIT, **more):
    def run(*args):
        moved = sum(a.size * 4 for a in args) + sum(4 * math.prod(s) for s in outs)
        return pl.pallas_call(
            kernel,
            out_shape=[jax.ShapeDtypeStruct(s, F32) for s in outs],
            scratch_shapes=[pltpu.VMEM(s, F32) if isinstance(s, tuple) else s for s in scratch],
            compiler_params=pltpu.CompilerParams(vmem_limit_bytes=limit),
            cost_estimate=pl.CostEstimate(flops=flops, bytes_accessed=moved, transcendentals=0),
            name=name,
            **more,
        )(*args)

    return run


T = (8, 128)
FACE = (232, 128)
PARTS = [FACE, FACE, (2, 27) + T, (2, 16, 128)]


def solution(mesh):
    gx, gy = mesh.shape["gx"], mesh.shape["gy"]

    def moved(value, by_x, by_y):
        pairs = [
            (i * gy + j, ((i + by_x) % gx) * gy + (j + by_y) % gy)
            for i in range(gx)
            for j in range(gy)
        ]
        return lax.ppermute(value, ("gx", "gy"), pairs)

    def complete(parts, *done):
        minus, plus_face, inner, rim = parts
        low = moved(plus_face, 1, 0)
        high = moved(minus, -1, 0)
        specs = [pl.BlockSpec(memory_space=pltpu.VMEM)] * 6
        specs += [pl.BlockSpec(memory_space=pltpu.VMEM)] * len(done)
        down, up = call(rows_kernel, [(40, 128), (40, 128)], [], "rows", in_specs=specs)(
            minus, plus_face, inner, rim, low, high, *done
        )
        from_up = moved(down, 0, -1)
        from_down = moved(up, 0, 1)
        return (minus, plus_face, inner, rim, low, high, from_down, from_up)

    def on_device(displacement, velocity, energy, mass_weight, pinned):
        weight = mass_weight.reshape((216,) + T)
        dofs = energy.reshape((27,) + T)
        flags = pinned.dtype
        face, row, corner = call(
            pack_kernel,
            [(9, 24, 384), (27, 384), (9, 384)],
            [
                (2, 3, 24, 384), pltpu.VMEM((3, 24, 384), flags), (2, 3, 3, 8, 384),
                pltpu.VMEM((3, 3, 8, 384), flags), pltpu.SemaphoreType.DMA((6,)),
            ],
            "pack",
            limit=62 * 1024 * 1024,
            in_specs=[pl.BlockSpec(memory_space=pltpu.HBM)] * 3,
        )(displacement, velocity, pinned)
        hx = moved(face, -1, 0)
        hy = moved(row, 0, -1)
        hc = moved(corner, -1, -1)
        nodes, heat = call(
            prep_kernel,
            [(6, 27) + T, (216,) + T],
            [(6, 3, 24, 128), (6, 9) + T, (6, 3) + T],
            "prep",
            flops=4000 * 1024,
        )(displacement, velocity, dofs)
        out = call(
            force_kernel,
            PARTS + [(216,) + T],
            [
                (6, 9) + T, (3, 40, 128), (6, 48) + T, (6, 6, 16) + T, (6, 6, 16) + T,
                (6, 3, 24) + T, (6, 3, 12) + T, (6, 3, 16) + T,
                (6, 3, 16) + T, (3, 48) + T, (6, 3, 24, 128),
            ],
            "force",
            flops=90000 * 1024,
        )(nodes, hx, hy, hc, heat, weight)
        parts, power = out[:4], out[4]
        energy_new, token, mask, face_mask, rim_mask = call(
            energy_kernel,
            [(27,) + T, T, (3, 27) + T, (27,) + T, (4, 16, 128)],
            [(27,) + T, (27,) + T, (6, 9) + T, (6, 3) + T, (3, 40, 128), (3, 3, 24, 128)],
            "energy",
            flops=2000 * 1024,
        )(power, weight, dofs, pinned, hx, hy, hc)
        free = (mask, face_mask, rim_mask)
        scratch = [
            (3, 48) + T, (6, 3, 16) + T, (3, 4, 6) + T, (6, 3, 16) + T, (3, 48) + T,
        ]
        apply = call(apply_kernel, [(3, 27) + T] + PARTS, scratch, "apply", flops=13000 * 1024)
        out = apply(*complete(parts, token), *free, weight)
        r, parts = out[0], out[1:]
        out = apply(*complete(parts), *free, weight)
        v, parts = out[0], out[1:]
        w, sums = call(
            moments_kernel, [(3, 27) + T, (gx * gy, 128)], scratch[:2], "moments", flops=8000 * 1024
        )(*complete(parts), *free, weight, r, v)
        sums = sums.reshape(gx * gy, -1, 128)
        sums = lax.all_to_all(sums, ("gx", "gy"), 0, 0).reshape(-1, 128)
        shape = displacement.shape
        acceleration, velocity_new, displacement_new = call(
            final_kernel,
            [shape] * 3,
            [(3, 3, 24, 128), shape, shape, shape, pltpu.SemaphoreType.DMA((3, 3))],
            "final",
            flops=1000 * 1024,
            out_specs=[pl.BlockSpec(memory_space=pltpu.HBM)] * 3,
        )(sums, r, v, w, displacement, velocity)
        return acceleration, velocity_new, displacement_new, energy_new.reshape(energy.shape)

    spec = P(None, "gx", "gy", None)
    return jax.shard_map(
        on_device, mesh=mesh, in_specs=(spec,) * 5, out_specs=(spec,) * 4, check_vma=False
    )
```

```python
import math

import jax
import jax.numpy as jnp
import numpy as np
from jax import lax
from jax.experimental import pallas as pl
from jax.experimental.pallas import tpu as pltpu
from jax.sharding import PartitionSpec as P

step_size = 0.05
viscosity = 0.3
gamma_less = 0.4
F32 = jnp.float32
VMEM_LIMIT = 32 * 1024 * 1024


def tables():
    root_five = 1.0 / math.sqrt(5.0)
    lobatto = np.array([0.0, 0.5 - 0.5 * root_five, 0.5 + 0.5 * root_five, 1.0])
    legendre = np.array(
        [
            -0.932469514203152,
            -0.6612093864662645,
            -0.2386191860831909,
            0.2386191860831909,
            0.6612093864662645,
            0.932469514203152,
        ]
    )
    t = 0.5 + 0.5 * legendre
    values = np.ones((6, 4))
    slopes = np.zeros((6, 4))
    for a in range(4):
        for b in range(4):
            if b != a:
                values[:, a] *= (t - lobatto[b]) / (lobatto[a] - lobatto[b])
        for c in range(4):
            if c != a:
                term = np.ones(6) / (lobatto[a] - lobatto[c])
                for b in range(4):
                    if b != a and b != c:
                        term = term * (t - lobatto[b]) / (lobatto[a] - lobatto[b])
                slopes[:, a] += term
    thermo = np.stack([(1.0 - t) * (1.0 - t), 2.0 * t * (1.0 - t), t * t], axis=1)
    return values, slopes, thermo


VALUES, SLOPES, THERMO = tables()
LOBATTO = np.array([0.0, 0.5 - 0.5 / math.sqrt(5.0), 0.5 + 0.5 / math.sqrt(5.0), 1.0]) - 0.5
ABSCISSA = VALUES @ LOBATTO
INVERSE = float(0.5 / LOBATTO[1])
RATIO = float(LOBATTO[0] / LOBATTO[1])
BK = [float((VALUES[q, 0] + VALUES[q, 3]) / 2) for q in range(3)]
BM = [float((VALUES[q, 0] - VALUES[q, 3]) / 2) for q in range(3)]
BL = [float(ABSCISSA[q]) for q in range(3)]
DK = [float((SLOPES[q, 0] + SLOPES[q, 3]) / 2) for q in range(3)]
DM = [float((SLOPES[q, 0] - SLOPES[q, 3]) / 2) for q in range(3)]
TE = [float((THERMO[q, 0] + THERMO[q, 2]) / 2) for q in range(3)]
TO = [float((THERMO[q, 0] - THERMO[q, 2]) / 2) for q in range(3)]
TM = [float(THERMO[q, 1]) for q in range(3)]


def butterfly(u):
    e0, e1, o0, o1 = u[0] + u[3], u[1] + u[2], u[0] - u[3], u[1] - u[2]
    return [0.5 * e1, e0 - e1, INVERSE * o1, o0 - RATIO * o1]


def unbutterfly(r):
    e0, e1, o0, o1 = r[1], 0.5 * r[0] - r[1], r[3], INVERSE * r[2] - RATIO * r[3]
    return [e0 + o0, e1 + o1, e1 - o1, e0 - o0]


def interp_pair(h, q):
    even = h[0] + BK[q] * h[1]
    odd = BL[q] * h[2] + BM[q] * h[3]
    return even + odd, even - odd


def slope_pair(h, q):
    even = h[2] + DM[q] * h[3]
    odd = DK[q] * h[1]
    return even + odd, even - odd


def along(pair_fn, h):
    out = [None] * 6
    for q in range(3):
        out[q], out[5 - q] = pair_fn(h, q)
    return out


def plus(total, term):
    return term if total is None else total + term


def interp_back_pair(h, q, even, odd):
    h[0] = plus(h[0], even)
    h[1] = plus(h[1], BK[q] * even)
    h[2] = plus(h[2], BL[q] * odd)
    h[3] = plus(h[3], BM[q] * odd)


def slope_back_pair(h, q, even, odd):
    h[1] = plus(h[1], DK[q] * odd)
    h[2] = plus(h[2], even)
    h[3] = plus(h[3], DM[q] * even)


def interp_back(f, h=None):
    h = [None] * 4 if h is None else list(h)
    for q in range(3):
        interp_back_pair(h, q, f[q] + f[5 - q], f[q] - f[5 - q])
    return h


def slope_back(f, h=None):
    h = [None] * 4 if h is None else list(h)
    for q in range(3):
        slope_back_pair(h, q, f[q] + f[5 - q], f[q] - f[5 - q])
    return h


def thermo_along(u):
    even, odd, mid = u[0] + u[2], u[0] - u[2], u[1]
    out = [None] * 6
    for q in range(3):
        both, one = TE[q] * even + TM[q] * mid, TO[q] * odd
        out[q], out[5 - q] = both + one, both - one
    return out


def thermo_back(f):
    even = mid = odd = None
    for q in range(3):
        both, one = f[q] + f[5 - q], f[q] - f[5 - q]
        even = plus(even, TE[q] * both)
        mid = plus(mid, TM[q] * both)
        odd = plus(odd, TO[q] * one)
    return [even + odd, mid, even - odd]


def iotas(rows=8):
    shape = (rows, 128)
    return lax.broadcasted_iota(jnp.int32, shape, 0), lax.broadcasted_iota(jnp.int32, shape, 1)


def gather_lanes(x, index):
    return jnp.take_along_axis(x, index, axis=1, mode="promise_in_bounds")


def split_lanes(parts, rows=8):
    lane = iotas(rows)[1]
    out = []
    for g in range(3):
        place = 3 * ((43 * (lane - g)) & 127) + g
        held = jnp.where(place < 128, parts[0], jnp.where(place < 256, parts[1], parts[2]))
        out.append(gather_lanes(held, (3 * lane + g) & 127))
    return out


def join_lanes(parts):
    lane = iotas()[1]
    moved = [gather_lanes(p, (43 * (lane - g)) & 127) for g, p in enumerate(parts)]
    out = []
    for v in range(3):
        g = (lane + 128 * v) % 3
        out.append(jnp.where(g == 0, moved[0], jnp.where(g == 1, moved[1], moved[2])))
    return out


def next_lane(x):
    return pltpu.roll(x, 127, 1)


def previous_lane(x):
    return pltpu.roll(x, 1, 1)


def pack_kernel(d_ref, v_ref, f_ref, x_ref, y_ref, c_ref, face, face_f, low, low_f, sems):
    copies = []
    for n, ref in enumerate((d_ref, v_ref, f_ref)):
        to_face, to_low = (face.at[n], low.at[n]) if n < 2 else (face_f, low_f)
        copies.append(pltpu.make_async_copy(ref.at[:, 0], to_face, sems.at[2 * n]))
        copies.append(pltpu.make_async_copy(ref.at[:, :, 0:8], to_low, sems.at[2 * n + 1]))
    for copy in copies:
        copy.start()
    for copy in copies:
        copy.wait()
    for n in range(3):
        for c in range(3):
            k = 3 * n + c
            layer = (face[n, c] if n < 2 else face_f[c]).astype(F32)
            x_ref[k] = layer
            c_ref[k : k + 1, :] = layer[0:1]
            for x in range(3):
                r = 9 * x + k
                row = low[n, c, x, 0:1, :] if n < 2 else low_f[c, x, 0:1, :]
                y_ref[r : r + 1, :] = row.astype(F32)


def element_rows(load, place):
    for t in range(3):
        tiles = split_lanes([load(8 * t, 128 * v) for v in range(3)])
        for g in range(3):
            place[g, 8 * t : 8 * t + 8, :] = tiles[g]
    return [place[g, pl.ds(b, 8, stride=3), :] for b in range(3) for g in range(3)]


def prep_kernel(d_ref, v_ref, e_ref, u_ref, eq_ref, place, ez_s, ey_s):
    def body(c, _):
        for x in range(3):
            for k, ref in enumerate((d_ref, v_ref)):
                tiles = element_rows(
                    lambda s, l: ref[c, x, s : s + 8, l : l + 128], place.at[2 * x + k]
                )
                for n in range(9):
                    u_ref[3 * k + c, x * 9 + n] = tiles[n]
        return 0

    lax.fori_loop(0, 3, body, 0)
    for n in range(9):
        for q, t in enumerate(thermo_along([gamma_less * e_ref[3 * n + g] for g in range(3)])):
            ez_s[q, n] = t

    def plane(z, _):
        for x in range(3):
            for q, t in enumerate(thermo_along([ez_s[z, 3 * x + y] for y in range(3)])):
                ey_s[q, x] = t
        for y in range(6):
            for q, t in enumerate(thermo_along([ey_s[y, x] for x in range(3)])):
                eq_ref[q * 36 + y * 6 + z] = t
        return 0

    lax.fori_loop(0, 6, plane, 0)


def project(at_ref, z_s, x_s, out_ref):
    def plane(z, _):
        for y in range(6):
            for x, t in enumerate(thermo_back([at_ref[p * 36 + y * 6 + z] for p in range(6)])):
                x_s[y, x] = t
        for x in range(3):
            for y, t in enumerate(thermo_back([x_s[q, x] for q in range(6)])):
                z_s[z, 3 * x + y] = t
        return 0

    lax.fori_loop(0, 6, plane, 0)
    for n in range(9):
        for g, t in enumerate(thermo_back([z_s[q, n] for q in range(6)])):
            out_ref[3 * n + g] = t


def energy_kernel(
    power_ref, w_ref, e_ref, f_ref, hx_ref, hy_ref, hc_ref,
    out_ref, token_ref, mask_ref, face_mask_ref, rim_mask_ref,
    lump_ref, sum_s, z_s, x_s, hy_s, place,
):
    masks(hx_ref, hy_ref, hc_ref, face_mask_ref, rim_mask_ref, hy_s, place)

    def own(c, _):
        for x in range(3):
            tiles = element_rows(
                lambda s, l: f_ref[c, x, s : s + 8, l : l + 128].astype(F32), place.at[x]
            )
            for n in range(9):
                mask_ref[x, c * 9 + n] = 1.0 - tiles[n]
        return 0

    lax.fori_loop(0, 3, own, 0)
    project(w_ref, z_s, x_s, lump_ref)
    project(power_ref, z_s, x_s, sum_s)

    def body(n, _):
        out_ref[n] = e_ref[n] + step_size * (sum_s[n] / lump_ref[n])
        return 0

    lax.fori_loop(0, 27, body, 0)
    token_ref[...] = sum_s[0]


def point(jac, vel, energy, mass):
    cof = [
        [
            jac[(c + 1) % 3][(d + 1) % 3] * jac[(c + 2) % 3][(d + 2) % 3]
            - jac[(c + 1) % 3][(d + 2) % 3] * jac[(c + 2) % 3][(d + 1) % 3]
            for d in range(3)
        ]
        for c in range(3)
    ]
    det = jac[0][0] * cof[0][0] + jac[0][1] * cof[0][1] + jac[0][2] * cof[0][2]
    inv = pl.reciprocal(det, approx=True)
    inv = inv * (2.0 - det * inv)
    scale = mass * inv
    shear = (viscosity * scale) * inv
    twice = shear + shear
    press = scale * energy
    rate = [
        [vel[c][0] * cof[e][0] + vel[c][1] * cof[e][1] + vel[c][2] * cof[e][2] for e in range(3)]
        for c in range(3)
    ]
    stress = [[None] * 3 for _ in range(3)]
    power = None
    for c in range(3):
        stress[c][c] = twice * rate[c][c] - press
        power = plus(power, stress[c][c] * rate[c][c])
        for d in range(c + 1, 3):
            both = rate[c][d] + rate[d][c]
            stress[c][d] = stress[d][c] = shear * both
            power = power + stress[c][d] * both
    flux = [
        [
            stress[c][0] * cof[0][f] + stress[c][1] * cof[1][f] + stress[c][2] * cof[2][f]
            for f in range(3)
        ]
        for c in range(3)
    ]
    return flux, power


def spread_y(first, row):
    sub = iotas()[0]
    return jnp.where(sub == 7, row, pltpu.roll(first, 7, 0))


def store_parts(nodes_of, minus_ref, plus_ref, inner_ref, rim_ref):
    sub = iotas()[0]

    def body(c, _):
        for g in range(3):
            nodes = nodes_of(c, g)
            for x in range(4):
                over = nodes[x][3]
                nodes[x][0] = nodes[x][0] + jnp.where(sub == 0, 0.0, pltpu.roll(over, 1, 0))
                r = c * 3 + g
                if x in (0, 3):
                    ref = minus_ref if x == 0 else plus_ref
                    ref[pl.ds(216 + r, 1), :] = over[7:8]
                    for b in range(3):
                        ref[pl.ds(pl.multiple_of((c * 9 + b * 3 + g) * 8, 8), 8), :] = nodes[x][b]
                else:
                    rim_ref[x - 1, pl.ds(r, 1), :] = over[7:8]
                    for b in range(3):
                        inner_ref[x - 1, c * 9 + b * 3 + g] = nodes[x][b]
        return 0

    lax.fori_loop(0, 3, body, 0)


def rim_rows(hy_ref, hc_ref, hy_s):
    rows = [
        jnp.concatenate(
            [hy_ref[:, 128 * v : 128 * v + 128], hc_ref[:, 128 * v : 128 * v + 128]], axis=0
        )
        for v in range(3)
    ]
    rows = [jnp.concatenate([r, jnp.zeros((4, 128), F32)], axis=0) for r in rows]
    for t in range(5):
        for g, tile in enumerate(split_lanes([r[8 * t : 8 * t + 8] for r in rows])):
            hy_s[g, 8 * t : 8 * t + 8, :] = tile


def masks(hx_ref, hy_ref, hc_ref, face_mask_ref, rim_mask_ref, hy_s, place):
    rim_rows(hy_ref, hc_ref, hy_s)
    for x in range(4):
        for c in range(3):
            for g in range(3):
                r = 9 * x + 6 + c
                rim_mask_ref[x, c * 3 + g : c * 3 + g + 1, :] = 1.0 - hy_s[g, r : r + 1, :]
    for c in range(3):
        tiles = element_rows(lambda s, l: hx_ref[6 + c, s : s + 8, l : l + 128], place.at[c])
        for n in range(9):
            face_mask_ref[c * 9 + n] = 1.0 - tiles[n]


def force_kernel(
    u_ref, hx_ref, hy_ref, hc_ref, eq_ref, w_ref,
    minus_ref, plus_ref, inner_ref, rim_ref, power_ref,
    hx_s, hy_s, q_s, zv_s, zs_s, w_s, xt_s, ya_s, yb_s, zn_s, place,
):
    rim_rows(hy_ref, hc_ref, hy_s)
    for k in range(6):
        tiles = element_rows(lambda s, l: hx_ref[k, s : s + 8, l : l + 128], place.at[k])
        for n in range(9):
            hx_s[k, n] = tiles[n]
    def gather_nodes(c, _):
        for g in range(3):
            cols = []
            for x in range(4):
                if x < 3:
                    u = [u_ref[c, x * 9 + b * 3 + g] for b in range(3)]
                else:
                    u = [hx_s[c, b * 3 + g] for b in range(3)]
                row = hy_s[g, pl.ds(9 * x + c, 1), :]
                u.append(spread_y(u[0], row))
                cols.append(butterfly(u))
            for y in range(4):
                for x, t in enumerate(butterfly([cols[x][y] for x in range(4)])):
                    q_s[c, (x * 4 + y) * 3 + g] = t
        return 0

    lax.fori_loop(0, 6, gather_nodes, 0)
    for c, n in ((0, 2 * 4), (1, 2)):
        for g in range(3):
            q_s[c, n * 3 + g] = q_s[c, n * 3 + g] + 1.0

    def along_z(c, _):
        for n in range(16):
            u = [q_s[c, 3 * n + g] for g in range(3)]
            u.append(next_lane(u[0]))
            h = butterfly(u)
            if n == 0:
                h[2] = h[2] + jnp.where(c == 2, 1.0, 0.0)
            for q, t in enumerate(along(interp_pair, h)):
                zv_s[q, c, n] = t
            for q, t in enumerate(along(slope_pair, h)):
                zs_s[q, c, n] = t
        return 0

    lax.fori_loop(0, 6, along_z, 0)

    def plane(z, _):
        def along_y(c, _):
            for x in range(4):
                h = [zv_s[z, c, x * 4 + y] for y in range(4)]
                s = [zs_s[z, c, x * 4 + y] for y in range(4)]
                for q, t in enumerate(along(interp_pair, h)):
                    w_s[q, 0, c * 4 + x] = t
                for q, t in enumerate(along(slope_pair, h)):
                    w_s[q, 1, c * 4 + x] = t
                for q, t in enumerate(along(interp_pair, s)):
                    w_s[q, 2, c * 4 + x] = t
            return 0

        lax.fori_loop(0, 6, along_y, 0)

        def line(y, _):
            back = [[[None] * 4 for _ in range(3)] for _ in range(3)]
            for q in range(3):
                grads = [[[None] * 3 for _ in range(6)] for _ in range(2)]
                for c in range(6):
                    for d in range(3):
                        h = [w_s[y, d, c * 4 + x] for x in range(4)]
                        pair = slope_pair(h, q) if d == 0 else interp_pair(h, q)
                        for side in range(2):
                            grads[side][c][d] = pair[side]
                flux = []
                for side in range(2):
                    p = q if side == 0 else 5 - q
                    n = p * 36 + y * 6 + z
                    f, power_ref[n] = point(grads[side][:3], grads[side][3:], eq_ref[n], w_ref[n])
                    flux.append(f)
                for c in range(3):
                    for f in range(3):
                        even = flux[0][c][f] + flux[1][c][f]
                        odd = flux[0][c][f] - flux[1][c][f]
                        (slope_back_pair if f == 0 else interp_back_pair)(back[c][f], q, even, odd)
            for c in range(3):
                for f in range(3):
                    for x in range(4):
                        if back[c][f][x] is not None:
                            xt_s[y, f, c * 4 + x] = back[c][f][x]
            return 0

        lax.fori_loop(0, 6, line, 0)

        def back_y(c, _):
            for x in range(4):
                f = [
                    [xt_s[q, d, c * 4 + x] for q in range(6)] if d or x else None
                    for d in range(3)
                ]
                h = slope_back(f[1], interp_back(f[0]) if x else None)
                s = interp_back(f[2])
                for y in range(4):
                    ya_s[z, c, x * 4 + y] = jnp.zeros((8, 128), F32) if h[y] is None else h[y]
                    yb_s[z, c, x * 4 + y] = s[y]
            return 0

        lax.fori_loop(0, 3, back_y, 0)
        return 0

    lax.fori_loop(0, 6, plane, 0)

    def back_z(c, _):
        for n in range(16):
            h = interp_back([ya_s[q, c, n] for q in range(6)])
            h = slope_back([yb_s[q, c, n] for q in range(6)], h)
            u = unbutterfly(h)
            zn_s[c, n * 3] = -(u[0] + previous_lane(u[3]))
            zn_s[c, n * 3 + 1] = -u[1]
            zn_s[c, n * 3 + 2] = -u[2]
        return 0

    lax.fori_loop(0, 3, back_z, 0)
    store_parts(lambda c, g: nodes_from(zn_s, c, g), minus_ref, plus_ref, inner_ref, rim_ref)


def nodes_from(zn_s, c, g):
    cols = [unbutterfly([zn_s[c, (x * 4 + y) * 3 + g] for y in range(4)]) for x in range(4)]
    rows = [unbutterfly([cols[x][b] for x in range(4)]) for b in range(4)]
    return [[rows[b][x] for b in range(4)] for x in range(4)]


def rows_kernel(minus_ref, plus_ref, inner_ref, rim_ref, got_low_ref, got_high_ref, *rest):
    down_ref, up_ref = rest[-2:]
    for c in range(3):
        for g in range(3):
            r = c * 3 + g
            n = (c * 9 + g) * 8
            down_ref[r : r + 1, :] = minus_ref[n : n + 1, :] + got_low_ref[n : n + 1, :]
            down_ref[27 + r : 28 + r, :] = plus_ref[n : n + 1, :] + got_high_ref[n : n + 1, :]
            for x in range(2):
                down_ref[9 * (x + 1) + r : 9 * (x + 1) + r + 1, :] = inner_ref[x, c * 9 + g, 0:1, :]
    up_ref[0:9, :] = minus_ref[216:225, :] + got_low_ref[216:225, :]
    up_ref[27:36, :] = plus_ref[216:225, :] + got_high_ref[216:225, :]
    for x in range(2):
        up_ref[9 * (x + 1) : 9 * (x + 1) + 9, :] = rim_ref[x, 0:9, :]


def assemble(c, parts, mask_ref, face_mask_ref, rim_mask_ref, own_ref, q_s):
    minus_ref, plus_ref, inner_ref, rim_ref, low_ref, high_ref, from_down_ref, from_up_ref = parts
    sub = iotas()[0]
    for g in range(3):
        r = c * 3 + g
        cols = []
        for x in range(4):
            u = []
            for b in range(3):
                n = c * 9 + b * 3 + g
                tile = pl.ds(pl.multiple_of(n * 8, 8), 8)
                if x == 0:
                    t = minus_ref[tile, :] + low_ref[tile, :]
                elif x == 3:
                    t = plus_ref[tile, :] + high_ref[tile, :]
                else:
                    t = inner_ref[x - 1, n]
                if b == 0:
                    below = from_down_ref[pl.ds(9 * x + r, 1), :]
                    t = t + jnp.where(sub == 0, below, 0.0)
                t = t * (face_mask_ref[n] if x == 3 else mask_ref[x, n])
                u.append(t)
                if x < 3:
                    own_ref[x, n] = t
            edge = pl.ds(216 + r, 1)
            if x == 0:
                top = minus_ref[edge, :] + low_ref[edge, :]
            elif x == 3:
                top = plus_ref[edge, :] + high_ref[edge, :]
            else:
                top = rim_ref[x - 1, pl.ds(r, 1), :]
            top = (top + from_up_ref[pl.ds(9 * x + r, 1), :]) * rim_mask_ref[x, pl.ds(r, 1), :]
            u.append(spread_y(u[0], top))
            cols.append(butterfly(u))
        for y in range(4):
            for x, t in enumerate(butterfly([cols[x][y] for x in range(4)])):
                q_s[c, (x * 4 + y) * 3 + g] = t


def mass_along_z(c, q_s, zv_s):
    for n in range(16):
        u = [q_s[c, 3 * n + g] for g in range(3)]
        u.append(next_lane(u[0]))
        for q, t in enumerate(along(interp_pair, butterfly(u))):
            zv_s[q, c, n] = t


def apply_kernel(
    minus_ref, plus_ref, inner_ref, rim_ref, low_ref, high_ref, from_down_ref, from_up_ref,
    mask_ref, face_mask_ref, rim_mask_ref, w_ref,
    own_ref, out_minus_ref, out_plus_ref, out_inner_ref, out_rim_ref,
    q_s, zv_s, xt_s, ya_s, zn_s,
):
    parts = (
        minus_ref, plus_ref, inner_ref, rim_ref, low_ref, high_ref, from_down_ref, from_up_ref,
    )

    def first(c, _):
        assemble(c, parts, mask_ref, face_mask_ref, rim_mask_ref, own_ref, q_s)
        mass_along_z(c, q_s, zv_s)
        return 0

    lax.fori_loop(0, 3, first, 0, unroll=True)

    def plane(z, _):
        for c in range(3):
            lines = [along(interp_pair, [zv_s[z, c, x * 4 + y] for y in range(4)]) for x in range(4)]
            for y in range(6):
                h = [lines[x][y] for x in range(4)]
                at = along(interp_pair, h)
                at = [at[p] * w_ref[p * 36 + y * 6 + z] for p in range(6)]
                for x, t in enumerate(interp_back(at)):
                    xt_s[c, x, y] = t
            for x in range(4):
                for y, t in enumerate(interp_back([xt_s[c, x, q] for q in range(6)])):
                    ya_s[z, c, x * 4 + y] = t
        return 0

    lax.fori_loop(0, 6, plane, 0)

    def back_z(c, _):
        for n in range(16):
            u = unbutterfly(interp_back([ya_s[q, c, n] for q in range(6)]))
            zn_s[c, n * 3] = u[0] + previous_lane(u[3])
            zn_s[c, n * 3 + 1] = u[1]
            zn_s[c, n * 3 + 2] = u[2]
        return 0

    lax.fori_loop(0, 3, back_z, 0)
    store_parts(
        lambda c, g: nodes_from(zn_s, c, g), out_minus_ref, out_plus_ref, out_inner_ref, out_rim_ref
    )


def total(t):
    return jnp.sum(jnp.sum(t, axis=0, keepdims=True), axis=1, keepdims=True)


def moments_kernel(
    minus_ref, plus_ref, inner_ref, rim_ref, low_ref, high_ref, from_down_ref, from_up_ref,
    mask_ref, face_mask_ref, rim_mask_ref, w_ref, r_ref, v_ref,
    own_ref, sums_ref, q_s, zv_s,
):
    parts = (
        minus_ref, plus_ref, inner_ref, rim_ref, low_ref, high_ref, from_down_ref, from_up_ref,
    )

    def first(c, _):
        assemble(c, parts, mask_ref, face_mask_ref, rim_mask_ref, own_ref, q_s)
        mass_along_z(c, q_s, zv_s)
        return 0

    lax.fori_loop(0, 3, first, 0, unroll=True)
    zero = jnp.zeros((8, 128), F32)

    def dots(n, s):
        s = list(s)
        for x in range(3):
            r, v, w = r_ref[x, n], v_ref[x, n], own_ref[x, n]
            s = [
                s[0] + r * r, s[1] + r * v, s[2] + v * v, s[3] + v * w, s[4] + w * w,
            ]
        return tuple(s)

    sums = lax.fori_loop(0, 27, dots, (zero,) * 5)

    def plane(z, s):
        s = list(s)
        for c in range(3):
            lines = [along(interp_pair, [zv_s[z, c, x * 4 + y] for y in range(4)]) for x in range(4)]
            for y in range(6):
                at = along(interp_pair, [lines[x][y] for x in range(4)])
                for p in range(6):
                    s[c] = s[c] + (at[p] * at[p]) * w_ref[p * 36 + y * 6 + z]
        return tuple(s)

    last = lax.fori_loop(0, 6, plane, (zero,) * 3)
    sums = list(sums) + [last[0] + last[1] + last[2]]
    lane = iotas(1)[1]
    row = jnp.zeros((1, 128), F32)
    for k in range(6):
        row = row + jnp.where(lane == k, total(sums[k]), 0.0)
    sums_ref[...] = jnp.broadcast_to(row, sums_ref.shape)


def coefficients(mu):
    unit = mu[1] / mu[0]
    m = [None] * 6
    scale = 1.0 / mu[0]
    for k in range(6):
        m[k] = mu[k] * scale
        scale = scale / unit
    a0 = m[0] / m[1]
    rr1 = a0 * a0 * m[2] - 2.0 * a0 * m[1] + m[0]
    b0 = rr1 / m[0]
    d1 = [1.0 + b0, -a0]
    a1 = rr1 / (d1[0] * d1[0] * m[1] + 2.0 * d1[0] * d1[1] * m[2] + d1[1] * d1[1] * m[3])
    p1 = -(a0 + a1 * d1[0])
    p2 = -a1 * d1[1]
    rr2 = (
        m[0] + p1 * p1 * m[2] + p2 * p2 * m[4]
        + 2.0 * (p1 * m[1] + p2 * m[2] + p1 * p2 * m[3])
    )
    b1 = rr2 / rr1
    q = [1.0 + b1 * d1[0], p1 + b1 * d1[1], p2]
    a2 = rr2 / (
        q[0] * q[0] * m[1] + q[1] * q[1] * m[3] + q[2] * q[2] * m[5]
        + 2.0 * (q[0] * q[1] * m[2] + q[0] * q[2] * m[3] + q[1] * q[2] * m[4])
    )
    x = [a0 + a1 * d1[0] + a2 * q[0], a1 * d1[1] + a2 * q[1], a2 * q[2]]
    return [x[0] / unit, x[1] / (unit * unit), x[2] / (unit * unit * unit)]


def final_kernel(
    sums_ref, r_ref, v_ref, w_ref, d_ref, vel_ref, a_out, v_out, d_out, place, a_s, v_s, d_s, sems
):
    lane = iotas(1)[1]
    row = jnp.sum(sums_ref[...], axis=0, keepdims=True)
    mu = [
        jnp.broadcast_to(jnp.sum(jnp.where(lane == k, row, 0.0), axis=1, keepdims=True), (8, 128))
        for k in range(6)
    ]
    k0, k1, k2 = coefficients(mu)

    def copies(c):
        pairs = ((a_s, a_out), (v_s, v_out), (d_s, d_out))
        return [
            pltpu.make_async_copy(src.at[c], dst.at[c], sems.at[c, i])
            for i, (src, dst) in enumerate(pairs)
        ]

    def body(c, _):
        for x in range(3):
            for b in range(3):
                for g in range(3):
                    n = c * 9 + b * 3 + g
                    place[x, g, pl.ds(b, 8, stride=3), :] = (
                        k0 * r_ref[x, n] + k1 * v_ref[x, n] + k2 * w_ref[x, n]
                    )
            for s in range(3):
                rows = slice(8 * s, 8 * s + 8)
                for v, t in enumerate(join_lanes([place[x, g, rows, :] for g in range(3)])):
                    lanes = slice(128 * v, 128 * v + 128)
                    a_s[c, x, rows, lanes] = t
                    new = vel_ref[c, x, rows, lanes] + step_size * t
                    v_s[c, x, rows, lanes] = new
                    d_s[c, x, rows, lanes] = d_ref[c, x, rows, lanes] + step_size * new
        for copy in copies(c):
            copy.start()
        return 0

    lax.fori_loop(0, 3, body, 0)
    for c in range(3):
        for copy in copies(c):
            copy.wait()


def call(kernel, outs, scratch, name, flops=0, limit=VMEM_LIMIT, **more):
    def run(*args):
        moved = sum(a.size * 4 for a in args) + sum(4 * math.prod(s) for s in outs)
        return pl.pallas_call(
            kernel,
            out_shape=[jax.ShapeDtypeStruct(s, F32) for s in outs],
            scratch_shapes=[pltpu.VMEM(s, F32) if isinstance(s, tuple) else s for s in scratch],
            compiler_params=pltpu.CompilerParams(vmem_limit_bytes=limit),
            cost_estimate=pl.CostEstimate(flops=flops, bytes_accessed=moved, transcendentals=0),
            name=name,
            **more,
        )(*args)

    return run


T = (8, 128)
FACE = (232, 128)
PARTS = [FACE, FACE, (2, 27) + T, (2, 16, 128)]


def solution(mesh):
    gx, gy = mesh.shape["gx"], mesh.shape["gy"]

    def moved(value, by_x, by_y):
        pairs = [
            (i * gy + j, ((i + by_x) % gx) * gy + (j + by_y) % gy)
            for i in range(gx)
            for j in range(gy)
        ]
        return lax.ppermute(value, ("gx", "gy"), pairs)

    def complete(parts, *done):
        minus, plus_face, inner, rim = parts
        low = moved(plus_face, 1, 0)
        high = moved(minus, -1, 0)
        specs = [pl.BlockSpec(memory_space=pltpu.VMEM)] * 6
        specs += [pl.BlockSpec(memory_space=pltpu.VMEM)] * len(done)
        down, up = call(rows_kernel, [(40, 128), (40, 128)], [], "rows", in_specs=specs)(
            minus, plus_face, inner, rim, low, high, *done
        )
        from_up = moved(down, 0, -1)
        from_down = moved(up, 0, 1)
        return (minus, plus_face, inner, rim, low, high, from_down, from_up)

    def on_device(displacement, velocity, energy, mass_weight, pinned):
        weight = mass_weight.reshape((216,) + T)
        dofs = energy.reshape((27,) + T)
        flags = pinned.dtype
        face, row, corner = call(
            pack_kernel,
            [(9, 24, 384), (27, 384), (9, 384)],
            [
                (2, 3, 24, 384), pltpu.VMEM((3, 24, 384), flags), (2, 3, 3, 8, 384),
                pltpu.VMEM((3, 3, 8, 384), flags), pltpu.SemaphoreType.DMA((6,)),
            ],
            "pack",
            limit=62 * 1024 * 1024,
            in_specs=[pl.BlockSpec(memory_space=pltpu.HBM)] * 3,
        )(displacement, velocity, pinned)
        hx = moved(face, -1, 0)
        hy = moved(row, 0, -1)
        hc = moved(corner, -1, -1)
        nodes, heat = call(
            prep_kernel,
            [(6, 27) + T, (216,) + T],
            [(6, 3, 24, 128), (6, 9) + T, (6, 3) + T],
            "prep",
            flops=4000 * 1024,
        )(displacement, velocity, dofs)
        out = call(
            force_kernel,
            PARTS + [(216,) + T],
            [
                (6, 9) + T, (3, 40, 128), (6, 48) + T, (6, 6, 16) + T, (6, 6, 16) + T,
                (6, 3, 24) + T, (6, 3, 12) + T, (6, 3, 16) + T,
                (6, 3, 16) + T, (3, 48) + T, (6, 3, 24, 128),
            ],
            "force",
            flops=90000 * 1024,
        )(nodes, hx, hy, hc, heat, weight)
        parts, power = out[:4], out[4]
        energy_new, token, mask, face_mask, rim_mask = call(
            energy_kernel,
            [(27,) + T, T, (3, 27) + T, (27,) + T, (4, 16, 128)],
            [(27,) + T, (27,) + T, (6, 9) + T, (6, 3) + T, (3, 40, 128), (3, 3, 24, 128)],
            "energy",
            flops=2000 * 1024,
        )(power, weight, dofs, pinned, hx, hy, hc)
        free = (mask, face_mask, rim_mask)
        scratch = [
            (3, 48) + T, (6, 3, 16) + T, (3, 4, 6) + T, (6, 3, 16) + T, (3, 48) + T,
        ]
        apply = call(apply_kernel, [(3, 27) + T] + PARTS, scratch, "apply", flops=13000 * 1024)
        out = apply(*complete(parts, token), *free, weight)
        r, parts = out[0], out[1:]
        out = apply(*complete(parts), *free, weight)
        v, parts = out[0], out[1:]
        w, sums = call(
            moments_kernel, [(3, 27) + T, (gx * gy, 128)], scratch[:2], "moments", flops=8000 * 1024
        )(*complete(parts), *free, weight, r, v)
        sums = sums.reshape(gx * gy, -1, 128)
        sums = lax.all_to_all(sums, ("gx", "gy"), 0, 0).reshape(-1, 128)
        shape = displacement.shape
        acceleration, velocity_new, displacement_new = call(
            final_kernel,
            [shape] * 3,
            [(3, 3, 24, 128), shape, shape, shape, pltpu.SemaphoreType.DMA((3, 3))],
            "final",
            flops=1000 * 1024,
            out_specs=[pl.BlockSpec(memory_space=pltpu.HBM)] * 3,
        )(sums, r, v, w, displacement, velocity)
        return acceleration, velocity_new, displacement_new, energy_new.reshape(energy.shape)

    spec = P(None, "gx", "gy", None)
    return jax.shard_map(
        on_device, mesh=mesh, in_specs=(spec,) * 5, out_specs=(spec,) * 4, check_vma=False
    )
```
